32 devices in a mesh: dp: 8 (over y, x, core), tensor: 4 (over z).
Axes of the slice: x: 2, y: 2, z: 4, core: 2. Of those that a mesh axis runs over, the one named last changes fastest.
Arguments:
- streams: bfloat16 [8192, 4, 2048], P(('dp', 'tensor')), may hold values from -6 to 6
- cotangent: bfloat16 [8192, 4, 2048], P(('dp', 'tensor')), may hold values from -6 to 6
- lengths: int32 [24], replicated, may hold values from 1 to 1021, as said below
- permutation: int32 [24], replicated, may hold values from 0 to 23, as said below
- query_weight: bfloat16 [2048, 2048], P('dp', 'tensor'), may hold values from -0.125 to 0.125
- key_weight: bfloat16 [2048, 2048], P('dp', 'tensor'), may hold values from -0.125 to 0.125
- value_weight: bfloat16 [2048, 2048], P('dp', 'tensor'), may hold values from -0.125 to 0.125
- out_weight: bfloat16 [2048, 2048], P('dp', 'tensor'), may hold values from -3 to 3
- gate_weight: bfloat16 [2048, 8192], P('dp', 'tensor'), may hold values from -0.125 to 0.125
- up_weight: bfloat16 [2048, 8192], P('dp', 'tensor'), may hold values from -0.125 to 0.125
- down_weight: bfloat16 [2048, 8192], P('dp', 'tensor'), may hold values from -0.0625 to 0.0625
- mix_static: float32 [2, 4, 6], replicated, may hold values from -1 to 1
- mix_weight: float32 [2, 2048, 6], replicated, may hold values from -0.125 to 0.125
- mix_scale: float32 [2, 6], replicated, may hold values from 0.3 to 1
Outputs:
- out_streams: bfloat16 [8192, 4, 2048], P(('dp', 'tensor'))
- stream_grads: bfloat16 [8192, 4, 2048], P(('dp', 'tensor'))
- query_weight_grad: float32 [2048, 2048], P(None, 'tensor')
- key_weight_grad: float32 [2048, 2048], P(None, 'tensor')
- value_weight_grad: float32 [2048, 2048], P(None, 'tensor')
- out_weight_grad: float32 [2048, 2048], P(None, 'tensor')
- gate_weight_grad: float32 [2048, 8192], P(None, 'tensor')
- up_weight_grad: float32 [2048, 8192], P(None, 'tensor')
- down_weight_grad: float32 [2048, 8192], P(None, 'tensor')
- mix_static_grad: float32 [2, 4, 6], replicated
- mix_weight_grad: float32 [2, 2048, 6], replicated
- mix_scale_grad: float32 [2, 6], replicated
The draws below stay inside these ranges and needn't reach their ends.
Inputs may be any that keep to these rules, and one draw needn't show every extreme that they name: The lengths of the 3 sequences that the permutation deals to one data group add up to 1023 or less. `permutation`: each number appears once.
All inputs are finite; a program needn't handle non-finite values.
Results may differ from the reference program's by a relative error of at most 0.014.
The reference program's roundings to bfloat16 on the way count: a program that leaves them out, or rounds other values in their place, can miss the bound.
Values may be sent and summed in bfloat16 or wider, within the bound.
A program may use at most 384 MiB of HBM per device.

```python
import jax
import jax.numpy as jnp
from jax import lax

D = 2048
HEADS = 16
HEAD_DIM = 128
FF = 8192
STREAMS = 4
GROUP_TOK = 1024
SEQ_GROUP = 3
HQ = 2048
TOKENS = 8192
N_DP = 8
N_TENSOR = 4


def dealing(key):
    shard_rows = GROUP_TOK // N_TENSOR
    short_most = max(shard_rows // 4, 1)
    subkeys = jax.random.split(key, 5)
    shorts = jax.random.randint(subkeys[0], (N_DP, SEQ_GROUP - 1), 1, short_most + 1).astype(jnp.int32)
    spare_rows = jax.random.randint(subkeys[1], (N_DP,), 1, short_most + 1).astype(jnp.int32)
    chosen = jax.random.randint(subkeys[2], (), 0, N_DP)
    picked_group = jnp.arange(N_DP) == chosen
    shorts = jnp.where(picked_group[:, None], 1, shorts).astype(jnp.int32)
    spare_rows = jnp.where(picked_group, 1, spare_rows).astype(jnp.int32)
    longest = (GROUP_TOK - jnp.sum(shorts, axis=1) - spare_rows).astype(jnp.int32)
    placed = jax.random.randint(subkeys[3], (N_DP,), 0, SEQ_GROUP).astype(jnp.int32)
    slot_ids = jnp.arange(SEQ_GROUP, dtype=jnp.int32)[None, :]
    short_index = jnp.clip(slot_ids - (slot_ids > placed[:, None]).astype(jnp.int32), 0, SEQ_GROUP - 2)
    picked = jnp.take_along_axis(shorts, short_index, axis=1)
    slot_lengths = jnp.where(slot_ids == placed[:, None], longest[:, None], picked).astype(jnp.int32)
    dealt = jax.random.permutation(subkeys[4], N_DP * SEQ_GROUP).astype(jnp.int32)
    lengths = jnp.zeros((N_DP * SEQ_GROUP,), jnp.int32).at[dealt].set(slot_lengths.reshape(-1))
    return (lengths, dealt)


def draw_lengths(key, part):
    lengths, dealt = dealing(key)
    return lengths


def draw_permutation(key, part):
    lengths, dealt = dealing(key)
    return dealt


def shard_levels(rng, dims, cuts, least, top_value):
    factor_of, own = 1.0, jax.random.fold_in(rng, 6)
    for dim, blocks in cuts:
        heights = jnp.exp(jax.random.uniform(jax.random.fold_in(own, dim), (blocks,), jnp.float32, least / len(cuts), top_value / len(cuts)))
        factor_of = factor_of * jnp.repeat(heights, dims[dim] // blocks).reshape([-1 if axis == dim else 1 for axis in range(len(dims))])
    return factor_of


def normal_values(own_key, shape, deviation, limit, pieces=(), kind=jnp.bfloat16):
    loudness = shard_levels(own_key, shape, pieces, -0.22, 0.18) if pieces else 1.0
    values = jax.random.normal(own_key, shape, jnp.float32) * deviation * loudness
    return jnp.minimum(jnp.maximum(values, -limit), limit).astype(kind)


def setup_inputs(seed: int = 0) -> dict:
    keys = jax.random.split(jax.random.key(seed), 15)
    streams = normal_values(keys[0], (TOKENS, STREAMS, D), 1.0, 6.0, ((0, 32),))
    cotangent = normal_values(keys[1], (TOKENS, STREAMS, D), 1.0, 6.0, ((0, 32),))
    lengths = draw_lengths(jax.random.fold_in(keys[14], 71), 0)
    permutation = draw_permutation(jax.random.fold_in(keys[14], 71), 0)
    query_weight = normal_values(keys[4], (D, HQ), D ** -0.5, 0.125, ((0, 8), (1, 4)))
    key_weight = normal_values(keys[5], (D, HQ), D ** -0.5, 0.125, ((0, 8), (1, 4)))
    value_weight = normal_values(keys[6], (D, HQ), D ** -0.5, 0.125, ((0, 8), (1, 4)))
    out_weight = normal_values(keys[7], (D, HQ), (max(HQ // 512, 1)) ** -0.5, 3.0, ((0, 8), (1, 4)))
    gate_weight = normal_values(keys[8], (D, FF), D ** -0.5, 0.125, ((0, 8), (1, 4)))
    up_weight = normal_values(keys[9], (D, FF), D ** -0.5, 0.125, ((0, 8), (1, 4)))
    down_weight = normal_values(keys[10], (D, FF), FF ** -0.5, 0.0625, ((0, 8), (1, 4)))
    mix_static = jnp.clip(jax.random.uniform(keys[11], (2, STREAMS, STREAMS + 2), jnp.float32, -1.0, 1.0), -1.0, 1.0)
    mix_weight = normal_values(keys[12], (2, D, STREAMS + 2), D ** -0.5, 0.125, (), jnp.float32)
    mix_scale = jnp.clip(jax.random.uniform(keys[13], (2, STREAMS + 2), jnp.float32, 0.3, 1.0), 0.3, 1.0)
    return dict(streams=streams, cotangent=cotangent, lengths=lengths, permutation=permutation, query_weight=query_weight, key_weight=key_weight, value_weight=value_weight, out_weight=out_weight, gate_weight=gate_weight, up_weight=up_weight, down_weight=down_weight, mix_static=mix_static, mix_weight=mix_weight, mix_scale=mix_scale)


@jax.custom_vjp
def low(v):
    return lax.optimization_barrier(v.astype(jnp.bfloat16)).astype(jnp.float32)

@jax.custom_vjp
def low_back(v):
    return v

def low_keep(v):
    return (low(v), None)

def low_pass(kept, grad):
    return (grad,)

def back_keep(v):
    return (v, None)

def back_low(kept, grad):
    return (low(grad),)
low.defvjp(low_keep, low_pass)
low_back.defvjp(back_keep, back_low)
EPSILON = 1e-05
THETA = 10000.0
HIGHEST = lax.Precision.HIGHEST
MASKED = -1e+30

def product(left, right):
    return jnp.dot(left, right, precision=HIGHEST, preferred_element_type=jnp.float32)

def layer_norm(values):
    centre = values - lax.optimization_barrier(jnp.mean(values, axis=-1, keepdims=True))
    spread = lax.optimization_barrier(jnp.mean(centre * centre, axis=-1, keepdims=True))
    return centre * lax.rsqrt(spread + EPSILON)

def mix_streams(streams, static, mix_weight, mix_scale):
    stream_count = static.shape[0]
    normed = layer_norm(streams)
    dynamic = jnp.tanh(jnp.einsum('rjd,dc->rjc', normed, mix_weight, precision=HIGHEST))
    coeffs = static[None] + mix_scale[None, None, :] * dynamic
    entering = jnp.einsum('rj,rjd->rd', coeffs[:, :, 0], streams, precision=HIGHEST)
    carried = jnp.einsum('rji,rjd->rid', coeffs[:, :, 1:stream_count + 1], streams, precision=HIGHEST)
    return (layer_norm(entering), carried, coeffs[:, :, stream_count + 1])

def rope_tables(position, head_dim):
    halfway = head_dim // 2
    frequency = THETA ** (-(2.0 * jnp.arange(halfway, dtype=jnp.float32)) / head_dim)
    angles = position.astype(jnp.float32)[:, None] * frequency[None, :]
    angles = jnp.concatenate([angles, angles], axis=1)
    return (jnp.cos(angles), jnp.sin(angles))

def rotate(heads_in, cosine_table, sine_table):
    halfway = heads_in.shape[-1] // 2
    turned = jnp.concatenate([-heads_in[..., halfway:], heads_in[..., :halfway]], axis=-1)
    return heads_in * cosine_table[:, None, :] + turned * sine_table[:, None, :]

def segments_from(slot_lengths, group_rows):
    bounds = jnp.cumsum(slot_lengths).astype(jnp.int32)
    row_ids = jnp.arange(group_rows, dtype=jnp.int32)
    segment = lax.optimization_barrier(jnp.sum((row_ids[:, None] >= bounds[None, :]).astype(jnp.int32), axis=1)).astype(jnp.int32)
    starting = jnp.concatenate([jnp.zeros((1,), jnp.int32), bounds])
    labels = jnp.arange(starting.shape[0], dtype=jnp.int32)
    begins = lax.optimization_barrier(jnp.sum(jnp.where(segment[:, None] == labels[None, :], starting[None, :], 0), axis=1)).astype(jnp.int32)
    return (segment, (row_ids - begins).astype(jnp.int32))

def group_layer(block_streams, segment, position, weights, mixing):
    query_weight, key_weight, value_weight, out_weight, gate_weight, up_weight, down_weight = weights
    mix_static, mix_weight, mix_scale = mixing
    group_rows = block_streams.shape[0]
    cosine_table, sine_table = rope_tables(position, HEAD_DIM)
    row_ids = jnp.arange(group_rows, dtype=jnp.int32)
    allowed = (segment[:, None] == segment[None, :]) & (row_ids[None, :] <= row_ids[:, None])
    normed, carried, branch = mix_streams(block_streams, mix_static[0], mix_weight[0], mix_scale[0])
    attention_input = low(normed)
    query_heads = low(rotate(low_back(product(attention_input, query_weight)).reshape(group_rows, HEADS, HEAD_DIM), cosine_table, sine_table))
    key_heads = low(rotate(low_back(product(attention_input, key_weight)).reshape(group_rows, HEADS, HEAD_DIM), cosine_table, sine_table))
    value_heads = low_back(low(product(attention_input, value_weight))).reshape(group_rows, HEADS, HEAD_DIM)
    scores = low_back(jnp.einsum('qhd,khd->hqk', query_heads, key_heads, precision=HIGHEST) * HEAD_DIM ** (-0.5))
    scores = jnp.where(allowed[None], scores, MASKED)
    highest = lax.optimization_barrier(jnp.max(scores, axis=-1, keepdims=True))
    exponent = jnp.exp(scores - highest)
    probabilities = low(exponent / lax.optimization_barrier(jnp.sum(exponent, axis=-1, keepdims=True)))
    attended = low_back(low(jnp.einsum('hqk,khd->qhd', probabilities, value_heads, precision=HIGHEST))).reshape(group_rows, HQ)
    attention_output = low_back(product(attended, out_weight.T))
    middle = carried + branch[:, :, None] * attention_output[:, None, :]
    normed_ffn, carried_ffn, branch_ffn = mix_streams(middle, mix_static[1], mix_weight[1], mix_scale[1])
    feedforward_input = low(normed_ffn)
    gate_value = low_back(product(feedforward_input, gate_weight))
    up_value = low_back(product(feedforward_input, up_weight))
    hidden = low(gate_value / (1.0 + jnp.exp(-gate_value)) * up_value)
    feedforward_output = low_back(product(hidden, down_weight.T))
    return carried_ffn + branch_ffn[:, :, None] * feedforward_output[:, None, :]

def reference(streams, cotangent, lengths, permutation, query_weight, key_weight, value_weight, out_weight, gate_weight, up_weight, down_weight, mix_static, mix_weight, mix_scale):
    slot_lengths = lengths[permutation].reshape(N_DP, SEQ_GROUP)
    segments, positions = jax.vmap(lambda one_group: segments_from(one_group, GROUP_TOK))(slot_lengths)
    valid_rows = (segments < SEQ_GROUP).astype(jnp.float32).reshape(TOKENS)
    weights = tuple((matrix.astype(jnp.float32) for matrix in (query_weight, key_weight, value_weight, out_weight, gate_weight, up_weight, down_weight)))
    mixing = (mix_static, mix_weight, mix_scale)
    inputs = streams.astype(jnp.float32)
    checked_layer = jax.checkpoint(group_layer)

    def whole_layer(inputs, weights, mixing):
        grouped = inputs.reshape(N_DP, GROUP_TOK, STREAMS, D)

        def per_group(packed):
            return checked_layer(packed[0], packed[1], packed[2], weights, mixing)
        outputs = lax.map(per_group, (grouped, segments, positions))
        return outputs.reshape(TOKENS, STREAMS, D)
    outputs, pullback = jax.vjp(whole_layer, inputs, weights, mixing)
    input_grad, weight_grads, mixing_grads = pullback(cotangent.astype(jnp.float32) * valid_rows[:, None, None])
    return (outputs.astype(jnp.bfloat16), input_grad.astype(jnp.bfloat16), weight_grads[0], weight_grads[1], weight_grads[2], weight_grads[3], weight_grads[4], weight_grads[5], weight_grads[6], mixing_grads[0], mixing_grads[1], mixing_grads[2])
```

```python
import functools
import jax
import jax.numpy as jnp
from jax import lax
from jax.experimental import pallas as pl
from jax.experimental.pallas import tpu as pltpu
from jax.sharding import PartitionSpec as P

HEAD_DIM = 128
EPSILON = 1e-05
THETA = 10000.0
MASKED = -1e30
LANES = 128
GROUP = 16
CHUNK = 512
PARAMS = pltpu.CompilerParams(vmem_limit_bytes=50 * 1024 * 1024)


def matmul(left, right):
    return jnp.dot(left, right, preferred_element_type=jnp.float32)


def times_transposed(left, right):
    return lax.dot_general(
        left, right, (((1,), (1,)), ((), ())), preferred_element_type=jnp.float32
    )


def transposed_times(left, right):
    return lax.dot_general(
        left, right, (((0,), (0,)), ((), ())), preferred_element_type=jnp.float32
    )


def lanes_of(rows):
    return lax.broadcasted_iota(jnp.int32, (rows, LANES), 1)


def column(values, lane):
    return values[:, lane : lane + 1]


def place(values, columns, first):
    lane = lanes_of(values.shape[0])
    for offset, one in enumerate(columns):
        values = jnp.where(lane == first + offset, one, values)
    return values


def fold(values):
    total = values[:, :LANES]
    for start in range(LANES, values.shape[1], LANES):
        total = total + values[:, start : start + LANES]
    return total


def row_sum(values):
    return jnp.sum(values, axis=1, keepdims=True)


def rolled(values, shift):
    shift = shift % LANES
    return values if shift == 0 else pltpu.roll(values, shift, 1)


def coefficients(projected, means, rsqrts, param_ref, streams, uses, parts, centred):
    rows = projected[0].shape[0]
    lane = lanes_of(rows)
    gathered = jnp.zeros((rows, LANES), jnp.float32)
    for j in range(streams):
        total = projected[j]
        for part in range(1, parts):
            total = total + rolled(projected[j], -part * uses)
        if not centred:
            total = total - means[j] * param_ref[2:3, :]
        total = total * rsqrts[j]
        inside = (lane >= j * uses) & (lane < (j + 1) * uses)
        gathered = jnp.where(inside, rolled(total, j * uses), gathered)
    bent = jnp.tanh(gathered)
    return gathered, bent, param_ref[0:1, :] + param_ref[1:2, :] * bent


def pack_saved(coeffs, bent, gathered, means, rsqrts, mean_e, rsqrt_e, streams, uses):
    lane = lanes_of(coeffs.shape[0])
    count = streams * uses
    saved = jnp.where(lane < count, coeffs, 0.0)
    saved = jnp.where((lane >= count) & (lane < 2 * count), rolled(bent, count), saved)
    saved = jnp.where((lane >= 2 * count) & (lane < 3 * count), rolled(gathered, 2 * count), saved)
    return place(saved, [*means, *rsqrts, mean_e, rsqrt_e], 3 * count)


def centre_stats(total, values_of, width):
    mean = row_sum(total) * (1.0 / width)
    spread = None
    for start in range(0, width, CHUNK):
        centred = values_of(start) - mean
        square = fold(centred * centred)
        spread = square if spread is None else spread + square
    return mean, lax.rsqrt(row_sum(spread) * (1.0 / width) + EPSILON)


def entering_norm(read, coeffs, streams, uses, width, entering_ref, rows):
    total = None
    for start in range(0, width, CHUNK):
        entering = column(coeffs, 0) * read(0, start)
        for j in range(1, streams):
            entering = entering + column(coeffs, j * uses) * read(j, start)
        entering_ref[rows, start : start + CHUNK] = entering
        part = fold(entering)
        total = part if total is None else total + part
    return centre_stats(total, lambda start: entering_ref[rows, start : start + CHUNK], width)


def open_attention_kernel(streams, uses, width, x_ref, w_ref, param_ref, normed_ref, saved_ref, raw_ref, entering_ref):
    block = x_ref.shape[0]
    stacked = jnp.concatenate([x_ref[:, j * width : (j + 1) * width] for j in range(streams)], axis=0)
    raw_ref[...] = jnp.dot(stacked, w_ref[...], preferred_element_type=jnp.float32)

    def body(index, carry):
        first = pl.multiple_of(index * GROUP, GROUP)
        rows = pl.ds(first, GROUP)

        def read(j, start):
            return x_ref[rows, j * width + start : j * width + start + CHUNK].astype(jnp.float32)

        means, rsqrts, projected = [], [], []
        for j in range(streams):
            total = None
            for start in range(0, width, CHUNK):
                part = fold(read(j, start))
                total = part if total is None else total + part
            mean, rsqrt = centre_stats(total, functools.partial(read, j), width)
            means.append(mean)
            rsqrts.append(rsqrt)
            projected.append(raw_ref[pl.ds(pl.multiple_of(j * block + first, GROUP), GROUP), :])
        gathered, bent, coeffs = coefficients(projected, means, rsqrts, param_ref, streams, uses, 3, False)
        mean_e, rsqrt_e = entering_norm(read, coeffs, streams, uses, width, entering_ref, rows)
        for start in range(0, width, CHUNK):
            normed_ref[rows, start : start + CHUNK] = (
                (entering_ref[rows, start : start + CHUNK] - mean_e) * rsqrt_e
            ).astype(jnp.bfloat16)
        saved_ref[rows, :] = pack_saved(coeffs, bent, gathered, means, rsqrts, mean_e, rsqrt_e, streams, uses)
        return carry

    lax.fori_loop(0, block // GROUP, body, 0)


def open_feedforward_kernel(
    streams, uses, width,
    x_ref, saved_a_ref, arrived_ref, partial_ref, g_ref, valid_ref, w_ref, param_ref,
    normed_ref, grad_ref, saved_ref, h_ref, out_ref,
    high_ref, low_ref, raw_ref, entering_ref, stats_ref,
):
    block = x_ref.shape[0]
    count = streams * uses

    def first_pass(index, carry):
        first = pl.multiple_of(index * GROUP, GROUP)
        rows = pl.ds(first, GROUP)
        coeffs = saved_a_ref[rows, :]
        totals = [None] * streams
        for start in range(0, width, CHUNK):
            out = arrived_ref[rows, start : start + CHUNK].astype(jnp.float32) + partial_ref[rows, start : start + CHUNK]
            out_ref[rows, start : start + CHUNK] = out
            values = [
                x_ref[rows, j * width + start : j * width + start + CHUNK].astype(jnp.float32)
                for j in range(streams)
            ]
            for i in range(streams):
                mixed = column(coeffs, i * uses + streams + 1) * out
                for j in range(streams):
                    mixed = mixed + column(coeffs, j * uses + 1 + i) * values[j]
                h_ref[rows, i * width + start : i * width + start + CHUNK] = mixed
                part = fold(mixed)
                totals[i] = part if totals[i] is None else totals[i] + part
        stats = jnp.zeros((GROUP, LANES), jnp.float32)
        means, rsqrts = [], []
        for i in range(streams):
            mean = row_sum(totals[i]) * (1.0 / width)
            spread = None
            for start in range(0, width, CHUNK):
                centred = h_ref[rows, i * width + start : i * width + start + CHUNK] - mean
                high = centred.astype(jnp.bfloat16)
                target = pl.ds(pl.multiple_of(i * block + first, GROUP), GROUP)
                high_ref[target, start : start + CHUNK] = high
                low_ref[target, start : start + CHUNK] = (centred - high.astype(jnp.float32)).astype(jnp.bfloat16)
                square = fold(centred * centred)
                spread = square if spread is None else spread + square
            means.append(mean)
            rsqrts.append(lax.rsqrt(row_sum(spread) * (1.0 / width) + EPSILON))
        stats_ref[rows, :] = place(stats, [*means, *rsqrts], 0)
        return carry

    lax.fori_loop(0, block // GROUP, first_pass, 0)
    raw_ref[...] = jnp.dot(high_ref[...], w_ref[...], preferred_element_type=jnp.float32) + jnp.dot(
        low_ref[...], w_ref[...], preferred_element_type=jnp.float32
    )

    def second_pass(index, carry):
        first = pl.multiple_of(index * GROUP, GROUP)
        rows = pl.ds(first, GROUP)
        stats = stats_ref[rows, :]
        means = [column(stats, j) for j in range(streams)]
        rsqrts = [column(stats, streams + j) for j in range(streams)]
        projected = [raw_ref[pl.ds(pl.multiple_of(j * block + first, GROUP), GROUP), :] for j in range(streams)]
        gathered, bent, coeffs = coefficients(projected, means, rsqrts, param_ref, streams, uses, 2, True)

        def read(j, start):
            return h_ref[rows, j * width + start : j * width + start + CHUNK]

        mean_e, rsqrt_e = entering_norm(read, coeffs, streams, uses, width, entering_ref, rows)
        branch = [column(coeffs, i * uses + streams + 1) * valid_ref[rows, 0:1] for i in range(streams)]
        for start in range(0, width, CHUNK):
            normed_ref[rows, start : start + CHUNK] = (
                (entering_ref[rows, start : start + CHUNK] - mean_e) * rsqrt_e
            ).astype(jnp.bfloat16)
            grad = None
            for i in range(streams):
                term = branch[i] * g_ref[rows, i * width + start : i * width + start + CHUNK].astype(jnp.float32)
                grad = term if grad is None else grad + term
            grad_ref[rows, start : start + CHUNK] = grad.astype(jnp.bfloat16)
        saved_ref[rows, :] = pack_saved(coeffs, bent, gathered, means, rsqrts, mean_e, rsqrt_e, streams, uses)
        return carry

    lax.fori_loop(0, block // GROUP, second_pass, 0)


def finish_kernel(streams, uses, width, h_ref, saved_ref, arrived_ref, partial_ref, y_ref):
    def body(index, carry):
        rows = pl.ds(pl.multiple_of(index * GROUP, GROUP), GROUP)
        coeffs = saved_ref[rows, :]
        for start in range(0, width, CHUNK):
            out = arrived_ref[rows, start : start + CHUNK].astype(jnp.float32) + partial_ref[rows, start : start + CHUNK]
            values = [h_ref[rows, j * width + start : j * width + start + CHUNK] for j in range(streams)]
            for i in range(streams):
                mixed = column(coeffs, i * uses + streams + 1) * out
                for j in range(streams):
                    mixed = mixed + column(coeffs, j * uses + 1 + i) * values[j]
                y_ref[rows, i * width + start : i * width + start + CHUNK] = mixed.astype(jnp.bfloat16)
        return carry

    lax.fori_loop(0, h_ref.shape[0] // GROUP, body, 0)


def close_kernel(streams, uses, width, inner, *refs):
    if inner:
        (h_ref, saved_ref, g_ref, arrived_ref, partial_ref, arrived_f_ref, partial_f_ref, valid_ref, saved_a_ref,
         out_a_ref, wt_ref, param_ref, grad_ref, below_ref, branch_ref, weight_ref, small_ref,
         centre_ref, du_ref, left_ref, dl_ref, cols_ref, sums_ref) = refs
    else:
        (h_ref, saved_ref, g_ref, arrived_ref, partial_ref, branch_in_ref, wt_ref, param_ref,
         grad_ref, weight_ref, small_ref, centre_ref, du_ref, left_ref, dl_ref, cols_ref, sums_ref) = refs
    block = h_ref.shape[0]
    count = streams * uses
    step = pl.program_id(0)
    base = pl.multiple_of(step * block, GROUP)
    all_rows = centre_ref.shape[0] // streams

    @pl.when(step == 0)
    def _():
        sums_ref[...] = jnp.zeros_like(sums_ref)

    def read_h(rows, j, start):
        return h_ref[rows, j * width + start : j * width + start + CHUNK].astype(jnp.float32)

    def read_g(rows, i, start):
        values = g_ref[rows, i * width + start : i * width + start + CHUNK].astype(jnp.float32)
        return values * valid_ref[rows, 0:1] if inner else values

    def read_dn(rows, start):
        return arrived_ref[rows, start : start + CHUNK].astype(jnp.float32) + partial_ref[rows, start : start + CHUNK]

    def first_pass(index, carry):
        first = pl.multiple_of(index * GROUP, GROUP)
        rows = pl.ds(first, GROUP)
        saved = saved_ref[rows, :]
        means = [column(saved, 3 * count + j) for j in range(streams)]
        rsqrts = [column(saved, 3 * count + streams + j) for j in range(streams)]
        mean_e = column(saved, 3 * count + 2 * streams)
        rsqrt_e = column(saved, 3 * count + 2 * streams + 1)
        sums = {}

        def add(key, values):
            part = fold(values)
            sums[key] = part if key not in sums else sums[key] + part

        for start in range(0, width, CHUNK):
            dn = read_dn(rows, start)
            values = [read_h(rows, j, start) for j in range(streams)]
            for j in range(streams):
                target = pl.ds(pl.multiple_of(j * all_rows + base + first, GROUP), GROUP)
                centre_ref[target, start : start + CHUNK] = (values[j] - means[j]).astype(jnp.bfloat16)
            entering = column(saved, 0) * values[0]
            for j in range(1, streams):
                entering = entering + column(saved, j * uses) * values[j]
            normed = (entering - mean_e) * rsqrt_e
            add("dn", dn)
            add("dnn", dn * normed)
            for j in range(streams):
                add(("dnh", j), dn * values[j])
                add(("nh", j), normed * values[j])
            if inner:
                out = (
                    arrived_f_ref[rows, start : start + CHUNK].astype(jnp.float32)
                    + partial_f_ref[rows, start : start + CHUNK]
                )
            for i in range(streams):
                g = read_g(rows, i, start)
                for j in range(streams):
                    add(("gh", j, i), g * values[j])
                if inner:
                    add(("go", i), g * out)
        total = {key: row_sum(value) for key, value in sums.items()}
        mean_dn = total["dn"] * (1.0 / width)
        mean_dnn = total["dnn"] * (1.0 / width)
        columns = []
        for j in range(streams):
            columns.append(
                rsqrt_e * (total["dnh", j] - total["dn"] * means[j] - mean_dnn * total["nh", j])
            )
            columns.extend(total["gh", j, i] for i in range(streams))
            columns.append(total["go", j] if inner else branch_in_ref[rows, j : j + 1])
        d_coeffs = place(jnp.zeros((GROUP, LANES), jnp.float32), columns, 0)
        lane = lanes_of(GROUP)
        bent = jnp.where(lane < count, rolled(saved, -count), 0.0)
        projected = jnp.where(lane < count, rolled(saved, -2 * count), 0.0)
        sums_ref[0] += d_coeffs
        sums_ref[1] += d_coeffs * bent
        du = d_coeffs * param_ref[1:2, :] * (1.0 - bent * bent)
        with_mean = du * param_ref[3:4, :] * (1.0 / width)
        with_value = du * projected * (1.0 / width)
        shifts, slopes = [], []
        scaled = jnp.zeros((GROUP, LANES), jnp.float32)
        for j in range(streams):
            inside = (lane >= j * uses) & (lane < (j + 1) * uses)
            slope = rsqrts[j] * rsqrts[j] * row_sum(jnp.where(inside, with_value, 0.0))
            shifts.append(means[j] * slope - rsqrts[j] * row_sum(jnp.where(inside, with_mean, 0.0)))
            slopes.append(slope)
            scaled = jnp.where(inside, du * rsqrts[j], scaled)
        high = scaled.astype(jnp.bfloat16).astype(jnp.float32)
        low = (scaled - high).astype(jnp.bfloat16).astype(jnp.float32)
        spread = jnp.where(lane < count, high, 0.0)
        spread = jnp.where((lane >= count) & (lane < 2 * count), rolled(low, count), spread)
        spread = jnp.where((lane >= 2 * count) & (lane < 3 * count), rolled(high, 2 * count), spread)
        for j in range(streams):
            mine = lane < 0
            for part in range(3):
                begin = part * count + j * uses
                mine = mine | ((lane >= begin) & (lane < begin + uses))
            left_ref[pl.ds(pl.multiple_of(j * block + first, GROUP), GROUP), :] = jnp.where(
                mine, spread, 0.0
            ).astype(jnp.bfloat16)
            pair = jnp.where(lane < uses, rolled(high, -j * uses), 0.0)
            pair = jnp.where((lane >= uses) & (lane < 2 * uses), rolled(low, uses - j * uses), pair)
            du_ref[pl.ds(pl.multiple_of(j * all_rows + base + first, GROUP), GROUP), :] = pair.astype(jnp.bfloat16)
        cols_ref[rows, :] = place(
            jnp.zeros((GROUP, LANES), jnp.float32), [mean_dn, mean_dnn, *shifts, *slopes], 0
        )
        return carry

    lax.fori_loop(0, block // GROUP, first_pass, 0)
    dl_ref[...] = jnp.dot(left_ref[...], wt_ref[...], preferred_element_type=jnp.float32)

    def second_pass(index, carry):
        first = pl.multiple_of(index * GROUP, GROUP)
        rows = pl.ds(first, GROUP)
        saved = saved_ref[rows, :]
        cols = cols_ref[rows, :]
        mean_e = column(saved, 3 * count + 2 * streams)
        rsqrt_e = column(saved, 3 * count + 2 * streams + 1)
        scaled_mean = column(cols, 0) * rsqrt_e
        scaled_slope = column(cols, 1) * rsqrt_e
        branch_sums = [None] * streams
        for start in range(0, width, CHUNK):
            values = [read_h(rows, j, start) for j in range(streams)]
            entering = column(saved, 0) * values[0]
            for j in range(1, streams):
                entering = entering + column(saved, j * uses) * values[j]
            normed = (entering - mean_e) * rsqrt_e
            de = rsqrt_e * read_dn(rows, start) - scaled_mean - normed * scaled_slope
            gs = [read_g(rows, i, start) for i in range(streams)]
            below = None
            for j in range(streams):
                grad = column(saved, j * uses) * de + column(cols, 2 + j)
                grad = grad - values[j] * column(cols, 2 + streams + j)
                grad = grad + dl_ref[pl.ds(pl.multiple_of(j * block + first, GROUP), GROUP), start : start + CHUNK]
                for i in range(streams):
                    grad = grad + column(saved, j * uses + 1 + i) * gs[i]
                grad_ref[rows, j * width + start : j * width + start + CHUNK] = grad.astype(grad_ref.dtype)
                if inner:
                    part = fold(grad * out_a_ref[rows, start : start + CHUNK])
                    branch_sums[j] = part if branch_sums[j] is None else branch_sums[j] + part
                    term = saved_a_ref[rows, j * uses + streams + 1 : j * uses + streams + 2] * grad
                    below = term if below is None else below + term
            if inner:
                below_ref[rows, start : start + CHUNK] = below.astype(jnp.bfloat16)
        if inner:
            branch_ref[rows, :] = place(
                jnp.zeros((GROUP, LANES), jnp.float32), [row_sum(one) for one in branch_sums], 0
            )
        return carry

    lax.fori_loop(0, block // GROUP, second_pass, 0)

    @pl.when(step == pl.num_programs(0) - 1)
    def _():
        product = lax.dot_general(
            du_ref[...], centre_ref[...], (((0,), (0,)), ((), ())), preferred_element_type=jnp.float32
        )
        weight_ref[...] = product[: weight_ref.shape[0]]
        small_ref[0:1, :] = jnp.sum(sums_ref[0], axis=0, keepdims=True)
        small_ref[1:2, :] = jnp.sum(sums_ref[1], axis=0, keepdims=True)


def rows_block(rows):
    return min(64, rows)


def specs_for(arrays, block, whole):
    return [
        pl.BlockSpec(a.shape, lambda i: (0, 0)) if k in whole else pl.BlockSpec((block, a.shape[1]), lambda i: (i, 0))
        for k, a in enumerate(arrays)
    ]


def rounded(values):
    return lax.reduce_precision(values, 8, 7)


def mix_tables(static, weight, scale):
    streams, uses = static.shape
    width = weight.shape[0]
    high = rounded(weight)
    middle = rounded(weight - high)
    low = rounded(weight - high - middle)
    forward = jnp.pad(jnp.concatenate([high, middle, low], axis=1), ((0, 0), (0, LANES - 3 * uses))).astype(jnp.bfloat16)
    tall = [jnp.tile(part.T, (streams, 1)) for part in (high, high, middle)]
    backward = jnp.pad(jnp.concatenate(tall, axis=0), ((0, LANES - 3 * streams * uses), (0, 0))).astype(jnp.bfloat16)
    total = jnp.sum(weight, axis=0)
    count = streams * uses

    def row(values):
        return jnp.pad(values, (0, LANES - values.shape[0]))[None]

    params = jnp.concatenate(
        [row(static.reshape(count)), row(jnp.tile(scale, streams)), row(total), row(jnp.tile(total, streams)), jnp.zeros((4, LANES), jnp.float32)]
    )
    return forward, backward, params


def open_attention(x, tables, streams, uses):
    rows, width = x.shape[0], x.shape[1] // streams
    block = rows_block(rows)
    arrays = [x, tables[0], tables[2]]
    return pl.pallas_call(
        functools.partial(open_attention_kernel, streams, uses, width),
        grid=(rows // block,),
        in_specs=specs_for(arrays, block, {1, 2}),
        out_specs=[pl.BlockSpec((block, width), lambda i: (i, 0)), pl.BlockSpec((block, LANES), lambda i: (i, 0))],
        out_shape=[jax.ShapeDtypeStruct((rows, width), jnp.bfloat16), jax.ShapeDtypeStruct((rows, LANES), jnp.float32)],
        scratch_shapes=[pltpu.VMEM((streams * block, LANES), jnp.float32), pltpu.VMEM((block, width), jnp.float32)],
        compiler_params=PARAMS,
        name="open_attention",
    )(*arrays)


def open_feedforward(x, saved_a, arrived, partial, g, valid, tables, streams, uses):
    rows, width = x.shape[0], x.shape[1] // streams
    block = rows_block(rows)
    arrays = [x, saved_a, arrived, partial, g, valid, tables[0], tables[2]]

    def by_rows(columns):
        return pl.BlockSpec((block, columns), lambda i: (i, 0))

    return pl.pallas_call(
        functools.partial(open_feedforward_kernel, streams, uses, width),
        grid=(rows // block,),
        in_specs=specs_for(arrays, block, {6, 7}),
        out_specs=[by_rows(width), by_rows(width), by_rows(LANES), by_rows(streams * width), by_rows(width)],
        out_shape=[
            jax.ShapeDtypeStruct((rows, width), jnp.bfloat16),
            jax.ShapeDtypeStruct((rows, width), jnp.bfloat16),
            jax.ShapeDtypeStruct((rows, LANES), jnp.float32),
            jax.ShapeDtypeStruct((rows, streams * width), jnp.float32),
            jax.ShapeDtypeStruct((rows, width), jnp.float32),
        ],
        scratch_shapes=[
            pltpu.VMEM((streams * block, width), jnp.bfloat16),
            pltpu.VMEM((streams * block, width), jnp.bfloat16),
            pltpu.VMEM((streams * block, LANES), jnp.float32),
            pltpu.VMEM((block, width), jnp.float32),
            pltpu.VMEM((block, LANES), jnp.float32),
        ],
        compiler_params=PARAMS,
        name="open_feedforward",
    )(*arrays)


def finish(h, saved, arrived, partial, streams, uses):
    rows, width = h.shape[0], h.shape[1] // streams
    block = rows_block(rows)
    arrays = [h, saved, arrived, partial]
    return pl.pallas_call(
        functools.partial(finish_kernel, streams, uses, width),
        grid=(rows // block,),
        in_specs=specs_for(arrays, block, set()),
        out_specs=pl.BlockSpec((block, streams * width), lambda i: (i, 0)),
        out_shape=jax.ShapeDtypeStruct((rows, streams * width), jnp.bfloat16),
        compiler_params=PARAMS,
        name="finish",
    )(*arrays)


def close_mix(inner, arrays, tables, streams, uses):
    h = arrays[0]
    rows, width = h.shape[0], h.shape[1] // streams
    block = rows_block(rows)
    arrays = [*arrays, tables[1], tables[2]]
    last = len(arrays)

    def by_rows(columns):
        return pl.BlockSpec((block, columns), lambda i: (i, 0))

    def fixed(height, columns):
        return pl.BlockSpec((height, columns), lambda i: (0, 0))

    out_specs = [by_rows(streams * width)]
    out_shape = [jax.ShapeDtypeStruct((rows, streams * width), jnp.float32 if inner else jnp.bfloat16)]
    if inner:
        out_specs += [by_rows(width), by_rows(LANES)]
        out_shape += [
            jax.ShapeDtypeStruct((rows, width), jnp.bfloat16),
            jax.ShapeDtypeStruct((rows, LANES), jnp.float32),
        ]
    out_specs += [fixed(16, width), fixed(8, LANES)]
    out_shape += [jax.ShapeDtypeStruct((16, width), jnp.float32), jax.ShapeDtypeStruct((8, LANES), jnp.float32)]
    return pl.pallas_call(
        functools.partial(close_kernel, streams, uses, width, inner),
        grid=(rows // block,),
        in_specs=specs_for(arrays, block, {last - 2, last - 1}),
        out_specs=out_specs,
        out_shape=out_shape,
        scratch_shapes=[
            pltpu.VMEM((streams * rows, width), jnp.bfloat16),
            pltpu.VMEM((streams * rows, LANES), jnp.bfloat16),
            pltpu.VMEM((streams * block, LANES), jnp.bfloat16),
            pltpu.VMEM((streams * block, width), jnp.float32),
            pltpu.VMEM((block, LANES), jnp.float32),
            pltpu.VMEM((2, GROUP, LANES), jnp.float32),
        ],
        compiler_params=PARAMS,
        name="close_feedforward" if inner else "close_attention",
    )(*arrays)


def mix_grads(weight_sum, small, streams, uses):
    count = streams * uses
    return (
        small[0, :count].reshape(streams, uses),
        (weight_sum[:uses] + weight_sum[uses : 2 * uses]).T,
        jnp.sum(small[1, :count].reshape(streams, uses), axis=0),
    )


QUERY_ROWS = 256


def turn(values, cosine, sine):
    return values * cosine + pltpu.roll(values, HEAD_DIM // 2, 1) * sine


def turn_back(values, cosine, sine):
    return values * cosine - pltpu.roll(values, HEAD_DIM // 2, 1) * sine


def block_offset(mine, step, size, rows):
    return pl.multiple_of(lax.rem(mine + size - step, size) * rows, rows)


def allowed_keys(start_ref, first, rows, keys):
    row = first + lax.broadcasted_iota(jnp.int32, (rows, keys), 0)
    key = lax.broadcasted_iota(jnp.int32, (rows, keys), 1)
    return (key <= row) & (key >= start_ref[first : first + rows, 0:1])


def attend_kernel(size, *refs):
    mine_ref, start_ref, cosine_ref, sine_ref = refs[:4]
    raw = [refs[4 + 3 * s : 7 + 3 * s] for s in range(size)]
    q_ref, k_ref, v_ref, out_ref, log_ref, attended_ref = refs[4 + 3 * size :]
    mine = mine_ref[0]
    block = raw[0][0].shape[0]
    total = size * block
    for step in range(size):
        rows = pl.ds(block_offset(mine, step, size, block), block)
        cosine, sine = cosine_ref[rows, :], sine_ref[rows, :]
        q_ref[rows, :] = turn(raw[step][0][...], cosine, sine).astype(jnp.bfloat16)
        k_ref[rows, :] = turn(raw[step][1][...], cosine, sine).astype(jnp.bfloat16)
        v_ref[rows, :] = raw[step][2][...].astype(jnp.bfloat16)
    height = min(QUERY_ROWS, total)
    for first in range(0, total, height):
        keys = first + height
        scores = times_transposed(q_ref[first:keys, :], k_ref[:keys, :]) * HEAD_DIM**-0.5
        scores = jnp.where(allowed_keys(start_ref, first, height, keys), scores, MASKED)
        highest = jnp.max(scores, axis=1, keepdims=True)
        exponent = jnp.exp(scores - highest)
        row_total = jnp.sum(exponent, axis=1, keepdims=True)
        probs = (exponent * (1.0 / row_total)).astype(jnp.bfloat16)
        attended_ref[first:keys, :] = jnp.dot(
            probs, v_ref[:keys, :], preferred_element_type=jnp.float32
        ).astype(jnp.bfloat16)
        log_ref[first:keys, :] = jnp.broadcast_to(highest + jnp.log(row_total), (height, LANES))
    for step in range(size):
        rows = pl.ds(block_offset(mine, step, size, block), block)
        out_ref[step * block : (step + 1) * block, :] = attended_ref[rows, :]


def attend_back_kernel(size, *refs):
    mine_ref, start_ref, cosine_ref, sine_ref, q_ref, k_ref, v_ref, log_ref = refs[:8]
    grads = refs[8 : 8 + size]
    dqkv_ref, d_out_ref, dq_ref, dk_ref, dv_ref = refs[8 + size :]
    mine = mine_ref[0]
    head, heads = pl.program_id(0), pl.num_programs(0)
    block = grads[0].shape[0]
    total = size * block
    for step in range(size):
        d_out_ref[pl.ds(block_offset(mine, step, size, block), block), :] = grads[step][...]
    height = min(QUERY_ROWS, total)
    dk_ref[...] = jnp.zeros_like(dk_ref)
    dv_ref[...] = jnp.zeros_like(dv_ref)
    for first in range(0, total, height):
        keys = first + height
        q, d_out = q_ref[first:keys, :], d_out_ref[first:keys, :]
        k, v = k_ref[:keys, :], v_ref[:keys, :]
        scores = times_transposed(q, k) * HEAD_DIM**-0.5
        probs = jnp.where(
            allowed_keys(start_ref, first, height, keys), jnp.exp(scores - log_ref[first:keys, 0:1]), 0.0
        )
        d_probs = times_transposed(d_out, v)
        centre = jnp.sum(probs * d_probs, axis=1, keepdims=True)
        d_scores = (probs * (d_probs - centre)).astype(jnp.bfloat16)
        dv_ref[:keys, :] += transposed_times(probs.astype(jnp.bfloat16), d_out)
        dk_ref[:keys, :] += transposed_times(d_scores, q)
        dq_ref[first:keys, :] = jnp.dot(d_scores, k, preferred_element_type=jnp.float32)
    for step in range(size):
        rows = pl.ds(block_offset(mine, step, size, block), block)
        cosine, sine = cosine_ref[rows, :], sine_ref[rows, :]
        target = slice(step * block, (step + 1) * block)
        for part, values in enumerate(
            (
                turn_back(dq_ref[rows, :] * HEAD_DIM**-0.5, cosine, sine),
                turn_back(dk_ref[rows, :] * HEAD_DIM**-0.5, cosine, sine),
                dv_ref[rows, :],
            )
        ):
            columns = pl.ds(pl.multiple_of((part * heads + head) * HEAD_DIM, HEAD_DIM), HEAD_DIM)
            dqkv_ref[target, columns] = values.astype(jnp.bfloat16)


def whole_spec(shape):
    return pl.BlockSpec(shape, lambda h: (0,) * len(shape))


def head_spec(rows, first=0):
    return pl.BlockSpec((rows, HEAD_DIM), lambda h: (0, first + h))


def attend(raw_blocks, mine, starts, cosine, sine):
    size, block = len(raw_blocks), raw_blocks[0].shape[0]
    heads = raw_blocks[0].shape[1] // (3 * HEAD_DIM)
    total = size * block
    flat = jax.ShapeDtypeStruct((total, heads * HEAD_DIM), jnp.bfloat16)
    return pl.pallas_call(
        functools.partial(attend_kernel, size),
        grid=(heads,),
        in_specs=[pl.BlockSpec(memory_space=pltpu.SMEM)]
        + [whole_spec(a.shape) for a in (starts, cosine, sine)]
        + [head_spec(block, part * heads) for _ in range(size) for part in range(3)],
        out_specs=[head_spec(total)] * 5,
        out_shape=[flat] * 4 + [jax.ShapeDtypeStruct(flat.shape, jnp.float32)],
        scratch_shapes=[pltpu.VMEM((total, HEAD_DIM), jnp.bfloat16)],
        compiler_params=PARAMS,
        name="attend",
    )(mine, starts, cosine, sine, *[raw for raw in raw_blocks for _ in range(3)])


def attend_back(heads_kept, grad_blocks, mine, starts, cosine, sine):
    size, block = len(grad_blocks), grad_blocks[0].shape[0]
    total, columns = heads_kept[0].shape
    heads = columns // HEAD_DIM
    return pl.pallas_call(
        functools.partial(attend_back_kernel, size),
        grid=(heads,),
        in_specs=[pl.BlockSpec(memory_space=pltpu.SMEM)]
        + [whole_spec(a.shape) for a in (starts, cosine, sine)]
        + [head_spec(total)] * 4
        + [head_spec(block)] * size,
        out_specs=whole_spec((total, 3 * columns)),
        out_shape=jax.ShapeDtypeStruct((total, 3 * columns), jnp.bfloat16),
        scratch_shapes=[pltpu.VMEM((total, HEAD_DIM), jnp.bfloat16)] + [pltpu.VMEM((total, HEAD_DIM), jnp.float32)] * 3,
        compiler_params=PARAMS,
        name="attend_back",
    )(mine, starts, cosine, sine, *heads_kept, *grad_blocks)


def ring_shift(block):
    size = lax.axis_size("tensor")
    return lax.ppermute(block, "tensor", [(i, (i + 1) % size) for i in range(size)])


def ring_gather(block):
    blocks = [block]
    for _ in range(lax.axis_size("tensor") - 1):
        blocks.append(ring_shift(blocks[-1]))
    return blocks


def ring_scatter(partials):
    total = partials[1]
    for step in range(2, len(partials) + 1):
        arrived = ring_shift(total.astype(jnp.bfloat16))
        own = partials[step % len(partials)]
        total = arrived.astype(jnp.float32) + own
    return arrived, own


def swap(values, axis, bit):
    return lax.ppermute(values, axis, [(i, i ^ (1 << bit)) for i in range(lax.axis_size(axis))])


def bit_of(axis, bit):
    return (lax.axis_index(axis) >> bit) & 1


def halves_by(bit_value, mine, other):
    return jnp.where(
        bit_value == 0, jnp.concatenate([mine, other], axis=0), jnp.concatenate([other, mine], axis=0)
    )


def product_sum(left, right):
    bits = (lax.axis_size("dp") - 1).bit_length()
    half = left.shape[1] // 2
    core = bit_of("dp", 0)
    away = transposed_times(lax.dynamic_slice_in_dim(left, (1 - core) * half, half, 1), right)
    arrived = swap(away.astype(jnp.bfloat16), "dp", 0)
    total = transposed_times(lax.dynamic_slice_in_dim(left, core * half, half, 1), right)
    total = total + arrived.astype(jnp.float32)
    gathered = []
    for part, order in zip(jnp.split(total, 2), (list(range(1, bits)), list(range(bits - 1, 0, -1)))):
        for bit in order:
            rows, which = part.shape[0] // 2, bit_of("dp", bit)
            away = lax.dynamic_slice_in_dim(part, (1 - which) * rows, rows).astype(jnp.bfloat16)
            arrived = swap(away, "dp", bit)
            part = lax.dynamic_slice_in_dim(part, which * rows, rows) + arrived.astype(jnp.float32)
        part = part.astype(jnp.bfloat16)
        for bit in reversed(order):
            part = halves_by(bit_of("dp", bit), part, swap(part, "dp", bit))
        gathered.append(part)
    mine = jnp.concatenate(gathered)
    return mine, swap(mine, "dp", 0)


def sum_everywhere(values):
    for axis in ("dp", "tensor"):
        for bit in range((lax.axis_size(axis) - 1).bit_length()):
            values = values + swap(values, axis, bit)
    return values


def in_order(halves):
    return halves_by(bit_of("dp", 0), *halves).astype(jnp.float32)


def segments_from(slot_lengths, group_rows):
    bounds = jnp.cumsum(slot_lengths)
    row_ids = jnp.arange(group_rows, dtype=jnp.int32)
    segment = jnp.sum((row_ids[:, None] >= bounds[None, :]).astype(jnp.int32), axis=1)
    starting = jnp.concatenate([jnp.zeros((1,), jnp.int32), bounds])
    labels = jnp.arange(starting.shape[0], dtype=jnp.int32)
    begins = jnp.sum(jnp.where(segment[:, None] == labels[None, :], starting[None, :], 0), axis=1)
    return (segment, begins)


def group_layout(lengths, permutation, group_rows, seq_count):
    group_index = lax.axis_index("dp")
    chosen = lax.dynamic_slice_in_dim(permutation, group_index * seq_count, seq_count)
    matches = chosen[:, None] == jnp.arange(permutation.shape[0], dtype=jnp.int32)[None, :]
    slot_lengths = jnp.sum(jnp.where(matches, lengths[None, :], 0), axis=1)
    return segments_from(slot_lengths, group_rows)


def rope_tables(position):
    halfway = HEAD_DIM // 2
    frequency = THETA ** (-(2.0 * jnp.arange(halfway, dtype=jnp.float32)) / HEAD_DIM)
    angles = position.astype(jnp.float32)[:, None] * frequency[None, :]
    cosine, sine = jnp.cos(angles), jnp.sin(angles)
    return jnp.concatenate([cosine, cosine], axis=1), jnp.concatenate([-sine, sine], axis=1)


def gather_rows(*weights):
    return lax.all_gather(jnp.concatenate(weights, axis=1), "dp", axis=0, tiled=True)


def per_device(
    streams,
    cotangent,
    lengths,
    permutation,
    query_weight,
    key_weight,
    value_weight,
    out_weight,
    gate_weight,
    up_weight,
    down_weight,
    mix_static,
    mix_weight,
    mix_scale,
):
    qkv_full = gather_rows(query_weight, key_weight, value_weight)
    out_full = gather_rows(out_weight)
    gate_up_full = gather_rows(gate_weight, up_weight)
    down_full = gather_rows(down_weight)
    local_rows, count, width = streams.shape
    uses = mix_static.shape[2]
    sizes = (count, uses)
    size = lax.axis_size("tensor")
    group_rows = local_rows * size
    mine = lax.axis_index("tensor")
    place_index = jnp.full((1,), mine, jnp.int32)
    units = gate_weight.shape[1]
    seq_count = permutation.shape[0] // lax.axis_size("dp")

    inputs = streams.reshape(local_rows, count * width)
    cotangents = cotangent.reshape(local_rows, count * width)
    tables_a = mix_tables(mix_static[0], mix_weight[0], mix_scale[0])
    tables_f = mix_tables(mix_static[1], mix_weight[1], mix_scale[1])
    segment, begins = group_layout(lengths, permutation, group_rows, seq_count)
    cosine, sine = rope_tables(jnp.arange(group_rows, dtype=jnp.int32) - begins)
    starts = jnp.broadcast_to(begins[:, None], (group_rows, LANES))
    local_segment = lax.dynamic_slice_in_dim(segment, mine * local_rows, local_rows)
    valid = jnp.broadcast_to((local_segment < seq_count).astype(jnp.float32)[:, None], (local_rows, LANES))

    normed_a, saved_a = open_attention(inputs, tables_a, *sizes)
    input_blocks = ring_gather(normed_a)
    query, key, value, attended, log_totals = attend(
        [matmul(block, qkv_full) for block in input_blocks], place_index, starts, cosine, sine
    )
    arrived_a, own_a = ring_scatter([times_transposed(block, out_full) for block in jnp.split(attended, size)])
    normed_f, d_out_f, saved_f, middle, out_a = open_feedforward(
        inputs, saved_a, arrived_a, own_a, cotangents, valid, tables_f, *sizes
    )
    feedforward_blocks = ring_gather(normed_f)
    grad_blocks = ring_gather(d_out_f)
    hidden_blocks, unit_grads = [], []
    for block, grad in zip(feedforward_blocks, grad_blocks):
        gate_up = matmul(block, gate_up_full)
        gate, up = gate_up[:, :units], gate_up[:, units:]
        hidden_blocks.append((gate / (1.0 + jnp.exp(-gate)) * up).astype(jnp.bfloat16))
        d_hidden = matmul(grad, down_full)
        sigmoid = 1.0 / (1.0 + jnp.exp(-gate))
        d_gate = (d_hidden * up * (sigmoid + gate * sigmoid * (1.0 - sigmoid))).astype(jnp.bfloat16)
        d_up = (d_hidden * gate * sigmoid).astype(jnp.bfloat16)
        unit_grads.append(jnp.concatenate([d_gate, d_up], axis=1))
    arrived_f, own_f = ring_scatter([times_transposed(hidden, down_full) for hidden in hidden_blocks])
    out_streams = finish(middle, saved_f, arrived_f, own_f, *sizes)
    arrived_n, own_n = ring_scatter([times_transposed(grads, gate_up_full) for grads in unit_grads])
    down_grad = product_sum(jnp.concatenate(grad_blocks), jnp.concatenate(hidden_blocks))
    gate_up_grad = product_sum(jnp.concatenate(feedforward_blocks), jnp.concatenate(unit_grads))

    middle_grad, d_out_a, d_branch_a, weight_sum_f, small_f = close_mix(
        True,
        [middle, saved_f, cotangents, arrived_n, own_n, arrived_f, own_f, valid, saved_a, out_a],
        tables_f,
        *sizes,
    )
    output_grads = ring_gather(d_out_a)
    attended_grads = [matmul(block, out_full).astype(jnp.bfloat16) for block in output_grads]
    d_qkv = attend_back([query, key, value, log_totals], attended_grads, place_index, starts, cosine, sine)
    arrived_i, own_i = ring_scatter([times_transposed(block, qkv_full) for block in jnp.split(d_qkv, size)])
    out_grad = product_sum(jnp.concatenate(output_grads), attended)
    qkv_grad = product_sum(jnp.concatenate(input_blocks), d_qkv)
    input_grad, weight_sum_a, small_a = close_mix(
        False, [inputs, saved_a, middle_grad, arrived_i, own_i, d_branch_a], tables_a, *sizes
    )

    def summed(weight_sum, small):
        height = width // LANES
        flat = sum_everywhere(
            jnp.concatenate([weight_sum.reshape(weight_sum.shape[0] * height, LANES)[: 2 * uses * height], small])
        )
        return mix_grads(flat[: 2 * uses * height].reshape(2 * uses, width), flat[2 * uses * height :], *sizes)

    static_f, weight_f, scale_f = summed(weight_sum_f, small_f)
    static_a, weight_a, scale_a = summed(weight_sum_a, small_a)
    query_grad, key_grad, value_grad = (
        in_order([part[:, i * query_weight.shape[1] : (i + 1) * query_weight.shape[1]] for part in qkv_grad])
        for i in range(3)
    )
    gate_grad, up_grad = (
        in_order([part[:, i * units : (i + 1) * units] for part in gate_up_grad]) for i in range(2)
    )
    shape = streams.shape
    return (
        out_streams.reshape(shape),
        input_grad.reshape(shape),
        query_grad,
        key_grad,
        value_grad,
        in_order(out_grad),
        gate_grad,
        up_grad,
        in_order(down_grad),
        jnp.stack([static_a, static_f]),
        jnp.stack([weight_a, weight_f]),
        jnp.stack([scale_a, scale_f]),
    )


def solution(mesh):
    placed = (
        P(("dp", "tensor"), None, None),
        P(("dp", "tensor"), None, None),
        P(),
        P(),
        P("dp", "tensor"),
        P("dp", "tensor"),
        P("dp", "tensor"),
        P("dp", "tensor"),
        P("dp", "tensor"),
        P("dp", "tensor"),
        P("dp", "tensor"),
        P(),
        P(),
        P(),
    )
    return jax.shard_map(
        per_device,
        mesh=mesh,
        in_specs=placed,
        out_specs=(
            P(("dp", "tensor"), None, None),
            P(("dp", "tensor"), None, None),
            P(None, "tensor"),
            P(None, "tensor"),
            P(None, "tensor"),
            P(None, "tensor"),
            P(None, "tensor"),
            P(None, "tensor"),
            P(None, "tensor"),
            P(),
            P(),
            P(),
        ),
        check_vma=False,
    )
```

```python
import functools
import jax
import jax.numpy as jnp
from jax import lax
from jax.experimental import pallas as pl
from jax.experimental.pallas import tpu as pltpu
from jax.sharding import PartitionSpec as P

HEAD_DIM = 128
EPSILON = 1e-05
THETA = 10000.0
MASKED = -1e30
LANES = 128
GROUP = 16
CHUNK = 512
PARAMS = pltpu.CompilerParams(vmem_limit_bytes=50 * 1024 * 1024)


def matmul(left, right):
    return jnp.dot(left, right, preferred_element_type=jnp.float32)


def times_transposed(left, right):
    return lax.dot_general(
        left, right, (((1,), (1,)), ((), ())), preferred_element_type=jnp.float32
    )


def transposed_times(left, right):
    return lax.dot_general(
        left, right, (((0,), (0,)), ((), ())), preferred_element_type=jnp.float32
    )


def anywhere(count):
    return [pl.BlockSpec(memory_space=pl.ANY)] * count


def cost(microseconds):
    return pl.CostEstimate(flops=int(microseconds * 1e9), bytes_accessed=0, transcendentals=0)


def lanes_of(rows):
    return lax.broadcasted_iota(jnp.int32, (rows, LANES), 1)


def column(values, lane):
    return values[:, lane : lane + 1]


def place(values, columns, first):
    lane = lanes_of(values.shape[0])
    for offset, one in enumerate(columns):
        values = jnp.where(lane == first + offset, one, values)
    return values


def fold(values):
    total = values[:, :LANES]
    for start in range(LANES, values.shape[1], LANES):
        total = total + values[:, start : start + LANES]
    return total


def row_sum(values):
    return jnp.sum(values, axis=1, keepdims=True)


def rolled(values, shift):
    shift = shift % LANES
    return values if shift == 0 else pltpu.roll(values, shift, 1)


def coefficients(projected, means, rsqrts, param_ref, sums_ref, streams, uses, parts):
    rows = projected[0].shape[0]
    lane = lanes_of(rows)
    gathered = jnp.zeros((rows, LANES), jnp.float32)
    for j in range(streams):
        total = projected[j]
        for part in range(1, parts):
            total = total + rolled(projected[j], -part * uses)
        if sums_ref is not None:
            total = total - means[j] * sums_ref[0:1, :]
        total = total * rsqrts[j]
        inside = (lane >= j * uses) & (lane < (j + 1) * uses)
        gathered = jnp.where(inside, rolled(total, j * uses), gathered)
    bent = jnp.tanh(gathered)
    return gathered, bent, param_ref[0:1, :] + param_ref[1:2, :] * bent


def pack_saved(coeffs, bent, gathered, means, rsqrts, mean_e, rsqrt_e, streams, uses):
    lane = lanes_of(coeffs.shape[0])
    count = streams * uses
    saved = jnp.where(lane < count, coeffs, 0.0)
    saved = jnp.where((lane >= count) & (lane < 2 * count), rolled(bent, count), saved)
    saved = jnp.where((lane >= 2 * count) & (lane < 3 * count), rolled(gathered, 2 * count), saved)
    return place(saved, [*means, *rsqrts, mean_e, rsqrt_e], 3 * count)


def centre_stats(total, values_of, width):
    mean = row_sum(total) * (1.0 / width)
    spread = None
    for start in range(0, width, CHUNK):
        centred = values_of(start) - mean
        square = fold(centred * centred)
        spread = square if spread is None else spread + square
    return mean, lax.rsqrt(row_sum(spread) * (1.0 / width) + EPSILON)


def entering_norm(read, coeffs, streams, uses, width, entering_ref, rows):
    total = None
    for start in range(0, width, CHUNK):
        entering = column(coeffs, 0) * read(0, start)
        for j in range(1, streams):
            entering = entering + column(coeffs, j * uses) * read(j, start)
        entering_ref[rows, start : start + CHUNK] = entering
        part = fold(entering)
        total = part if total is None else total + part
    return centre_stats(total, lambda start: entering_ref[rows, start : start + CHUNK], width)


def weight_parts(w_ref, parts_ref, sums_ref, uses, parts):
    @pl.when(pl.program_id(0) == 0)
    def _():
        rest = w_ref[...]
        sums_ref[0:1, :] = jnp.sum(rest, axis=0, keepdims=True)
        total = None
        for part in range(parts):
            one = rest.astype(jnp.bfloat16).astype(jnp.float32)
            rest = rest - one
            total = one if total is None else total + rolled(one, part * uses)
        parts_ref[...] = total.astype(jnp.bfloat16)


def open_attention_kernel(
    streams, uses, width, x_ref, w_ref, param_ref, normed_ref, saved_ref, raw_ref, entering_ref, parts_ref, sums_ref
):
    block = x_ref.shape[0]
    weight_parts(w_ref, parts_ref, sums_ref, uses, 3)
    stacked = jnp.concatenate([x_ref[:, j * width : (j + 1) * width] for j in range(streams)], axis=0)
    raw_ref[...] = jnp.dot(stacked, parts_ref[...], preferred_element_type=jnp.float32)

    def body(index, carry):
        first = pl.multiple_of(index * GROUP, GROUP)
        rows = pl.ds(first, GROUP)

        def read(j, start):
            return x_ref[rows, j * width + start : j * width + start + CHUNK].astype(jnp.float32)

        means, rsqrts, projected = [], [], []
        for j in range(streams):
            total = None
            for start in range(0, width, CHUNK):
                part = fold(read(j, start))
                total = part if total is None else total + part
            mean, rsqrt = centre_stats(total, functools.partial(read, j), width)
            means.append(mean)
            rsqrts.append(rsqrt)
            projected.append(raw_ref[pl.ds(pl.multiple_of(j * block + first, GROUP), GROUP), :])
        gathered, bent, coeffs = coefficients(projected, means, rsqrts, param_ref, sums_ref, streams, uses, 3)
        mean_e, rsqrt_e = entering_norm(read, coeffs, streams, uses, width, entering_ref, rows)
        for start in range(0, width, CHUNK):
            normed_ref[rows, start : start + CHUNK] = (
                (entering_ref[rows, start : start + CHUNK] - mean_e) * rsqrt_e
            ).astype(jnp.bfloat16)
        saved_ref[rows, :] = pack_saved(coeffs, bent, gathered, means, rsqrts, mean_e, rsqrt_e, streams, uses)
        return carry

    lax.fori_loop(0, block // GROUP, body, 0)


def open_feedforward_kernel(
    streams, uses, width,
    x_ref, saved_a_ref, arrived_ref, partial_ref, g_ref, valid_ref, w_ref, param_ref,
    normed_ref, grad_ref, saved_ref, h_ref, out_ref,
    high_ref, low_ref, raw_ref, entering_ref, stats_ref, parts_ref, sums_ref,
):
    block = x_ref.shape[0]
    weight_parts(w_ref, parts_ref, sums_ref, uses, 2)
    count = streams * uses

    def first_pass(index, carry):
        first = pl.multiple_of(index * GROUP, GROUP)
        rows = pl.ds(first, GROUP)
        coeffs = saved_a_ref[rows, :]
        totals = [None] * streams
        for start in range(0, width, CHUNK):
            out = arrived_ref[rows, start : start + CHUNK].astype(jnp.float32) + partial_ref[rows, start : start + CHUNK]
            out_ref[rows, start : start + CHUNK] = out
            values = [
                x_ref[rows, j * width + start : j * width + start + CHUNK].astype(jnp.float32)
                for j in range(streams)
            ]
            for i in range(streams):
                mixed = column(coeffs, i * uses + streams + 1) * out
                for j in range(streams):
                    mixed = mixed + column(coeffs, j * uses + 1 + i) * values[j]
                h_ref[rows, i * width + start : i * width + start + CHUNK] = mixed
                part = fold(mixed)
                totals[i] = part if totals[i] is None else totals[i] + part
        stats = jnp.zeros((GROUP, LANES), jnp.float32)
        means, rsqrts = [], []
        for i in range(streams):
            mean = row_sum(totals[i]) * (1.0 / width)
            spread = None
            for start in range(0, width, CHUNK):
                centred = h_ref[rows, i * width + start : i * width + start + CHUNK] - mean
                high = centred.astype(jnp.bfloat16)
                target = pl.ds(pl.multiple_of(i * block + first, GROUP), GROUP)
                high_ref[target, start : start + CHUNK] = high
                low_ref[target, start : start + CHUNK] = (centred - high.astype(jnp.float32)).astype(jnp.bfloat16)
                square = fold(centred * centred)
                spread = square if spread is None else spread + square
            means.append(mean)
            rsqrts.append(lax.rsqrt(row_sum(spread) * (1.0 / width) + EPSILON))
        stats_ref[rows, :] = place(stats, [*means, *rsqrts], 0)
        return carry

    lax.fori_loop(0, block // GROUP, first_pass, 0)
    raw_ref[...] = jnp.dot(high_ref[...], parts_ref[...], preferred_element_type=jnp.float32) + jnp.dot(
        low_ref[...], parts_ref[...], preferred_element_type=jnp.float32
    )

    def second_pass(index, carry):
        first = pl.multiple_of(index * GROUP, GROUP)
        rows = pl.ds(first, GROUP)
        stats = stats_ref[rows, :]
        means = [column(stats, j) for j in range(streams)]
        rsqrts = [column(stats, streams + j) for j in range(streams)]
        projected = [raw_ref[pl.ds(pl.multiple_of(j * block + first, GROUP), GROUP), :] for j in range(streams)]
        gathered, bent, coeffs = coefficients(projected, means, rsqrts, param_ref, None, streams, uses, 2)

        def read(j, start):
            return h_ref[rows, j * width + start : j * width + start + CHUNK]

        mean_e, rsqrt_e = entering_norm(read, coeffs, streams, uses, width, entering_ref, rows)
        branch = [column(coeffs, i * uses + streams + 1) * valid_ref[rows, 0:1] for i in range(streams)]
        for start in range(0, width, CHUNK):
            normed_ref[rows, start : start + CHUNK] = (
                (entering_ref[rows, start : start + CHUNK] - mean_e) * rsqrt_e
            ).astype(jnp.bfloat16)
            grad = None
            for i in range(streams):
                term = branch[i] * g_ref[rows, i * width + start : i * width + start + CHUNK].astype(jnp.float32)
                grad = term if grad is None else grad + term
            grad_ref[rows, start : start + CHUNK] = grad.astype(jnp.bfloat16)
        saved_ref[rows, :] = pack_saved(coeffs, bent, gathered, means, rsqrts, mean_e, rsqrt_e, streams, uses)
        return carry

    lax.fori_loop(0, block // GROUP, second_pass, 0)


def finish_kernel(streams, uses, width, h_ref, saved_ref, arrived_ref, partial_ref, y_ref):
    def body(index, carry):
        rows = pl.ds(pl.multiple_of(index * GROUP, GROUP), GROUP)
        coeffs = saved_ref[rows, :]
        for start in range(0, width, CHUNK):
            out = arrived_ref[rows, start : start + CHUNK].astype(jnp.float32) + partial_ref[rows, start : start + CHUNK]
            values = [h_ref[rows, j * width + start : j * width + start + CHUNK] for j in range(streams)]
            for i in range(streams):
                mixed = column(coeffs, i * uses + streams + 1) * out
                for j in range(streams):
                    mixed = mixed + column(coeffs, j * uses + 1 + i) * values[j]
                y_ref[rows, i * width + start : i * width + start + CHUNK] = mixed.astype(jnp.bfloat16)
        return carry

    lax.fori_loop(0, h_ref.shape[0] // GROUP, body, 0)


def close_kernel(streams, uses, width, inner, kept, *refs):
    inputs = 12 if inner else 8
    refs = refs[:inputs] + refs[inputs + kept :]
    if inner:
        (h_ref, saved_ref, g_ref, arrived_ref, partial_ref, arrived_f_ref, partial_f_ref, valid_ref, saved_a_ref,
         out_a_ref, wt_ref, param_ref, grad_ref, below_ref, branch_ref, weight_ref, small_ref,
         centre_ref, du_ref, left_ref, dl_ref, cols_ref, sums_ref) = refs
    else:
        (h_ref, saved_ref, g_ref, arrived_ref, partial_ref, branch_in_ref, wt_ref, param_ref,
         grad_ref, weight_ref, small_ref, centre_ref, du_ref, left_ref, dl_ref, cols_ref, sums_ref) = refs
    block = h_ref.shape[0]
    count = streams * uses
    step = pl.program_id(0)
    base = pl.multiple_of(step * block, GROUP)
    all_rows = centre_ref.shape[0] // streams

    @pl.when(step == 0)
    def _():
        sums_ref[...] = jnp.zeros_like(sums_ref)

    def read_h(rows, j, start):
        return h_ref[rows, j * width + start : j * width + start + CHUNK].astype(jnp.float32)

    def read_g(rows, i, start):
        values = g_ref[rows, i * width + start : i * width + start + CHUNK].astype(jnp.float32)
        return values * valid_ref[rows, 0:1] if inner else values

    def read_dn(rows, start):
        return arrived_ref[rows, start : start + CHUNK].astype(jnp.float32) + partial_ref[rows, start : start + CHUNK]

    def first_pass(index, carry):
        first = pl.multiple_of(index * GROUP, GROUP)
        rows = pl.ds(first, GROUP)
        saved = saved_ref[rows, :]
        means = [column(saved, 3 * count + j) for j in range(streams)]
        rsqrts = [column(saved, 3 * count + streams + j) for j in range(streams)]
        mean_e = column(saved, 3 * count + 2 * streams)
        rsqrt_e = column(saved, 3 * count + 2 * streams + 1)
        sums = {}

        def add(key, values):
            part = fold(values)
            sums[key] = part if key not in sums else sums[key] + part

        for start in range(0, width, CHUNK):
            dn = read_dn(rows, start)
            values = [read_h(rows, j, start) for j in range(streams)]
            for j in range(streams):
                target = pl.ds(pl.multiple_of(j * all_rows + base + first, GROUP), GROUP)
                centre_ref[target, start : start + CHUNK] = (values[j] - means[j]).astype(jnp.bfloat16)
            entering = column(saved, 0) * values[0]
            for j in range(1, streams):
                entering = entering + column(saved, j * uses) * values[j]
            normed = (entering - mean_e) * rsqrt_e
            add("dn", dn)
            add("dnn", dn * normed)
            for j in range(streams):
                add(("dnh", j), dn * values[j])
                add(("nh", j), normed * values[j])
            if inner:
                out = (
                    arrived_f_ref[rows, start : start + CHUNK].astype(jnp.float32)
                    + partial_f_ref[rows, start : start + CHUNK]
                )
            for i in range(streams):
                g = read_g(rows, i, start)
                for j in range(streams):
                    add(("gh", j, i), g * values[j])
                if inner:
                    add(("go", i), g * out)
        total = {key: row_sum(value) for key, value in sums.items()}
        mean_dn = total["dn"] * (1.0 / width)
        mean_dnn = total["dnn"] * (1.0 / width)
        columns = []
        for j in range(streams):
            columns.append(
                rsqrt_e * (total["dnh", j] - total["dn"] * means[j] - mean_dnn * total["nh", j])
            )
            columns.extend(total["gh", j, i] for i in range(streams))
            columns.append(total["go", j] if inner else branch_in_ref[rows, j : j + 1])
        d_coeffs = place(jnp.zeros((GROUP, LANES), jnp.float32), columns, 0)
        lane = lanes_of(GROUP)
        bent = jnp.where(lane < count, rolled(saved, -count), 0.0)
        projected = jnp.where(lane < count, rolled(saved, -2 * count), 0.0)
        sums_ref[0] += d_coeffs
        sums_ref[1] += d_coeffs * bent
        du = d_coeffs * param_ref[1:2, :] * (1.0 - bent * bent)
        with_mean = du * param_ref[3:4, :] * (1.0 / width)
        with_value = du * projected * (1.0 / width)
        shifts, slopes = [], []
        scaled = jnp.zeros((GROUP, LANES), jnp.float32)
        for j in range(streams):
            inside = (lane >= j * uses) & (lane < (j + 1) * uses)
            slope = rsqrts[j] * rsqrts[j] * row_sum(jnp.where(inside, with_value, 0.0))
            shifts.append(means[j] * slope - rsqrts[j] * row_sum(jnp.where(inside, with_mean, 0.0)))
            slopes.append(slope)
            scaled = jnp.where(inside, du * rsqrts[j], scaled)
        high = scaled.astype(jnp.bfloat16).astype(jnp.float32)
        low = (scaled - high).astype(jnp.bfloat16).astype(jnp.float32)
        spread = jnp.where(lane < count, high, 0.0)
        spread = jnp.where((lane >= count) & (lane < 2 * count), rolled(low, count), spread)
        spread = jnp.where((lane >= 2 * count) & (lane < 3 * count), rolled(high, 2 * count), spread)
        for j in range(streams):
            mine = lane < 0
            for part in range(3):
                begin = part * count + j * uses
                mine = mine | ((lane >= begin) & (lane < begin + uses))
            left_ref[pl.ds(pl.multiple_of(j * block + first, GROUP), GROUP), :] = jnp.where(
                mine, spread, 0.0
            ).astype(jnp.bfloat16)
            pair = jnp.where(lane < uses, rolled(high, -j * uses), 0.0)
            pair = jnp.where((lane >= uses) & (lane < 2 * uses), rolled(low, uses - j * uses), pair)
            du_ref[pl.ds(pl.multiple_of(j * all_rows + base + first, GROUP), GROUP), :] = pair.astype(jnp.bfloat16)
        cols_ref[rows, :] = place(
            jnp.zeros((GROUP, LANES), jnp.float32), [mean_dn, mean_dnn, *shifts, *slopes], 0
        )
        return carry

    lax.fori_loop(0, block // GROUP, first_pass, 0)
    dl_ref[...] = jnp.dot(left_ref[...], wt_ref[...], preferred_element_type=jnp.float32)

    def second_pass(index, carry):
        first = pl.multiple_of(index * GROUP, GROUP)
        rows = pl.ds(first, GROUP)
        saved = saved_ref[rows, :]
        cols = cols_ref[rows, :]
        mean_e = column(saved, 3 * count + 2 * streams)
        rsqrt_e = column(saved, 3 * count + 2 * streams + 1)
        scaled_mean = column(cols, 0) * rsqrt_e
        scaled_slope = column(cols, 1) * rsqrt_e
        branch_sums = [None] * streams
        for start in range(0, width, CHUNK):
            values = [read_h(rows, j, start) for j in range(streams)]
            entering = column(saved, 0) * values[0]
            for j in range(1, streams):
                entering = entering + column(saved, j * uses) * values[j]
            normed = (entering - mean_e) * rsqrt_e
            de = rsqrt_e * read_dn(rows, start) - scaled_mean - normed * scaled_slope
            gs = [read_g(rows, i, start) for i in range(streams)]
            below = None
            for j in range(streams):
                grad = column(saved, j * uses) * de + column(cols, 2 + j)
                grad = grad - values[j] * column(cols, 2 + streams + j)
                grad = grad + dl_ref[pl.ds(pl.multiple_of(j * block + first, GROUP), GROUP), start : start + CHUNK]
                for i in range(streams):
                    grad = grad + column(saved, j * uses + 1 + i) * gs[i]
                grad_ref[rows, j * width + start : j * width + start + CHUNK] = grad.astype(grad_ref.dtype)
                if inner:
                    part = fold(grad * out_a_ref[rows, start : start + CHUNK])
                    branch_sums[j] = part if branch_sums[j] is None else branch_sums[j] + part
                    term = saved_a_ref[rows, j * uses + streams + 1 : j * uses + streams + 2] * grad
                    below = term if below is None else below + term
            if inner:
                below_ref[rows, start : start + CHUNK] = below.astype(jnp.bfloat16)
        if inner:
            branch_ref[rows, :] = place(
                jnp.zeros((GROUP, LANES), jnp.float32), [row_sum(one) for one in branch_sums], 0
            )
        return carry

    lax.fori_loop(0, block // GROUP, second_pass, 0)

    @pl.when(step == pl.num_programs(0) - 1)
    def _():
        product = lax.dot_general(
            du_ref[...], centre_ref[...], (((0,), (0,)), ((), ())), preferred_element_type=jnp.float32
        )
        weight_ref[...] = product[: weight_ref.shape[0]]
        small_ref[0:1, :] = jnp.sum(sums_ref[0], axis=0, keepdims=True)
        small_ref[1:2, :] = jnp.sum(sums_ref[1], axis=0, keepdims=True)


def rows_block(rows):
    return min(64, rows)


def specs_for(arrays, block, whole):
    return [
        pl.BlockSpec(a.shape, lambda i: (0, 0)) if k in whole else pl.BlockSpec((block, a.shape[1]), lambda i: (i, 0))
        for k, a in enumerate(arrays)
    ]


def rounded(values):
    return lax.reduce_precision(values, 8, 7)


def mix_tables(static, weight, scale):
    streams, uses = static.shape
    high = rounded(weight)
    middle = rounded(weight - high)
    forward = jnp.pad(weight, ((0, 0), (0, LANES - uses)))
    tall = [jnp.tile(part.T, (streams, 1)) for part in (high, high, middle)]
    backward = jnp.pad(jnp.concatenate(tall, axis=0), ((0, LANES - 3 * streams * uses), (0, 0))).astype(jnp.bfloat16)
    count = streams * uses

    def row(values):
        return jnp.pad(values, (0, LANES - values.shape[0]))[None]

    constants = jnp.concatenate([row(static.reshape(count)), row(jnp.tile(scale, streams)), jnp.zeros((6, LANES), jnp.float32)])
    with_sums = jnp.concatenate([constants[:3], row(jnp.tile(jnp.sum(weight, axis=0), streams)), constants[4:]])
    return forward, backward, constants, with_sums


def open_attention(x, tables, streams, uses):
    rows, width = x.shape[0], x.shape[1] // streams
    block = rows_block(rows)
    arrays = [x, tables[0], tables[2]]
    return pl.pallas_call(
        functools.partial(open_attention_kernel, streams, uses, width),
        grid=(rows // block,),
        in_specs=specs_for(arrays, block, {1, 2}),
        out_specs=[pl.BlockSpec((block, width), lambda i: (i, 0)), pl.BlockSpec((block, LANES), lambda i: (i, 0))],
        out_shape=[jax.ShapeDtypeStruct((rows, width), jnp.bfloat16), jax.ShapeDtypeStruct((rows, LANES), jnp.float32)],
        scratch_shapes=[
            pltpu.VMEM((streams * block, LANES), jnp.float32),
            pltpu.VMEM((block, width), jnp.float32),
            pltpu.VMEM((width, LANES), jnp.bfloat16),
            pltpu.VMEM((8, LANES), jnp.float32),
        ],
        compiler_params=PARAMS,
        cost_estimate=cost(13),
        name="open_attention",
    )(*arrays)


def open_feedforward(x, saved_a, arrived, partial, g, valid, tables, streams, uses):
    rows, width = x.shape[0], x.shape[1] // streams
    block = rows_block(rows)
    arrays = [x, saved_a, arrived, partial, g, valid, tables[0], tables[2]]

    def by_rows(columns):
        return pl.BlockSpec((block, columns), lambda i: (i, 0))

    return pl.pallas_call(
        functools.partial(open_feedforward_kernel, streams, uses, width),
        grid=(rows // block,),
        in_specs=specs_for(arrays, block, {6, 7}),
        out_specs=[by_rows(width), by_rows(width), by_rows(LANES), by_rows(streams * width), by_rows(width)],
        out_shape=[
            jax.ShapeDtypeStruct((rows, width), jnp.bfloat16),
            jax.ShapeDtypeStruct((rows, width), jnp.bfloat16),
            jax.ShapeDtypeStruct((rows, LANES), jnp.float32),
            jax.ShapeDtypeStruct((rows, streams * width), jnp.float32),
            jax.ShapeDtypeStruct((rows, width), jnp.float32),
        ],
        scratch_shapes=[
            pltpu.VMEM((streams * block, width), jnp.bfloat16),
            pltpu.VMEM((streams * block, width), jnp.bfloat16),
            pltpu.VMEM((streams * block, LANES), jnp.float32),
            pltpu.VMEM((block, width), jnp.float32),
            pltpu.VMEM((block, LANES), jnp.float32),
            pltpu.VMEM((width, LANES), jnp.bfloat16),
            pltpu.VMEM((8, LANES), jnp.float32),
        ],
        compiler_params=PARAMS,
        cost_estimate=cost(21),
        name="open_feedforward",
    )(*arrays)


def finish(h, saved, arrived, partial, streams, uses):
    rows, width = h.shape[0], h.shape[1] // streams
    block = rows_block(rows)
    arrays = [h, saved, arrived, partial]
    return pl.pallas_call(
        functools.partial(finish_kernel, streams, uses, width),
        grid=(rows // block,),
        in_specs=specs_for(arrays, block, set()),
        out_specs=pl.BlockSpec((block, streams * width), lambda i: (i, 0)),
        out_shape=jax.ShapeDtypeStruct((rows, streams * width), jnp.bfloat16),
        compiler_params=PARAMS,
        cost_estimate=cost(8),
        name="finish",
    )(*arrays)


def close_mix(inner, arrays, tables, streams, uses, tokens=()):
    h = arrays[0]
    rows, width = h.shape[0], h.shape[1] // streams
    block = rows_block(rows)
    arrays = [*arrays, tables[1], tables[3]]
    last = len(arrays)

    def by_rows(columns):
        return pl.BlockSpec((block, columns), lambda i: (i, 0))

    def fixed(height, columns):
        return pl.BlockSpec((height, columns), lambda i: (0, 0))

    out_specs = [by_rows(streams * width)]
    out_shape = [jax.ShapeDtypeStruct((rows, streams * width), jnp.float32 if inner else jnp.bfloat16)]
    if inner:
        out_specs += [by_rows(width), by_rows(LANES)]
        out_shape += [
            jax.ShapeDtypeStruct((rows, width), jnp.bfloat16),
            jax.ShapeDtypeStruct((rows, LANES), jnp.float32),
        ]
    out_specs += [fixed(16, width), fixed(8, LANES)]
    out_shape += [jax.ShapeDtypeStruct((16, width), jnp.float32), jax.ShapeDtypeStruct((8, LANES), jnp.float32)]
    return pl.pallas_call(
        functools.partial(close_kernel, streams, uses, width, inner, len(tokens)),
        grid=(rows // block,),
        in_specs=specs_for(arrays, block, {last - 2, last - 1}) + anywhere(len(tokens)),
        out_specs=out_specs,
        out_shape=out_shape,
        scratch_shapes=[
            pltpu.VMEM((streams * rows, width), jnp.bfloat16),
            pltpu.VMEM((streams * rows, LANES), jnp.bfloat16),
            pltpu.VMEM((streams * block, LANES), jnp.bfloat16),
            pltpu.VMEM((streams * block, width), jnp.float32),
            pltpu.VMEM((block, LANES), jnp.float32),
            pltpu.VMEM((2, GROUP, LANES), jnp.float32),
        ],
        compiler_params=PARAMS,
        cost_estimate=cost(30 if inner else 25),
        name="close_feedforward" if inner else "close_attention",
    )(*arrays, *tokens)


def mix_grads(weight_sum, small, streams, uses):
    count = streams * uses
    return (
        small[0, :count].reshape(streams, uses),
        (weight_sum[:uses] + weight_sum[uses : 2 * uses]).T,
        jnp.sum(small[1, :count].reshape(streams, uses), axis=0),
    )


QUERY_ROWS = 256


def turn(values, cosine, sine):
    return values * cosine + pltpu.roll(values, HEAD_DIM // 2, 1) * sine


def turn_back(values, cosine, sine):
    return values * cosine - pltpu.roll(values, HEAD_DIM // 2, 1) * sine


def block_offset(mine, step, size, rows):
    return pl.multiple_of(lax.rem(mine + size - step, size) * rows, rows)


def allowed_keys(start_ref, first, rows, keys):
    row = first + lax.broadcasted_iota(jnp.int32, (rows, keys), 0)
    key = lax.broadcasted_iota(jnp.int32, (rows, keys), 1)
    return (key <= row) & (key >= start_ref[first : first + rows, 0:1])


def attend_kernel(size, *refs):
    mine_ref, start_ref, cosine_ref, sine_ref = refs[:4]
    raw = [refs[4 + 3 * s : 7 + 3 * s] for s in range(size)]
    q_ref, k_ref, v_ref, out_ref, log_ref, attended_ref = refs[4 + 3 * size :]
    mine = mine_ref[0]
    block = raw[0][0].shape[0]
    total = size * block
    for step in range(size):
        rows = pl.ds(block_offset(mine, step, size, block), block)
        cosine, sine = cosine_ref[rows, :], sine_ref[rows, :]
        q_ref[rows, :] = turn(raw[step][0][...], cosine, sine).astype(jnp.bfloat16)
        k_ref[rows, :] = turn(raw[step][1][...], cosine, sine).astype(jnp.bfloat16)
        v_ref[rows, :] = raw[step][2][...].astype(jnp.bfloat16)
    height = min(QUERY_ROWS, total)
    for first in range(0, total, height):
        keys = first + height
        scores = times_transposed(q_ref[first:keys, :], k_ref[:keys, :]) * HEAD_DIM**-0.5
        scores = jnp.where(allowed_keys(start_ref, first, height, keys), scores, MASKED)
        highest = jnp.max(scores, axis=1, keepdims=True)
        exponent = jnp.exp(scores - highest)
        row_total = jnp.sum(exponent, axis=1, keepdims=True)
        probs = (exponent * (1.0 / row_total)).astype(jnp.bfloat16)
        attended_ref[first:keys, :] = jnp.dot(
            probs, v_ref[:keys, :], preferred_element_type=jnp.float32
        ).astype(jnp.bfloat16)
        log_ref[first:keys, :] = jnp.broadcast_to(highest + jnp.log(row_total), (height, LANES))
    for step in range(size):
        rows = pl.ds(block_offset(mine, step, size, block), block)
        out_ref[step * block : (step + 1) * block, :] = attended_ref[rows, :]


def attend_back_kernel(size, kept, *refs):
    mine_ref, start_ref, cosine_ref, sine_ref, q_ref, k_ref, v_ref, log_ref = refs[:8]
    grads = refs[8 : 8 + size]
    dqkv_ref, d_out_ref, dq_ref, dk_ref, dv_ref = refs[8 + size + kept :]
    mine = mine_ref[0]
    head, heads = pl.program_id(0), pl.num_programs(0)
    block = grads[0].shape[0]
    total = size * block
    for step in range(size):
        d_out_ref[pl.ds(block_offset(mine, step, size, block), block), :] = grads[step][...]
    height = min(QUERY_ROWS, total)
    dk_ref[...] = jnp.zeros_like(dk_ref)
    dv_ref[...] = jnp.zeros_like(dv_ref)
    for first in range(0, total, height):
        keys = first + height
        q, d_out = q_ref[first:keys, :], d_out_ref[first:keys, :]
        k, v = k_ref[:keys, :], v_ref[:keys, :]
        scores = times_transposed(q, k) * HEAD_DIM**-0.5
        probs = jnp.where(
            allowed_keys(start_ref, first, height, keys), jnp.exp(scores - log_ref[first:keys, 0:1]), 0.0
        )
        d_probs = times_transposed(d_out, v)
        centre = jnp.sum(probs * d_probs, axis=1, keepdims=True)
        d_scores = (probs * (d_probs - centre)).astype(jnp.bfloat16)
        dv_ref[:keys, :] += transposed_times(probs.astype(jnp.bfloat16), d_out)
        dk_ref[:keys, :] += transposed_times(d_scores, q)
        dq_ref[first:keys, :] = jnp.dot(d_scores, k, preferred_element_type=jnp.float32)
    for step in range(size):
        rows = pl.ds(block_offset(mine, step, size, block), block)
        cosine, sine = cosine_ref[rows, :], sine_ref[rows, :]
        target = slice(step * block, (step + 1) * block)
        for part, values in enumerate(
            (
                turn_back(dq_ref[rows, :] * HEAD_DIM**-0.5, cosine, sine),
                turn_back(dk_ref[rows, :] * HEAD_DIM**-0.5, cosine, sine),
                dv_ref[rows, :],
            )
        ):
            columns = pl.ds(pl.multiple_of((part * heads + head) * HEAD_DIM, HEAD_DIM), HEAD_DIM)
            dqkv_ref[target, columns] = values.astype(jnp.bfloat16)


def whole_spec(shape):
    return pl.BlockSpec(shape, lambda h: (0,) * len(shape))


def head_spec(rows, first=0):
    return pl.BlockSpec((rows, HEAD_DIM), lambda h: (0, first + h))


def attend(raw_blocks, mine, starts, cosine, sine):
    size, block = len(raw_blocks), raw_blocks[0].shape[0]
    heads = raw_blocks[0].shape[1] // (3 * HEAD_DIM)
    total = size * block
    flat = jax.ShapeDtypeStruct((total, heads * HEAD_DIM), jnp.bfloat16)
    return pl.pallas_call(
        functools.partial(attend_kernel, size),
        grid=(heads,),
        in_specs=[pl.BlockSpec(memory_space=pltpu.SMEM)]
        + [whole_spec(a.shape) for a in (starts, cosine, sine)]
        + [head_spec(block, part * heads) for _ in range(size) for part in range(3)],
        out_specs=[head_spec(total)] * 5,
        out_shape=[flat] * 4 + [jax.ShapeDtypeStruct(flat.shape, jnp.float32)],
        scratch_shapes=[pltpu.VMEM((total, HEAD_DIM), jnp.bfloat16)],
        compiler_params=PARAMS,
        cost_estimate=cost(15),
        name="attend",
    )(mine, starts, cosine, sine, *[raw for raw in raw_blocks for _ in range(3)])


def attend_back(heads_kept, grad_blocks, mine, starts, cosine, sine, tokens):
    size, block = len(grad_blocks), grad_blocks[0].shape[0]
    total, columns = heads_kept[0].shape
    heads = columns // HEAD_DIM
    return pl.pallas_call(
        functools.partial(attend_back_kernel, size, len(tokens)),
        grid=(heads,),
        in_specs=[pl.BlockSpec(memory_space=pltpu.SMEM)]
        + [whole_spec(a.shape) for a in (starts, cosine, sine)]
        + [head_spec(total)] * 4
        + [head_spec(block)] * size
        + anywhere(len(tokens)),
        out_specs=whole_spec((total, 3 * columns)),
        out_shape=jax.ShapeDtypeStruct((total, 3 * columns), jnp.bfloat16),
        scratch_shapes=[pltpu.VMEM((total, HEAD_DIM), jnp.bfloat16)] + [pltpu.VMEM((total, HEAD_DIM), jnp.float32)] * 3,
        compiler_params=PARAMS,
        cost_estimate=cost(18),
        name="attend_back",
    )(mine, starts, cosine, sine, *heads_kept, *grad_blocks, *tokens)


UNIT_TILE = 512


def forward_units_kernel(kept, *refs):
    x_ref, gate_w_ref, up_w_ref, down_w_ref = refs[:4]
    gate_ref, up_ref, partial_ref, rows_ref, hidden_ref = refs[4 + kept : 9 + kept]
    x = x_ref[...]
    gate, up = matmul(x, gate_w_ref[...]), matmul(x, up_w_ref[...])
    gate_ref[...] = gate
    up_ref[...] = up
    hidden = (gate / (1.0 + jnp.exp(-gate)) * up).astype(jnp.bfloat16)
    hidden_ref[...] = hidden
    part = times_transposed(hidden, down_w_ref[...])

    @pl.when(pl.program_id(0) == 0)
    def _():
        partial_ref[...] = part
        rows_ref[...] = x

    @pl.when(pl.program_id(0) > 0)
    def _():
        partial_ref[...] += part


def backward_units_kernel(kept, *refs):
    d_ref, gate_ref, up_ref, down_w_ref, gate_w_ref, up_w_ref = refs[:6]
    partial_ref, rows_ref, d_gate_ref, d_up_ref = refs[6 + kept : 10 + kept]
    d_out = d_ref[...]
    d_hidden = matmul(d_out, down_w_ref[...])
    gate = gate_ref[...]
    sigmoid = 1.0 / (1.0 + jnp.exp(-gate))
    d_gate = (d_hidden * up_ref[...] * (sigmoid + gate * sigmoid * (1.0 - sigmoid))).astype(jnp.bfloat16)
    d_up = (d_hidden * gate * sigmoid).astype(jnp.bfloat16)
    d_gate_ref[...] = d_gate
    d_up_ref[...] = d_up
    part = times_transposed(d_gate, gate_w_ref[...]) + times_transposed(d_up, up_w_ref[...])

    @pl.when(pl.program_id(0) == 0)
    def _():
        partial_ref[...] = part
        rows_ref[...] = d_out

    @pl.when(pl.program_id(0) > 0)
    def _():
        partial_ref[...] += part


def forward_units(step, size, x, gate_up, down, filled, passed, tokens):
    rows, width = x.shape
    units = down.shape[1]
    tile = min(UNIT_TILE, units)
    tiles = units // tile
    weight = functools.partial(pl.BlockSpec, (width, tile))
    kept = len(filled) + len(passed) + len(tokens)
    arrays = [x, gate_up, gate_up, down]
    outs = pl.pallas_call(
        functools.partial(forward_units_kernel, kept),
        grid=(tiles,),
        in_specs=[
            pl.BlockSpec((rows, width), lambda i: (0, 0)),
            weight(lambda i: (0, i)),
            weight(lambda i: (0, tiles + i)),
            weight(lambda i: (0, i)),
        ]
        + anywhere(kept),
        out_specs=[
            pl.BlockSpec((rows, tile), lambda i: (0, i)),
            pl.BlockSpec((rows, tile), lambda i: (0, i)),
            pl.BlockSpec((rows, width), lambda i: (0, 0)),
            pl.BlockSpec((rows, width), lambda i: (step, 0)),
            pl.BlockSpec((rows, tile), lambda i: (step, i)),
        ]
        + anywhere(len(passed)),
        out_shape=[
            jax.ShapeDtypeStruct((rows, units), jnp.float32),
            jax.ShapeDtypeStruct((rows, units), jnp.float32),
            jax.ShapeDtypeStruct((rows, width), jnp.float32),
            jax.ShapeDtypeStruct((size * rows, width), jnp.bfloat16),
            jax.ShapeDtypeStruct((size * rows, units), jnp.bfloat16),
        ]
        + [jax.ShapeDtypeStruct(a.shape, a.dtype) for a in passed],
        input_output_aliases={
            **{4 + k: 3 + k for k in range(len(filled))},
            **{4 + len(filled) + k: 5 + k for k in range(len(passed))},
        },
        compiler_params=PARAMS,
        cost_estimate=cost(9),
        name="forward_units",
    )(*arrays, *filled, *passed, *tokens)
    return outs[0], outs[1], outs[2], outs[3:5], outs[5:]


def backward_units(step, size, d_out, gate, up, gate_up, down, filled, tokens):
    rows, width = d_out.shape
    units = down.shape[1]
    tile = min(UNIT_TILE, units)
    tiles = units // tile
    weight = functools.partial(pl.BlockSpec, (width, tile))
    kept = len(filled) + len(tokens)
    by_tile = pl.BlockSpec((rows, tile), lambda i: (0, i))
    outs = pl.pallas_call(
        functools.partial(backward_units_kernel, kept),
        grid=(tiles,),
        in_specs=[
            pl.BlockSpec((rows, width), lambda i: (0, 0)),
            by_tile,
            by_tile,
            weight(lambda i: (0, i)),
            weight(lambda i: (0, i)),
            weight(lambda i: (0, tiles + i)),
        ]
        + anywhere(kept),
        out_specs=[
            pl.BlockSpec((rows, width), lambda i: (0, 0)),
            pl.BlockSpec((rows, width), lambda i: (step, 0)),
            pl.BlockSpec((rows, tile), lambda i: (step, i)),
            pl.BlockSpec((rows, tile), lambda i: (step, i)),
        ],
        out_shape=[
            jax.ShapeDtypeStruct((rows, width), jnp.float32),
            jax.ShapeDtypeStruct((size * rows, width), jnp.bfloat16),
            jax.ShapeDtypeStruct((size * rows, units), jnp.bfloat16),
            jax.ShapeDtypeStruct((size * rows, units), jnp.bfloat16),
        ],
        input_output_aliases={6 + k: 1 + k for k in range(len(filled))},
        compiler_params=PARAMS,
        cost_estimate=cost(10),
        name="backward_units",
    )(d_out, gate, up, down, gate_up, gate_up, *filled, *tokens)
    return outs[0], outs[1:]


def assemble_kernel(count, pieces, table_ref, *refs):
    out_ref = refs[-1]
    for k in range(count):

        @pl.when(pl.program_id(0) // pieces == k)
        def _(k=k):
            out_ref[...] = refs[k][...].astype(jnp.float32)


def assemble(arrays, part, columns, table):
    count = len(arrays)
    pieces = table.shape[0] // count
    rows = arrays[0].shape[0] // pieces
    return pl.pallas_call(
        functools.partial(assemble_kernel, count, pieces),
        grid_spec=pltpu.PrefetchScalarGridSpec(
            num_scalar_prefetch=1,
            grid=(count * pieces,),
            in_specs=[
                pl.BlockSpec((rows, columns), lambda i, t, k=k: (jnp.clip(i - k * pieces, 0, pieces - 1), part))
                for k in range(count)
            ],
            out_specs=pl.BlockSpec((rows, columns), lambda i, t: (t[i], 0)),
        ),
        out_shape=jax.ShapeDtypeStruct((count * arrays[0].shape[0], columns), jnp.float32),
        compiler_params=PARAMS,
        cost_estimate=cost(8 * columns / 2048),
        name="assemble",
    )(table, *arrays)


def ring_shift(block):
    size = lax.axis_size("tensor")
    return lax.ppermute(block, "tensor", [(i, (i + 1) % size) for i in range(size)])


def ring_gather(block):
    blocks = [block]
    for _ in range(lax.axis_size("tensor") - 1):
        blocks.append(ring_shift(blocks[-1]))
    return blocks


def ring_scatter(partials):
    total = partials[1 % len(partials)]
    for step in range(2, len(partials) + 1):
        arrived = ring_shift(total.astype(jnp.bfloat16))
        own = partials[step % len(partials)]
        total = arrived.astype(jnp.float32) + own
    return arrived, own


def swap(values, axis, bit):
    return lax.ppermute(values, axis, [(i, i ^ (1 << bit)) for i in range(lax.axis_size(axis))])


def bit_of(axis, bit):
    return (lax.axis_index(axis) >> bit) & 1


def axis_orders():
    bits = (lax.axis_size("dp") - 1).bit_length()
    return list(range(1, bits)), list(range(bits - 1, 0, -1))


def core_products(pairs):
    half = pairs[0][0].shape[1] // 2
    core = bit_of("dp", 0)

    def products(which):
        each = [
            transposed_times(lax.dynamic_slice_in_dim(left, which * half, half, 1), right) for left, right in pairs
        ]
        return each[0] if len(each) == 1 else jnp.concatenate(each, axis=1)

    arrived = swap(products(1 - core).astype(jnp.bfloat16), "dp", 0)
    return products(core) + arrived.astype(jnp.float32)


def butterfly(part, order):
    marks = []
    for bit in order:
        rows, which = part.shape[0] // 2, bit_of("dp", bit)
        away = lax.dynamic_slice_in_dim(part, (1 - which) * rows, rows).astype(jnp.bfloat16)
        arrived = swap(away, "dp", bit)
        marks += [away, arrived]
        part = lax.dynamic_slice_in_dim(part, which * rows, rows) + arrived.astype(jnp.float32)
    part = part.astype(jnp.bfloat16)
    for bit in reversed(order):
        part = jnp.concatenate([part, swap(part, "dp", bit)])
    return part, marks


def piece_rows(orders):
    levels = len(orders[0])
    entries = []
    for flip in (0, 1):
        core = bit_of("dp", 0) ^ flip
        for k, order in enumerate(orders):
            for position in range(1 << levels):
                row = jnp.int32(0)
                for level, bit in enumerate(order):
                    digit = (position >> (levels - 1 - level)) & 1
                    row = row * 2 + (bit_of("dp", bit) ^ digit)
                entries.append((core * len(orders) + k) * (1 << levels) + row)
    return jnp.stack(entries).astype(jnp.int32)


def with_partner(parts):
    return [*parts, *(swap(part, "dp", 0) for part in parts)]


def sum_everywhere(values):
    for axis in ("dp", "tensor"):
        for bit in range((lax.axis_size(axis) - 1).bit_length()):
            values = values + swap(values, axis, bit)
    return values


def segments_from(slot_lengths, group_rows):
    bounds = jnp.cumsum(slot_lengths)
    row_ids = jnp.arange(group_rows, dtype=jnp.int32)
    segment = jnp.sum((row_ids[:, None] >= bounds[None, :]).astype(jnp.int32), axis=1)
    starting = jnp.concatenate([jnp.zeros((1,), jnp.int32), bounds])
    labels = jnp.arange(starting.shape[0], dtype=jnp.int32)
    begins = jnp.sum(jnp.where(segment[:, None] == labels[None, :], starting[None, :], 0), axis=1)
    return (segment, begins)


def group_layout(lengths, permutation, group_rows, seq_count):
    group_index = lax.axis_index("dp")
    chosen = lax.dynamic_slice_in_dim(permutation, group_index * seq_count, seq_count)
    matches = chosen[:, None] == jnp.arange(permutation.shape[0], dtype=jnp.int32)[None, :]
    slot_lengths = jnp.sum(jnp.where(matches, lengths[None, :], 0), axis=1)
    return segments_from(slot_lengths, group_rows)


def rope_tables(position):
    halfway = HEAD_DIM // 2
    frequency = THETA ** (-(2.0 * jnp.arange(halfway, dtype=jnp.float32)) / HEAD_DIM)
    angles = position.astype(jnp.float32)[:, None] * frequency[None, :]
    cosine, sine = jnp.cos(angles), jnp.sin(angles)
    return jnp.concatenate([cosine, cosine], axis=1), jnp.concatenate([-sine, sine], axis=1)


def gather_rows(*weights):
    return lax.all_gather(jnp.concatenate(weights, axis=1), "dp", axis=0, tiled=True)


def per_device(
    streams,
    cotangent,
    lengths,
    permutation,
    query_weight,
    key_weight,
    value_weight,
    out_weight,
    gate_weight,
    up_weight,
    down_weight,
    mix_static,
    mix_weight,
    mix_scale,
):
    qkv_full = gather_rows(query_weight, key_weight, value_weight)
    out_full = gather_rows(out_weight)
    gate_up_full = gather_rows(gate_weight, up_weight)
    down_full = gather_rows(down_weight)
    local_rows, count, width = streams.shape
    uses = mix_static.shape[2]
    sizes = (count, uses)
    size = lax.axis_size("tensor")
    group_rows = local_rows * size
    mine = lax.axis_index("tensor")
    place_index = jnp.full((1,), mine, jnp.int32)
    units = gate_weight.shape[1]
    seq_count = permutation.shape[0] // lax.axis_size("dp")

    inputs = streams.reshape(local_rows, count * width)
    cotangents = cotangent.reshape(local_rows, count * width)
    tables_a = mix_tables(mix_static[0], mix_weight[0], mix_scale[0])
    tables_f = mix_tables(mix_static[1], mix_weight[1], mix_scale[1])
    segment, begins = group_layout(lengths, permutation, group_rows, seq_count)
    cosine, sine = rope_tables(jnp.arange(group_rows, dtype=jnp.int32) - begins)
    starts = jnp.broadcast_to(begins[:, None], (group_rows, LANES))
    local_segment = lax.dynamic_slice_in_dim(segment, mine * local_rows, local_rows)
    valid = jnp.broadcast_to((local_segment < seq_count).astype(jnp.float32)[:, None], (local_rows, LANES))

    normed_a, saved_a = open_attention(inputs, tables_a, *sizes)
    input_blocks = ring_gather(normed_a)
    query, key, value, attended, log_totals = attend(
        [matmul(block, qkv_full) for block in input_blocks], place_index, starts, cosine, sine
    )
    arrived_a, own_a = ring_scatter([times_transposed(block, out_full) for block in jnp.split(attended, size)])
    normed_f, d_out_f, saved_f, middle, out_a = open_feedforward(
        inputs, saved_a, arrived_a, own_a, cotangents, valid, tables_f, *sizes
    )
    feedforward_blocks = ring_gather(normed_f)
    gates, ups, partials_f, filled = [], [], [], []
    for step, block in enumerate(feedforward_blocks):
        last = step == size - 1
        passed = [d_out_f] if step == size - 2 else [partials_f[1].astype(jnp.bfloat16)] if last and step > 1 else []
        gate, up, partial, filled, passed = forward_units(step, size, block, gate_up_full, down_full, filled, passed, [])
        gates.append(gate)
        ups.append(up)
        partials_f.append(partial)
        if step == size - 2:
            (d_out_f,) = passed
        elif last and step > 1:
            partials_f[1] = passed[0]
    feedforward_rows, hidden_rows = filled
    partials_n, filled = [], []
    for step, grad in enumerate(ring_gather(d_out_f)):
        partial, filled = backward_units(step, size, grad, gates[step], ups[step], gate_up_full, down_full, filled, [])
        partials_n.append(partial)
    grad_rows, d_gate_rows, d_up_rows = filled
    arrived_f, own_f = ring_scatter(partials_f)
    out_streams = finish(middle, saved_f, arrived_f, own_f, *sizes)
    arrived_n, own_n = ring_scatter(partials_n)

    orders = axis_orders()
    whole_table, half_tables = piece_rows(orders), [piece_rows([order]) for order in orders]
    down_parts = [
        butterfly(part, order) for part, order in zip(jnp.split(core_products([(grad_rows, hidden_rows)]), 2), orders)
    ]
    gate_up_parts = [
        butterfly(core_products([(feedforward_rows, grads)]), order)
        for grads, order in zip((d_gate_rows, d_up_rows), orders)
    ]
    middle_grad, d_out_a, d_branch_a, weight_sum_f, small_f = close_mix(
        True,
        [middle, saved_f, cotangents, arrived_n, own_n, arrived_f, own_f, valid, saved_a, out_a],
        tables_f,
        *sizes,
        tokens=[marks[0] for _, marks in gate_up_parts],
    )
    down_grad = assemble(with_partner([part for part, _ in down_parts]), 0, units, whole_table)
    gate_grad, up_grad = (
        assemble(with_partner([part]), 0, units, table) for (part, _), table in zip(gate_up_parts, half_tables)
    )
    output_grads = ring_gather(d_out_a)
    attended_grads = [matmul(block, out_full).astype(jnp.bfloat16) for block in output_grads]
    d_qkv = attend_back(
        [query, key, value, log_totals],
        attended_grads,
        place_index,
        starts,
        cosine,
        sine,
        [marks[-1] for _, marks in [*gate_up_parts, *down_parts]],
    )
    arrived_i, own_i = ring_scatter([times_transposed(block, qkv_full) for block in jnp.split(d_qkv, size)])
    attention_parts = [
        butterfly(part, order)
        for part, order in zip(
            jnp.split(
                core_products([(jnp.concatenate(output_grads), attended), (jnp.concatenate(input_blocks), d_qkv)]), 2
            ),
            orders,
        )
    ]
    input_grad, weight_sum_a, small_a = close_mix(
        False,
        [inputs, saved_a, middle_grad, arrived_i, own_i, d_branch_a],
        tables_a,
        *sizes,
        tokens=[marks[1] for _, marks in attention_parts] + [down_grad, gate_grad, up_grad],
    )
    attention_halves = with_partner([part for part, _ in attention_parts])
    out_grad, query_grad, key_grad, value_grad = (
        assemble(attention_halves, part, out_weight.shape[1], whole_table) for part in range(4)
    )
    height = width // LANES
    taken = 2 * uses * height

    def flat(weight_sum, small):
        return jnp.concatenate([weight_sum.reshape(weight_sum.shape[0] * height, LANES)[:taken], small])

    sums = sum_everywhere(jnp.concatenate([flat(weight_sum_a, small_a), flat(weight_sum_f, small_f)]))
    (static_a, weight_a, scale_a), (static_f, weight_f, scale_f) = (
        mix_grads(part[:taken].reshape(2 * uses, width), part[taken:], *sizes) for part in jnp.split(sums, 2)
    )
    shape = streams.shape
    return (
        out_streams.reshape(shape),
        input_grad.reshape(shape),
        query_grad,
        key_grad,
        value_grad,
        out_grad,
        gate_grad,
        up_grad,
        down_grad,
        jnp.stack([static_a, static_f]),
        jnp.stack([weight_a, weight_f]),
        jnp.stack([scale_a, scale_f]),
    )


def solution(mesh):
    placed = (
        P(("dp", "tensor"), None, None),
        P(("dp", "tensor"), None, None),
        P(),
        P(),
        P("dp", "tensor"),
        P("dp", "tensor"),
        P("dp", "tensor"),
        P("dp", "tensor"),
        P("dp", "tensor"),
        P("dp", "tensor"),
        P("dp", "tensor"),
        P(),
        P(),
        P(),
    )
    return jax.shard_map(
        per_device,
        mesh=mesh,
        in_specs=placed,
        out_specs=(
            P(("dp", "tensor"), None, None),
            P(("dp", "tensor"), None, None),
            P(None, "tensor"),
            P(None, "tensor"),
            P(None, "tensor"),
            P(None, "tensor"),
            P(None, "tensor"),
            P(None, "tensor"),
            P(None, "tensor"),
            P(),
            P(),
            P(),
        ),
        check_vma=False,
    )
```

```python
import functools
import math
import jax
import jax.numpy as jnp
from jax import lax
from jax.experimental import pallas as pl
from jax.experimental.pallas import tpu as pltpu
from jax.sharding import PartitionSpec as P

HEAD_DIM = 128
EPSILON = 1e-05
THETA = 10000.0
MASKED = -1e30
LANES = 128
GROUP = 16
CHUNK = 512
PARAMS = pltpu.CompilerParams(vmem_limit_bytes=50 * 1024 * 1024)


def matmul(left, right):
    return jnp.dot(left, right, preferred_element_type=jnp.float32)


def times_transposed(left, right):
    return lax.dot_general(
        left, right, (((1,), (1,)), ((), ())), preferred_element_type=jnp.float32
    )


def transposed_times(left, right):
    return lax.dot_general(
        left, right, (((0,), (0,)), ((), ())), preferred_element_type=jnp.float32
    )


MARKS = {}


def marked(results, mark):
    for one in results:
        MARKS[id(one)] = (one, mark)
    return results


def waits(tokens):
    each = {id(t): t for t in (MARKS[id(one)][1] if id(one) in MARKS else one for one in tokens)}
    return list(each.values())


MARK_SPEC = pl.BlockSpec((8, LANES), lambda *index: (0, 0))
MARK_SHAPE = jax.ShapeDtypeStruct((8, LANES), jnp.float32)


def anywhere(count):
    return [pl.BlockSpec(memory_space=pl.ANY)] * count


def cost(microseconds=0):
    return pl.CostEstimate(flops=int(microseconds * 1e9), bytes_accessed=0, transcendentals=0)


def hold(values, *tokens):
    tokens = waits(tokens)

    def nothing(*refs):
        pass

    return pl.pallas_call(
        nothing,
        in_specs=anywhere(len(values) + len(tokens)),
        out_specs=anywhere(len(values)),
        out_shape=[jax.ShapeDtypeStruct(a.shape, a.dtype) for a in values],
        input_output_aliases={k: k for k in range(len(values))},
        name="hold",
    )(*values, *tokens)


def lanes_of(rows):
    return lax.broadcasted_iota(jnp.int32, (rows, LANES), 1)


def column(values, lane):
    return values[:, lane : lane + 1]


def place(values, columns, first):
    lane = lanes_of(values.shape[0])
    for offset, one in enumerate(columns):
        values = jnp.where(lane == first + offset, one, values)
    return values


def fold(values):
    total = values[:, :LANES]
    for start in range(LANES, values.shape[1], LANES):
        total = total + values[:, start : start + LANES]
    return total


def row_sum(values):
    return jnp.sum(values, axis=1, keepdims=True)


def rolled(values, shift):
    shift = shift % LANES
    return values if shift == 0 else pltpu.roll(values, shift, 1)


def coefficients(projected, means, rsqrts, param_ref, sums_ref, streams, uses, parts, centred):
    rows = projected[0].shape[0]
    lane = lanes_of(rows)
    gathered = jnp.zeros((rows, LANES), jnp.float32)
    sums = jnp.zeros((rows, LANES), jnp.float32)
    for j in range(streams):
        total = joined(projected[j], parts)
        if not centred:
            total = total - means[j] * sums_ref[0:1, :]
        total = total * rsqrts[j]
        inside = (lane >= j * uses) & (lane < (j + 1) * uses)
        gathered = jnp.where(inside, rolled(total, j * uses), gathered)
        sums = jnp.where(inside, rolled(jnp.broadcast_to(sums_ref[0:1, :], (rows, LANES)), j * uses), sums)
    bent = jnp.tanh(gathered)
    return gathered, bent, param_ref[0:1, :] + param_ref[1:2, :] * bent, sums


def pack_saved(coeffs, bent, gathered, sums, means, rsqrts, mean_e, rsqrt_e, streams, uses):
    lane = lanes_of(coeffs.shape[0])
    count = streams * uses
    saved = jnp.where(lane < count, coeffs, 0.0)
    saved = jnp.where((lane >= count) & (lane < 2 * count), rolled(bent, count), saved)
    saved = jnp.where((lane >= 2 * count) & (lane < 3 * count), rolled(gathered, 2 * count), saved)
    first = 3 * count + 2 * streams + 2
    saved = jnp.where((lane >= first) & (lane < first + count), rolled(sums, first), saved)
    return place(saved, [*means, *rsqrts, mean_e, rsqrt_e], 3 * count)


def centre_stats(total, values_of, width):
    mean = row_sum(total) * (1.0 / width)
    spread = None
    for start in range(0, width, CHUNK):
        centred = values_of(start) - mean
        square = fold(centred * centred)
        spread = square if spread is None else spread + square
    return mean, lax.rsqrt(row_sum(spread) * (1.0 / width) + EPSILON)


def entering_norm(read, coeffs, streams, uses, width, entering_ref, rows):
    total = None
    for start in range(0, width, CHUNK):
        entering = column(coeffs, 0) * read(0, start)
        for j in range(1, streams):
            entering = entering + column(coeffs, j * uses) * read(j, start)
        entering_ref[rows, start : start + CHUNK] = entering
        part = fold(entering)
        total = part if total is None else total + part
    return centre_stats(total, lambda start: entering_ref[rows, start : start + CHUNK], width)


def weight_parts(w_ref, parts_ref, sums_ref, parts):
    @pl.when(pl.program_id(0) == 0)
    def _():
        rest = w_ref[...]
        rows, width = rest.shape
        each = []
        for _ in range(parts):
            each.append(rest.astype(jnp.bfloat16).astype(jnp.float32))
            rest = rest - each[-1]
        each.append(jnp.zeros((LANES - parts * rows, width), jnp.float32))
        parts_ref[...] = jnp.concatenate(each, axis=0).astype(jnp.bfloat16)
        sums = times_transposed(jnp.ones((8, width), jnp.bfloat16), parts_ref[...])
        sums_ref[...] = joined(sums, parts)


def joined(values, parts):
    total = values
    for part in range(1, parts):
        total = total + rolled(values, -8 * part)
    return total


def open_attention_kernel(
    streams, uses, width, x_ref, w_ref, param_ref, normed_ref, saved_ref, raw_ref, entering_ref, parts_ref, sums_ref
):
    block = x_ref.shape[0]
    weight_parts(w_ref, parts_ref, sums_ref, 3)
    stacked = jnp.concatenate([x_ref[:, j * width : (j + 1) * width] for j in range(streams)], axis=0)
    raw_ref[...] = times_transposed(stacked, parts_ref[...])

    def body(index, carry):
        first = pl.multiple_of(index * GROUP, GROUP)
        rows = pl.ds(first, GROUP)

        def read(j, start):
            return x_ref[rows, j * width + start : j * width + start + CHUNK].astype(jnp.float32)

        means, rsqrts, projected = [], [], []
        for j in range(streams):
            total = None
            for start in range(0, width, CHUNK):
                part = fold(read(j, start))
                total = part if total is None else total + part
            mean, rsqrt = centre_stats(total, functools.partial(read, j), width)
            means.append(mean)
            rsqrts.append(rsqrt)
            projected.append(raw_ref[pl.ds(pl.multiple_of(j * block + first, GROUP), GROUP), :])
        gathered, bent, coeffs, sums = coefficients(
            projected, means, rsqrts, param_ref, sums_ref, streams, uses, 3, False
        )
        mean_e, rsqrt_e = entering_norm(read, coeffs, streams, uses, width, entering_ref, rows)
        for start in range(0, width, CHUNK):
            normed_ref[rows, start : start + CHUNK] = (
                (entering_ref[rows, start : start + CHUNK] - mean_e) * rsqrt_e
            ).astype(jnp.bfloat16)
        saved_ref[rows, :] = pack_saved(
            coeffs, bent, gathered, sums, means, rsqrts, mean_e, rsqrt_e, streams, uses
        )
        return carry

    lax.fori_loop(0, block // GROUP, body, 0)


def open_feedforward_kernel(streams, uses, width, *refs):
    x_ref, saved_a_ref, out_ref, g_ref, valid_ref, w_ref, param_ref = refs[:7]
    normed_ref, grad_ref, saved_ref, h_ref = refs[7:11]
    high_ref, low_ref, raw_ref, entering_ref, stats_ref, parts_ref, sums_ref = refs[11:]
    block = x_ref.shape[0]
    weight_parts(w_ref, parts_ref, sums_ref, 2)
    count = streams * uses

    def first_pass(index, carry):
        first = pl.multiple_of(index * GROUP, GROUP)
        rows = pl.ds(first, GROUP)
        coeffs = saved_a_ref[rows, :]
        totals = [None] * streams
        for start in range(0, width, CHUNK):
            out = out_ref[rows, start : start + CHUNK]
            values = [
                x_ref[rows, j * width + start : j * width + start + CHUNK].astype(jnp.float32)
                for j in range(streams)
            ]
            for i in range(streams):
                mixed = column(coeffs, i * uses + streams + 1) * out
                for j in range(streams):
                    mixed = mixed + column(coeffs, j * uses + 1 + i) * values[j]
                h_ref[rows, i * width + start : i * width + start + CHUNK] = mixed
                part = fold(mixed)
                totals[i] = part if totals[i] is None else totals[i] + part
        stats = jnp.zeros((GROUP, LANES), jnp.float32)
        means, rsqrts = [], []
        for i in range(streams):
            mean = row_sum(totals[i]) * (1.0 / width)
            spread = None
            for start in range(0, width, CHUNK):
                centred = h_ref[rows, i * width + start : i * width + start + CHUNK] - mean
                high = centred.astype(jnp.bfloat16)
                target = pl.ds(pl.multiple_of(i * block + first, GROUP), GROUP)
                high_ref[target, start : start + CHUNK] = high
                low_ref[target, start : start + CHUNK] = (centred - high.astype(jnp.float32)).astype(jnp.bfloat16)
                square = fold(centred * centred)
                spread = square if spread is None else spread + square
            means.append(mean)
            rsqrts.append(lax.rsqrt(row_sum(spread) * (1.0 / width) + EPSILON))
        stats_ref[rows, :] = place(stats, [*means, *rsqrts], 0)
        return carry

    lax.fori_loop(0, block // GROUP, first_pass, 0)
    raw_ref[...] = times_transposed(high_ref[...], parts_ref[...]) + times_transposed(
        low_ref[...], parts_ref[...]
    )

    def second_pass(index, carry):
        first = pl.multiple_of(index * GROUP, GROUP)
        rows = pl.ds(first, GROUP)
        stats = stats_ref[rows, :]
        means = [column(stats, j) for j in range(streams)]
        rsqrts = [column(stats, streams + j) for j in range(streams)]
        projected = [raw_ref[pl.ds(pl.multiple_of(j * block + first, GROUP), GROUP), :] for j in range(streams)]
        gathered, bent, coeffs, sums = coefficients(
            projected, means, rsqrts, param_ref, sums_ref, streams, uses, 2, True
        )

        def read(j, start):
            return h_ref[rows, j * width + start : j * width + start + CHUNK]

        mean_e, rsqrt_e = entering_norm(read, coeffs, streams, uses, width, entering_ref, rows)
        branch = [column(coeffs, i * uses + streams + 1) * valid_ref[rows, 0:1] for i in range(streams)]
        for start in range(0, width, CHUNK):
            normed_ref[rows, start : start + CHUNK] = (
                (entering_ref[rows, start : start + CHUNK] - mean_e) * rsqrt_e
            ).astype(jnp.bfloat16)
            grad = None
            for i in range(streams):
                term = branch[i] * g_ref[rows, i * width + start : i * width + start + CHUNK].astype(jnp.float32)
                grad = term if grad is None else grad + term
            grad_ref[rows, start : start + CHUNK] = grad.astype(jnp.bfloat16)
        saved_ref[rows, :] = pack_saved(
            coeffs, bent, gathered, sums, means, rsqrts, mean_e, rsqrt_e, streams, uses
        )
        return carry

    lax.fori_loop(0, block // GROUP, second_pass, 0)


def finish_kernel(streams, uses, width, h_ref, saved_ref, arrived_ref, partial_ref, *refs):
    y_ref, mark_ref = refs[-2:]
    mark_ref[...] = jnp.zeros_like(mark_ref)

    def body(index, carry):
        rows = pl.ds(pl.multiple_of(index * GROUP, GROUP), GROUP)
        coeffs = saved_ref[rows, :]
        for start in range(0, width, CHUNK):
            out = arrived_ref[rows, start : start + CHUNK].astype(jnp.float32) + partial_ref[rows, start : start + CHUNK]
            values = [h_ref[rows, j * width + start : j * width + start + CHUNK] for j in range(streams)]
            for i in range(streams):
                mixed = column(coeffs, i * uses + streams + 1) * out
                for j in range(streams):
                    mixed = mixed + column(coeffs, j * uses + 1 + i) * values[j]
                y_ref[rows, i, start : start + CHUNK] = mixed.astype(jnp.bfloat16)
        return carry

    lax.fori_loop(0, h_ref.shape[0] // GROUP, body, 0)


def close_kernel(streams, uses, width, inner, kept, *refs):
    inputs = 12 if inner else 8
    refs = refs[:inputs] + refs[inputs + kept :]
    if inner:
        (h_ref, saved_ref, g_ref, arrived_ref, partial_ref, arrived_f_ref, partial_f_ref, valid_ref, saved_a_ref,
         out_a_ref, wt_ref, param_ref, grad_ref, branch_ref, below_ref, weight_ref, small_ref,
         centre_ref, du_ref, left_ref, dl_ref, cols_ref, sums_ref, parts_ref) = refs
    else:
        (h_ref, saved_ref, g_ref, arrived_ref, partial_ref, branch_in_ref, wt_ref, param_ref,
         grad_ref, weight_ref, small_ref, centre_ref, du_ref, left_ref, dl_ref, cols_ref, sums_ref, parts_ref) = refs
    block = h_ref.shape[0]
    count = streams * uses
    step = pl.program_id(0)
    base = pl.multiple_of(step * block, GROUP)
    all_rows = centre_ref.shape[0] // streams

    @pl.when(step == 0)
    def _():
        sums_ref[...] = jnp.zeros_like(sums_ref)
        weights = wt_ref[...]
        high = weights.astype(jnp.bfloat16).astype(jnp.float32)
        rest = jnp.zeros((LANES - 3 * weights.shape[0], width), jnp.float32)
        parts_ref[...] = jnp.concatenate([high, high, weights - high, rest], axis=0).astype(jnp.bfloat16)

    def read_h(rows, j, start):
        return h_ref[rows, j * width + start : j * width + start + CHUNK].astype(jnp.float32)

    def read_g(rows, i, start):
        values = g_ref[rows, i * width + start : i * width + start + CHUNK].astype(jnp.float32)
        return values * valid_ref[rows, 0:1] if inner else values

    def read_dn(rows, start):
        return arrived_ref[rows, start : start + CHUNK].astype(jnp.float32) + partial_ref[rows, start : start + CHUNK]

    def first_pass(index, carry):
        first = pl.multiple_of(index * GROUP, GROUP)
        rows = pl.ds(first, GROUP)
        saved = saved_ref[rows, :]
        means = [column(saved, 3 * count + j) for j in range(streams)]
        rsqrts = [column(saved, 3 * count + streams + j) for j in range(streams)]
        mean_e = column(saved, 3 * count + 2 * streams)
        rsqrt_e = column(saved, 3 * count + 2 * streams + 1)
        sums = {}

        def add(key, values):
            part = fold(values)
            sums[key] = part if key not in sums else sums[key] + part

        for start in range(0, width, CHUNK):
            dn = read_dn(rows, start)
            values = [read_h(rows, j, start) for j in range(streams)]
            for j in range(streams):
                target = pl.ds(pl.multiple_of(j * all_rows + base + first, GROUP), GROUP)
                centre_ref[target, start : start + CHUNK] = (values[j] - means[j]).astype(jnp.bfloat16)
            entering = column(saved, 0) * values[0]
            for j in range(1, streams):
                entering = entering + column(saved, j * uses) * values[j]
            normed = (entering - mean_e) * rsqrt_e
            add("dn", dn)
            add("dnn", dn * normed)
            for j in range(streams):
                add(("dnh", j), dn * values[j])
                add(("nh", j), normed * values[j])
            if inner:
                out = (
                    arrived_f_ref[rows, start : start + CHUNK].astype(jnp.float32)
                    + partial_f_ref[rows, start : start + CHUNK]
                )
            for i in range(streams):
                g = read_g(rows, i, start)
                for j in range(streams):
                    add(("gh", j, i), g * values[j])
                if inner:
                    add(("go", i), g * out)
        total = {key: row_sum(value) for key, value in sums.items()}
        mean_dn = total["dn"] * (1.0 / width)
        mean_dnn = total["dnn"] * (1.0 / width)
        columns = []
        for j in range(streams):
            columns.append(
                rsqrt_e * (total["dnh", j] - total["dn"] * means[j] - mean_dnn * total["nh", j])
            )
            columns.extend(total["gh", j, i] for i in range(streams))
            columns.append(total["go", j] if inner else branch_in_ref[rows, j : j + 1])
        d_coeffs = place(jnp.zeros((GROUP, LANES), jnp.float32), columns, 0)
        lane = lanes_of(GROUP)
        bent = jnp.where(lane < count, rolled(saved, -count), 0.0)
        projected = jnp.where(lane < count, rolled(saved, -2 * count), 0.0)
        sums_ref[0] += d_coeffs
        sums_ref[1] += d_coeffs * bent
        du = d_coeffs * param_ref[1:2, :] * (1.0 - bent * bent)
        with_mean = du * jnp.where(lane < count, rolled(saved, -(3 * count + 2 * streams + 2)), 0.0) * (1.0 / width)
        with_value = du * projected * (1.0 / width)
        shifts, slopes = [], []
        scaled = jnp.zeros((GROUP, LANES), jnp.float32)
        for j in range(streams):
            inside = (lane >= j * uses) & (lane < (j + 1) * uses)
            slope = rsqrts[j] * rsqrts[j] * row_sum(jnp.where(inside, with_value, 0.0))
            shifts.append(means[j] * slope - rsqrts[j] * row_sum(jnp.where(inside, with_mean, 0.0)))
            slopes.append(slope)
            scaled = jnp.where(inside, du * rsqrts[j], scaled)
        high = scaled.astype(jnp.bfloat16).astype(jnp.float32)
        low = (scaled - high).astype(jnp.bfloat16).astype(jnp.float32)
        for j in range(streams):
            own_high, own_low = rolled(high, -j * uses), rolled(low, -j * uses)
            left = jnp.where(lane < uses, own_high, 0.0)
            left = jnp.where((lane >= 8) & (lane < 8 + uses), rolled(own_low, 8), left)
            left = jnp.where((lane >= 16) & (lane < 16 + uses), rolled(own_high, 16), left)
            left_ref[pl.ds(pl.multiple_of(j * block + first, GROUP), GROUP), :] = left.astype(jnp.bfloat16)
            pair = jnp.where(lane < 8 + uses, left, 0.0)
            du_ref[pl.ds(pl.multiple_of(j * all_rows + base + first, GROUP), GROUP), :] = pair.astype(jnp.bfloat16)
        cols_ref[rows, :] = place(
            jnp.zeros((GROUP, LANES), jnp.float32), [mean_dn, mean_dnn, *shifts, *slopes], 0
        )
        return carry

    lax.fori_loop(0, block // GROUP, first_pass, 0)
    dl_ref[...] = jnp.dot(left_ref[...], parts_ref[...], preferred_element_type=jnp.float32)

    def second_pass(index, carry):
        first = pl.multiple_of(index * GROUP, GROUP)
        rows = pl.ds(first, GROUP)
        saved = saved_ref[rows, :]
        cols = cols_ref[rows, :]
        mean_e = column(saved, 3 * count + 2 * streams)
        rsqrt_e = column(saved, 3 * count + 2 * streams + 1)
        scaled_mean = column(cols, 0) * rsqrt_e
        scaled_slope = column(cols, 1) * rsqrt_e
        branch_sums = [None] * streams
        for start in range(0, width, CHUNK):
            values = [read_h(rows, j, start) for j in range(streams)]
            entering = column(saved, 0) * values[0]
            for j in range(1, streams):
                entering = entering + column(saved, j * uses) * values[j]
            normed = (entering - mean_e) * rsqrt_e
            de = rsqrt_e * read_dn(rows, start) - scaled_mean - normed * scaled_slope
            gs = [read_g(rows, i, start) for i in range(streams)]
            below = None
            for j in range(streams):
                grad = column(saved, j * uses) * de + column(cols, 2 + j)
                grad = grad - values[j] * column(cols, 2 + streams + j)
                grad = grad + dl_ref[pl.ds(pl.multiple_of(j * block + first, GROUP), GROUP), start : start + CHUNK]
                for i in range(streams):
                    grad = grad + column(saved, j * uses + 1 + i) * gs[i]
                if inner:
                    grad_ref[rows, j * width + start : j * width + start + CHUNK] = grad
                else:
                    grad_ref[rows, j, start : start + CHUNK] = grad.astype(jnp.bfloat16)
                if inner:
                    part = fold(grad * out_a_ref[rows, start : start + CHUNK])
                    branch_sums[j] = part if branch_sums[j] is None else branch_sums[j] + part
                    term = saved_a_ref[rows, j * uses + streams + 1 : j * uses + streams + 2] * grad
                    below = term if below is None else below + term
            if inner:
                below_ref[rows, start : start + CHUNK] = below.astype(jnp.bfloat16)
        if inner:
            branch_ref[rows, :] = place(
                jnp.zeros((GROUP, LANES), jnp.float32), [row_sum(one) for one in branch_sums], 0
            )
        return carry

    lax.fori_loop(0, block // GROUP, second_pass, 0)

    @pl.when(step == pl.num_programs(0) - 1)
    def _():
        product = lax.dot_general(
            du_ref[...], centre_ref[...], (((0,), (0,)), ((), ())), preferred_element_type=jnp.float32
        )
        weight_ref[...] = product[: weight_ref.shape[0]]
        small_ref[0:1, :] = jnp.sum(sums_ref[0], axis=0, keepdims=True)
        small_ref[1:2, :] = jnp.sum(sums_ref[1], axis=0, keepdims=True)


def rows_block(rows):
    return min(64, rows)


def specs_for(arrays, block, whole):
    specs = []
    for k, entry in enumerate(arrays):
        array, first = entry if isinstance(entry, tuple) else (entry, 0)
        if k in whole:
            specs.append(pl.BlockSpec(array.shape, lambda i: (0, 0)))
        else:
            specs.append(pl.BlockSpec((block, array.shape[1]), lambda i, first=first // block: (first + i, 0)))
    return specs


def plain(arrays):
    return [entry[0] if isinstance(entry, tuple) else entry for entry in arrays]


def mix_tables(static, weight, scale):
    streams, uses = static.shape
    count = streams * uses
    constants = jnp.stack([static.reshape(count), jnp.tile(scale, streams)])
    return jnp.pad(weight.T, ((0, 8 - uses), (0, 0))), jnp.pad(constants, ((0, 6), (0, LANES - count)))


def open_attention(x, tables, streams, uses):
    rows, width = x.shape[0], x.shape[1] // streams
    block = rows_block(rows)
    arrays = [x, *tables]
    return pl.pallas_call(
        functools.partial(open_attention_kernel, streams, uses, width),
        grid=(rows // block,),
        in_specs=specs_for(arrays, block, {1, 2}),
        out_specs=[pl.BlockSpec((block, width), lambda i: (i, 0)), pl.BlockSpec((block, LANES), lambda i: (i, 0))],
        out_shape=[jax.ShapeDtypeStruct((rows, width), jnp.bfloat16), jax.ShapeDtypeStruct((rows, LANES), jnp.float32)],
        scratch_shapes=[
            pltpu.VMEM((streams * block, LANES), jnp.float32),
            pltpu.VMEM((block, width), jnp.float32),
            pltpu.VMEM((LANES, width), jnp.bfloat16),
            pltpu.VMEM((8, LANES), jnp.float32),
        ],
        compiler_params=PARAMS,
        cost_estimate=cost(),
        name="open_attention",
    )(*plain(arrays))


def open_feedforward(x, saved_a, out_a, g, valid, tables, streams, uses):
    rows, width = x.shape[0], x.shape[1] // streams
    block = rows_block(rows)
    arrays = [x, saved_a, out_a, g, valid, *tables]

    def by_rows(columns):
        return pl.BlockSpec((block, columns), lambda i: (i, 0))

    return pl.pallas_call(
        functools.partial(open_feedforward_kernel, streams, uses, width),
        grid=(rows // block,),
        in_specs=specs_for(arrays, block, {5, 6}),
        out_specs=[by_rows(width), by_rows(width), by_rows(LANES), by_rows(streams * width)],
        out_shape=[
            jax.ShapeDtypeStruct((rows, width), jnp.bfloat16),
            jax.ShapeDtypeStruct((rows, width), jnp.bfloat16),
            jax.ShapeDtypeStruct((rows, LANES), jnp.float32),
            jax.ShapeDtypeStruct((rows, streams * width), jnp.float32),
        ],
        scratch_shapes=[
            pltpu.VMEM((streams * block, width), jnp.bfloat16),
            pltpu.VMEM((streams * block, width), jnp.bfloat16),
            pltpu.VMEM((streams * block, LANES), jnp.float32),
            pltpu.VMEM((block, width), jnp.float32),
            pltpu.VMEM((block, LANES), jnp.float32),
            pltpu.VMEM((LANES, width), jnp.bfloat16),
            pltpu.VMEM((8, LANES), jnp.float32),
        ],
        compiler_params=PARAMS,
        cost_estimate=cost(),
        name="open_feedforward",
    )(*plain(arrays))


def finish(first, h, saved, arrived, partial, streams, uses, filled, tokens=()):
    tokens = waits(tokens)
    rows, width = h.shape[0], h.shape[1] // streams
    block = rows_block(arrived[2])
    arrays = [(h, first), (saved, first), arrived[:2], (partial, first)]
    result, mark = pl.pallas_call(
        functools.partial(finish_kernel, streams, uses, width),
        grid=(arrived[2] // block,),
        in_specs=specs_for(arrays, block, set()) + anywhere(len(filled) + len(tokens)),
        out_specs=[pl.BlockSpec((block, streams, width), lambda i: (first // block + i, 0, 0)), MARK_SPEC],
        out_shape=[jax.ShapeDtypeStruct((rows, streams, width), jnp.bfloat16), MARK_SHAPE],
        input_output_aliases={4 + k: k for k in range(len(filled))},
        compiler_params=PARAMS,
        cost_estimate=cost(),
        name="finish",
    )(*plain(arrays), *filled, *tokens)
    return marked([result], mark)[0]


def close_mix(inner, first, rows, arrays, tables, streams, uses, filled=(), tokens=()):
    tokens = [*filled, *waits(tokens)]
    h = arrays[0][0]
    whole, width = h.shape[0], h.shape[1] // streams
    block = rows_block(rows)
    arrays = [*arrays, *tables]
    last = len(arrays)

    def by_rows(columns):
        return pl.BlockSpec((block, columns), lambda i: (first // block + i, 0))

    def fixed(height, columns):
        return pl.BlockSpec((height, columns), lambda i: (0, 0))

    if inner:
        out_specs = [by_rows(streams * width)]
        out_shape = [jax.ShapeDtypeStruct((whole, streams * width), jnp.float32)]
    else:
        out_specs = [pl.BlockSpec((block, streams, width), lambda i: (i, 0, 0))]
        out_shape = [jax.ShapeDtypeStruct((rows, streams, width), jnp.bfloat16)]
    if inner:
        out_specs += [by_rows(LANES), by_rows(width)]
        out_shape += [
            jax.ShapeDtypeStruct((whole, LANES), jnp.float32),
            jax.ShapeDtypeStruct((whole, width), jnp.bfloat16),
        ]
    out_specs += [fixed(16, width), fixed(8, LANES)]
    out_shape += [jax.ShapeDtypeStruct((16, width), jnp.float32), jax.ShapeDtypeStruct((8, LANES), jnp.float32)]
    return pl.pallas_call(
        functools.partial(close_kernel, streams, uses, width, inner, len(tokens)),
        grid=(rows // block,),
        in_specs=specs_for(arrays, block, {last - 2, last - 1}) + anywhere(len(tokens)),
        out_specs=out_specs,
        out_shape=out_shape,
        scratch_shapes=[
            pltpu.VMEM((streams * rows, width), jnp.bfloat16),
            pltpu.VMEM((streams * rows, LANES), jnp.bfloat16),
            pltpu.VMEM((streams * block, LANES), jnp.bfloat16),
            pltpu.VMEM((streams * block, width), jnp.float32),
            pltpu.VMEM((block, LANES), jnp.float32),
            pltpu.VMEM((2, GROUP, LANES), jnp.float32),
            pltpu.VMEM((LANES, width), jnp.bfloat16),
        ],
        input_output_aliases={len(arrays) + k: k for k in range(len(filled))},
        compiler_params=PARAMS,
        cost_estimate=cost(30 if inner else 0),
        name="close_feedforward" if inner else "close_attention",
    )(*plain(arrays), *tokens)


QUERY_ROWS = 256


def turn(values, cosine, sine):
    return values * cosine + pltpu.roll(values, HEAD_DIM // 2, 1) * sine


def turn_back(values, cosine, sine):
    return values * cosine - pltpu.roll(values, HEAD_DIM // 2, 1) * sine


def block_offset(mine, step, size, rows):
    return pl.multiple_of(lax.rem(mine + size - step, size) * rows, rows)


def allowed_keys(start_ref, first, rows, keys):
    row = first + lax.broadcasted_iota(jnp.int32, (rows, keys), 0)
    key = lax.broadcasted_iota(jnp.int32, (rows, keys), 1)
    return (key <= row) & (key >= start_ref[first : first + rows, 0:1])


def attend_kernel(size, *refs):
    mine_ref, start_ref, cosine_ref, sine_ref = refs[:4]
    raw = [refs[4 + 3 * s : 7 + 3 * s] for s in range(size)]
    q_ref, k_ref, v_ref, out_ref, log_ref, attended_ref = refs[4 + 3 * size :]
    mine = mine_ref[0]
    block = raw[0][0].shape[0]
    total = size * block
    for step in range(size):
        rows = pl.ds(block_offset(mine, step, size, block), block)
        cosine, sine = cosine_ref[rows, :], sine_ref[rows, :]
        q_ref[rows, :] = turn(raw[step][0][...], cosine, sine).astype(jnp.bfloat16)
        k_ref[rows, :] = turn(raw[step][1][...], cosine, sine).astype(jnp.bfloat16)
        v_ref[rows, :] = raw[step][2][...].astype(jnp.bfloat16)
    height = min(QUERY_ROWS, total)
    for first in range(0, total, height):
        keys = first + height
        scores = times_transposed(q_ref[first:keys, :], k_ref[:keys, :]) * HEAD_DIM**-0.5
        scores = jnp.where(allowed_keys(start_ref, first, height, keys), scores, MASKED)
        highest = jnp.max(scores, axis=1, keepdims=True)
        exponent = jnp.exp(scores - highest)
        row_total = jnp.sum(exponent, axis=1, keepdims=True)
        probs = (exponent * (1.0 / row_total)).astype(jnp.bfloat16)
        attended_ref[first:keys, :] = jnp.dot(
            probs, v_ref[:keys, :], preferred_element_type=jnp.float32
        ).astype(jnp.bfloat16)
        log_ref[first:keys, :] = jnp.broadcast_to(highest + jnp.log(row_total), (height, LANES))
    for step in range(size):
        rows = pl.ds(block_offset(mine, step, size, block), block)
        out_ref[step * block : (step + 1) * block, :] = attended_ref[rows, :]


def attend_back_kernel(size, kept, *refs):
    mine_ref, start_ref, cosine_ref, sine_ref, q_ref, k_ref, v_ref, log_ref = refs[:8]
    grads = refs[8 : 8 + size]
    dqkv_ref, d_out_ref, dq_ref, dk_ref, dv_ref = refs[8 + size + kept :]
    mine = mine_ref[0]
    head, heads = pl.program_id(0), pl.num_programs(0)
    block = grads[0].shape[0]
    total = size * block
    for step in range(size):
        d_out_ref[pl.ds(block_offset(mine, step, size, block), block), :] = grads[step][...]
    height = min(QUERY_ROWS, total)
    dk_ref[...] = jnp.zeros_like(dk_ref)
    dv_ref[...] = jnp.zeros_like(dv_ref)
    for first in range(0, total, height):
        keys = first + height
        q, d_out = q_ref[first:keys, :], d_out_ref[first:keys, :]
        k, v = k_ref[:keys, :], v_ref[:keys, :]
        scores = times_transposed(q, k) * HEAD_DIM**-0.5
        probs = jnp.where(
            allowed_keys(start_ref, first, height, keys), jnp.exp(scores - log_ref[first:keys, 0:1]), 0.0
        )
        d_probs = times_transposed(d_out, v)
        centre = jnp.sum(probs * d_probs, axis=1, keepdims=True)
        d_scores = (probs * (d_probs - centre)).astype(jnp.bfloat16)
        dv_ref[:keys, :] += transposed_times(probs.astype(jnp.bfloat16), d_out)
        dk_ref[:keys, :] += transposed_times(d_scores, q)
        dq_ref[first:keys, :] = jnp.dot(d_scores, k, preferred_element_type=jnp.float32)
    for step in range(size):
        rows = pl.ds(block_offset(mine, step, size, block), block)
        cosine, sine = cosine_ref[rows, :], sine_ref[rows, :]
        target = slice(step * block, (step + 1) * block)
        for part, values in enumerate(
            (
                turn_back(dq_ref[rows, :] * HEAD_DIM**-0.5, cosine, sine),
                turn_back(dk_ref[rows, :] * HEAD_DIM**-0.5, cosine, sine),
                dv_ref[rows, :],
            )
        ):
            columns = pl.ds(pl.multiple_of((part * heads + head) * HEAD_DIM, HEAD_DIM), HEAD_DIM)
            dqkv_ref[target, columns] = values.astype(jnp.bfloat16)


def whole_spec(shape):
    return pl.BlockSpec(shape, lambda h: (0,) * len(shape))


def head_spec(rows, first=0):
    return pl.BlockSpec((rows, HEAD_DIM), lambda h: (0, first + h))


def attend(raw_blocks, mine, starts, cosine, sine):
    size, block = len(raw_blocks), raw_blocks[0].shape[0]
    heads = raw_blocks[0].shape[1] // (3 * HEAD_DIM)
    total = size * block
    flat = jax.ShapeDtypeStruct((total, heads * HEAD_DIM), jnp.bfloat16)
    return pl.pallas_call(
        functools.partial(attend_kernel, size),
        grid=(heads,),
        in_specs=[pl.BlockSpec(memory_space=pltpu.SMEM)]
        + [whole_spec(a.shape) for a in (starts, cosine, sine)]
        + [head_spec(block, part * heads) for _ in range(size) for part in range(3)],
        out_specs=[head_spec(total)] * 5,
        out_shape=[flat] * 4 + [jax.ShapeDtypeStruct(flat.shape, jnp.float32)],
        scratch_shapes=[pltpu.VMEM((total, HEAD_DIM), jnp.bfloat16)],
        compiler_params=PARAMS,
        cost_estimate=cost(),
        name="attend",
    )(mine, starts, cosine, sine, *[raw for raw in raw_blocks for _ in range(3)])


def attend_back(heads_kept, grad_blocks, mine, starts, cosine, sine, tokens):
    tokens = waits(tokens)
    size, block = len(grad_blocks), grad_blocks[0].shape[0]
    total, columns = heads_kept[0].shape
    heads = columns // HEAD_DIM
    return pl.pallas_call(
        functools.partial(attend_back_kernel, size, len(tokens)),
        grid=(heads,),
        in_specs=[pl.BlockSpec(memory_space=pltpu.SMEM)]
        + [whole_spec(a.shape) for a in (starts, cosine, sine)]
        + [head_spec(total)] * 4
        + [head_spec(block)] * size
        + anywhere(len(tokens)),
        out_specs=whole_spec((total, 3 * columns)),
        out_shape=jax.ShapeDtypeStruct((total, 3 * columns), jnp.bfloat16),
        scratch_shapes=[pltpu.VMEM((total, HEAD_DIM), jnp.bfloat16)] + [pltpu.VMEM((total, HEAD_DIM), jnp.float32)] * 3,
        compiler_params=PARAMS,
        cost_estimate=cost(),
        name="attend_back",
    )(mine, starts, cosine, sine, *heads_kept, *grad_blocks, *tokens)


UNIT_TILE = 512


def forward_units_kernel(blocks, kept, *refs):
    gate_w_ref, up_w_ref, down_w_ref = refs[blocks : blocks + 3]
    gate_ref, up_ref, partial_ref, rows_ref, hidden_ref, mark_ref = refs[blocks + 3 + kept :]
    mark_ref[...] = jnp.zeros_like(mark_ref)
    x = jnp.concatenate([ref[...] for ref in refs[:blocks]], axis=0)
    gate, up = matmul(x, gate_w_ref[...]), matmul(x, up_w_ref[...])
    gate_ref[...] = gate
    up_ref[...] = up
    hidden = (gate / (1.0 + jnp.exp(-gate)) * up).astype(jnp.bfloat16)
    hidden_ref[...] = hidden
    part = times_transposed(hidden, down_w_ref[...])

    @pl.when(pl.program_id(0) == 0)
    def _():
        partial_ref[...] = part
        rows_ref[...] = x

    @pl.when(pl.program_id(0) > 0)
    def _():
        partial_ref[...] += part


def backward_units_kernel(kept, *refs):
    first_ref, second_ref, gate_ref, up_ref, down_w_ref, gate_w_ref, up_w_ref = refs[:7]
    partial_ref, rows_ref, d_gate_ref, d_up_ref, mark_ref = refs[7 + kept :]
    mark_ref[...] = jnp.zeros_like(mark_ref)
    d_out = jnp.concatenate([first_ref[...], second_ref[...]], axis=0)
    d_hidden = matmul(d_out, down_w_ref[...])
    gate = gate_ref[...]
    sigmoid = 1.0 / (1.0 + jnp.exp(-gate))
    d_gate = (d_hidden * up_ref[...] * (sigmoid + gate * sigmoid * (1.0 - sigmoid))).astype(jnp.bfloat16)
    d_up = (d_hidden * gate * sigmoid).astype(jnp.bfloat16)
    d_gate_ref[...] = d_gate
    d_up_ref[...] = d_up
    part = times_transposed(d_gate, gate_w_ref[...]) + times_transposed(d_up, up_w_ref[...])

    @pl.when(pl.program_id(0) == 0)
    def _():
        partial_ref[...] = part
        rows_ref[...] = d_out

    @pl.when(pl.program_id(0) > 0)
    def _():
        partial_ref[...] += part


def forward_units(pair, size, blocks, gate_up, down, filled, tokens=()):
    tokens = waits(tokens)
    each, width = blocks[0].shape
    count = len(blocks)
    rows = each * count // 2
    units = down.shape[1]
    tile = min(UNIT_TILE, units)
    tiles = units // tile
    weight = functools.partial(pl.BlockSpec, (width, tile))
    outs = pl.pallas_call(
        functools.partial(forward_units_kernel, count, len(filled) + len(tokens)),
        grid=(tiles,),
        in_specs=[pl.BlockSpec((each, width), lambda i: (0, 0))] * count
        + [weight(lambda i: (0, i)), weight(lambda i: (0, tiles + i)), weight(lambda i: (0, i))]
        + anywhere(len(filled) + len(tokens)),
        out_specs=[
            pl.BlockSpec((2 * rows, tile), lambda i: (0, i)),
            pl.BlockSpec((2 * rows, tile), lambda i: (0, i)),
            pl.BlockSpec((2 * rows, width), lambda i: (0, 0)),
            pl.BlockSpec((2 * rows, width), lambda i: (pair, 0)),
            pl.BlockSpec((2 * rows, tile), lambda i: (pair, i)),
            MARK_SPEC,
        ],
        out_shape=[
            jax.ShapeDtypeStruct((2 * rows, units), jnp.float32),
            jax.ShapeDtypeStruct((2 * rows, units), jnp.float32),
            jax.ShapeDtypeStruct((2 * rows, width), jnp.float32),
            jax.ShapeDtypeStruct((size * rows, width), jnp.bfloat16),
            jax.ShapeDtypeStruct((size * rows, units), jnp.bfloat16),
            MARK_SHAPE,
        ],
        input_output_aliases={count + 3 + k: 3 + k for k in range(len(filled))},
        compiler_params=PARAMS,
        cost_estimate=cost(),
        name="forward_units",
    )(*blocks, gate_up, gate_up, down, *filled, *tokens)
    outs = marked(outs[:-1], outs[-1])
    return outs[0], outs[1], outs[2], outs[3:]


def backward_units(pair, size, blocks, gate, up, gate_up, down, filled, tokens=()):
    tokens = waits(tokens)
    rows, width = blocks[0].shape
    units = down.shape[1]
    tile = min(UNIT_TILE, units)
    tiles = units // tile
    weight = functools.partial(pl.BlockSpec, (width, tile))
    by_tile = pl.BlockSpec((2 * rows, tile), lambda i: (0, i))
    outs = pl.pallas_call(
        functools.partial(backward_units_kernel, len(filled) + len(tokens)),
        grid=(tiles,),
        in_specs=[pl.BlockSpec((rows, width), lambda i: (0, 0))] * 2
        + [by_tile, by_tile]
        + [weight(lambda i: (0, i)), weight(lambda i: (0, i)), weight(lambda i: (0, tiles + i))]
        + anywhere(len(filled) + len(tokens)),
        out_specs=[
            pl.BlockSpec((2 * rows, width), lambda i: (0, 0)),
            pl.BlockSpec((2 * rows, width), lambda i: (pair, 0)),
            pl.BlockSpec((2 * rows, tile), lambda i: (pair, i)),
            pl.BlockSpec((2 * rows, tile), lambda i: (pair, i)),
            MARK_SPEC,
        ],
        out_shape=[
            jax.ShapeDtypeStruct((2 * rows, width), jnp.float32),
            jax.ShapeDtypeStruct((size * rows, width), jnp.bfloat16),
            jax.ShapeDtypeStruct((size * rows, units), jnp.bfloat16),
            jax.ShapeDtypeStruct((size * rows, units), jnp.bfloat16),
            MARK_SHAPE,
        ],
        input_output_aliases={7 + k: 1 + k for k in range(len(filled))},
        compiler_params=PARAMS,
        cost_estimate=cost(),
        name="backward_units",
    )(*blocks, gate, up, down, gate_up, gate_up, *filled, *tokens)
    outs = marked(outs[:-1], outs[-1])
    return outs[0], outs[1:]


def assemble_kernel(count, pieces, kept, table_ref, *refs):
    sources, outs, mark_ref = refs[:count], refs[count + kept : -1], refs[-1]
    mark_ref[...] = jnp.zeros_like(mark_ref)
    for k in range(count):

        @pl.when(pl.program_id(0) // pieces == k)
        def _(k=k):
            first = 0
            for out_ref in outs:
                columns = out_ref.shape[1]
                out_ref[...] = sources[k][:, first : first + columns].astype(jnp.float32)
                first += columns


def assemble(arrays, widths, table, tokens=()):
    tokens = waits(tokens)
    count = len(arrays)
    pieces = arrays[0][2]
    rows, columns = arrays[0][3], arrays[0][0].shape[1]
    *results, mark = pl.pallas_call(
        functools.partial(assemble_kernel, count, pieces, len(tokens)),
        grid_spec=pltpu.PrefetchScalarGridSpec(
            num_scalar_prefetch=1,
            grid=(count * pieces,),
            in_specs=[
                pl.BlockSpec(
                    (rows, columns),
                    lambda i, t, k=k, first=first: (first + jnp.clip(i - k * pieces, 0, pieces - 1), 0),
                )
                for k, (_, first, _, _) in enumerate(arrays)
            ]
            + anywhere(len(tokens)),
            out_specs=[pl.BlockSpec((rows, width), lambda i, t: (t[i], 0)) for width in widths] + [MARK_SPEC],
        ),
        out_shape=[jax.ShapeDtypeStruct((count * pieces * rows, width), jnp.float32) for width in widths] + [MARK_SHAPE],
        compiler_params=PARAMS,
        cost_estimate=cost(),
        name="assemble",
    )(table, *(array for array, *_ in arrays), *tokens)
    return marked(results, mark)


PRODUCT_TILE = 1024


def across_of(width, first):
    if width <= 2 * PRODUCT_TILE and first % width == 0:
        return width if width * 3 <= 5 * PRODUCT_TILE else width // 2
    return math.gcd(PRODUCT_TILE, width, first or width)


def joined_left(refs):
    left = [ref[...] for ref in refs]
    return left[0] if len(left) == 1 else jnp.concatenate(left, axis=0)


def away_kernel(blocks, core_ref, *refs):
    refs[-1][...] = jnp.zeros_like(refs[-1])
    refs[-2][...] = transposed_times(joined_left(refs[:blocks]), refs[blocks][...]).astype(jnp.bfloat16)


def own_kernel(blocks, scalars_ref, *refs):
    away_ref, kept_ref, mark_ref = refs[-3:]
    mark_ref[...] = jnp.zeros_like(mark_ref)
    product = transposed_times(joined_left(refs[:blocks]), refs[blocks][...])
    product = product + refs[blocks + 1][...].astype(jnp.float32)

    @pl.when(pl.program_id(0) == 0)
    def _():
        away_ref[...] = product.astype(jnp.bfloat16)

    @pl.when(pl.program_id(0) == 1)
    def _():
        kept_ref[...] = product


def away_product(core, left, right, columns, first, filled, tokens=()):
    tokens = waits(tokens)
    half = left[0].shape[1] // 2
    rows, width = right.shape
    down, across = min(PRODUCT_TILE, half), across_of(width, first)
    high, offset = half // down, first // across
    result, mark = pl.pallas_call(
        functools.partial(away_kernel, len(left)),
        grid_spec=pltpu.PrefetchScalarGridSpec(
            num_scalar_prefetch=1,
            grid=(high, width // across),
            in_specs=[
                pl.BlockSpec((block.shape[0], down), lambda i, j, c: (0, (1 - c[0]) * high + i)) for block in left
            ]
            + [pl.BlockSpec((rows, across), lambda i, j, c: (0, j))]
            + anywhere(len(filled) + len(tokens)),
            out_specs=[pl.BlockSpec((down, across), lambda i, j, c: (i, offset + j)), MARK_SPEC],
        ),
        out_shape=[jax.ShapeDtypeStruct((half, columns), jnp.bfloat16), MARK_SHAPE],
        input_output_aliases={2 + len(left): 0} if filled else {},
        compiler_params=PARAMS,
        cost_estimate=cost(),
        name="away_product",
    )(core, *left, right, *filled, *tokens)
    return marked([result], mark)[0]


def own_product(scalars, left, right, arrived, columns, first, rows_first, rows_here, filled, tokens=()):
    tokens = waits(tokens)
    half = left[0].shape[1] // 2
    rows, width = right.shape
    cut = rows_here // 2
    down, across = min(PRODUCT_TILE, cut), across_of(width, first)
    high, wide, offset = cut // down, width // across, first // across

    def row(g, i, c):
        return rows_first // down + jnp.where(g == 0, 1 - c[1], c[1]) * high + i

    *results, mark = pl.pallas_call(
        functools.partial(own_kernel, len(left)),
        grid_spec=pltpu.PrefetchScalarGridSpec(
            num_scalar_prefetch=1,
            grid=(2, high, wide),
            in_specs=[
                pl.BlockSpec((block.shape[0], down), lambda g, i, j, c: (0, c[0] * (half // down) + row(g, i, c)))
                for block in left
            ]
            + [
                pl.BlockSpec((rows, across), lambda g, i, j, c: (0, j)),
                pl.BlockSpec((down, across), lambda g, i, j, c: (row(g, i, c), offset + j)),
            ]
            + anywhere(len(filled) + len(tokens)),
            out_specs=[
                pl.BlockSpec(
                    (down, across),
                    lambda g, i, j, c: (jnp.where(g == 0, i, high - 1), offset + jnp.where(g == 0, j, wide - 1)),
                ),
                pl.BlockSpec(
                    (down, across),
                    lambda g, i, j, c: (jnp.where(g == 0, 0, i), offset + jnp.where(g == 0, 0, j)),
                ),
                MARK_SPEC,
            ],
        ),
        out_shape=[
            jax.ShapeDtypeStruct((cut, columns), jnp.bfloat16),
            jax.ShapeDtypeStruct((cut, columns), jnp.float32),
            MARK_SHAPE,
        ],
        input_output_aliases={3 + len(left) + k: k for k in range(len(filled))},
        compiler_params=PARAMS,
        cost_estimate=cost(),
        name="own_product",
    )(scalars, *left, right, arrived, *filled, *tokens)
    return marked(results, mark)


def backproject_kernel(d_ref, w_ref, *refs):
    refs[-1][...] = jnp.zeros_like(refs[-1])
    refs[-2][...] = times_transposed(d_ref[...], w_ref[...]).astype(refs[-2].dtype)


def backproject(rows_of, first, count, weight, kind, tokens=()):
    tokens = waits(tokens)
    array, rows = rows_of
    width, columns = weight.shape
    across = min(512, width)
    result, mark = pl.pallas_call(
        backproject_kernel,
        grid=(width // across, count),
        in_specs=[
            pl.BlockSpec((rows, columns), lambda j, i: (first + i, 0)),
            pl.BlockSpec((across, columns), lambda j, i: (j, 0)),
        ]
        + anywhere(len(tokens)),
        out_specs=[pl.BlockSpec((rows, across), lambda j, i: (i, j)), MARK_SPEC],
        out_shape=[jax.ShapeDtypeStruct((count * rows, width), kind), MARK_SHAPE],
        compiler_params=PARAMS,
        cost_estimate=cost(),
        name="backproject",
    )(array, weight, *tokens)
    return marked([result], mark)[0]


def project_kernel(count, *refs):
    refs[-1][...] = matmul(jnp.concatenate([ref[...] for ref in refs[:count]], axis=0), refs[count][...]).astype(jnp.bfloat16)


def project(blocks, weight, columns):
    rows, width = blocks[0].shape
    across = min(256, columns)
    return pl.pallas_call(
        functools.partial(project_kernel, len(blocks)),
        grid=(columns // across,),
        in_specs=[pl.BlockSpec((rows, width), lambda j: (0, 0))] * len(blocks)
        + [pl.BlockSpec((width, across), lambda j: (0, j))],
        out_specs=pl.BlockSpec((len(blocks) * rows, across), lambda j: (0, j)),
        out_shape=jax.ShapeDtypeStruct((len(blocks) * rows, columns), jnp.bfloat16),
        compiler_params=PARAMS,
        cost_estimate=cost(),
        name="project",
    )(*blocks, weight)


def out_project_kernel(count, *refs):
    refs[-1][...] = times_transposed(jnp.concatenate([ref[...] for ref in refs[:count]], axis=1), refs[count][...])


def out_project(blocks, weight):
    rows = blocks[0].shape[0]
    width, columns = weight.shape
    across = min(512, width)
    return pl.pallas_call(
        functools.partial(out_project_kernel, len(blocks)),
        grid=(width // across,),
        in_specs=[pl.BlockSpec(block.shape, lambda j: (0, 0)) for block in blocks]
        + [pl.BlockSpec((across, columns), lambda j: (j, 0))],
        out_specs=pl.BlockSpec((rows, across), lambda j: (0, j)),
        out_shape=jax.ShapeDtypeStruct((rows, width), jnp.float32),
        compiler_params=PARAMS,
        cost_estimate=cost(),
        name="out_project",
    )(*blocks, weight)


SUM_ROWS = 256


def halve_kernel(which_ref, own_ref, arrived_ref, *refs):
    away_ref, kept_ref, mark_ref = refs[-3:]
    mark_ref[...] = jnp.zeros_like(mark_ref)
    total = own_ref[...] + arrived_ref[...].astype(jnp.float32)

    @pl.when(pl.program_id(0) == 0)
    def _():
        away_ref[...] = total.astype(jnp.bfloat16)

    @pl.when(pl.program_id(0) == 1)
    def _():
        kept_ref[...] = total


def halve(own, arrived, which, tokens=()):
    tokens = waits(tokens)
    (own, own_first, rows), (arrived, arrived_first, _) = own, arrived
    half, columns = rows // 2, own.shape[1]
    tile = min(SUM_ROWS, half)
    tiles = half // tile

    def source(first):
        return pl.BlockSpec(
            (tile, columns), lambda g, t, w: (first // tile + jnp.where(g == 0, 1 - w[0], w[0]) * tiles + t, 0)
        )

    *results, mark = pl.pallas_call(
        halve_kernel,
        grid_spec=pltpu.PrefetchScalarGridSpec(
            num_scalar_prefetch=1,
            grid=(2, tiles),
            in_specs=[source(own_first), source(arrived_first)] + anywhere(len(tokens)),
            out_specs=[
                pl.BlockSpec((tile, columns), lambda g, t, w: (jnp.where(g == 0, t, tiles - 1), 0)),
                pl.BlockSpec((tile, columns), lambda g, t, w: (jnp.where(g == 0, 0, t), 0)),
                MARK_SPEC,
            ],
        ),
        out_shape=[
            jax.ShapeDtypeStruct((half, columns), jnp.bfloat16),
            jax.ShapeDtypeStruct((half, columns), jnp.float32),
            MARK_SHAPE,
        ],
        compiler_params=PARAMS,
        cost_estimate=cost(),
        name="halve",
    )(which, own, arrived, *tokens)
    return marked(results, mark)


def add_kernel(own, arrives, *refs):
    out_ref, mark_ref = refs[-2:]
    mark_ref[...] = jnp.zeros_like(mark_ref)
    rows = out_ref.shape[0] // own
    for k in range(own):
        values = refs[k][...].astype(jnp.float32)
        if arrives:
            values = values + refs[own + k][...].astype(jnp.float32)
        out_ref[k * rows : (k + 1) * rows, :] = values.astype(out_ref.dtype)


def add_low(own, arrived=(), tokens=(), kind=jnp.bfloat16):
    tokens = waits(tokens)
    rows, columns = own[0][2], own[0][0].shape[1]
    across = min(512, columns)
    total = rows * len(own)
    ranges = [*own, *arrived]
    result, mark = pl.pallas_call(
        functools.partial(add_kernel, len(own), bool(arrived)),
        grid=(columns // across,),
        in_specs=[
            pl.BlockSpec((rows, across), lambda j, first=first // rows: (first, j)) for _, first, rows in ranges
        ]
        + anywhere(len(tokens)),
        out_specs=[pl.BlockSpec((total, across), lambda j: (0, j)), MARK_SPEC],
        out_shape=[jax.ShapeDtypeStruct((total, columns), kind), MARK_SHAPE],
        compiler_params=PARAMS,
        cost_estimate=cost(),
        name="add_low",
    )(*(array for array, _, _ in ranges), *tokens)
    return marked([result], mark)[0]


def whole_range(array):
    return (array, 0, array.shape[0])


def join_kernel(count, tiles, *refs):
    out_ref, mark_ref = refs[-2:]
    mark_ref[...] = jnp.zeros_like(mark_ref)
    for k in range(count):

        @pl.when(pl.program_id(0) // tiles == k)
        def _(k=k):
            out_ref[...] = refs[k][...]


def join(arrays, tokens=()):
    tokens = waits(tokens)
    rows, columns = arrays[0].shape
    tile = min(2 * SUM_ROWS, rows)
    tiles = rows // tile
    result, mark = pl.pallas_call(
        functools.partial(join_kernel, len(arrays), tiles),
        grid=(len(arrays) * tiles,),
        in_specs=[
            pl.BlockSpec((tile, columns), lambda i, k=k: (jnp.clip(i - k * tiles, 0, tiles - 1), 0))
            for k in range(len(arrays))
        ]
        + anywhere(len(tokens)),
        out_specs=[pl.BlockSpec((tile, columns), lambda i: (i, 0)), MARK_SPEC],
        out_shape=[jax.ShapeDtypeStruct((len(arrays) * rows, columns), arrays[0].dtype), MARK_SHAPE],
        compiler_params=PARAMS,
        cost_estimate=cost(),
        name="join",
    )(*arrays, *tokens)
    return marked([result], mark)[0]


def ring_shift(block):
    size = lax.axis_size("tensor")
    return lax.ppermute(block, "tensor", [(i, (i + 1) % size) for i in range(size)])


def ring_gather(block):
    blocks = [block]
    for _ in range(lax.axis_size("tensor") - 1):
        blocks.append(ring_shift(blocks[-1]))
    return blocks


def row_halves(ranges):
    return [
        [(array, first + k * (rows // 2), rows // 2) for array, first, rows in ranges] for k in range(2)
    ]


def ring_sums(step, size, ranges, arrived, tokens):
    if step < size - 1:
        return [add_low(ranges, arrived, tokens)]
    arrived = row_halves(arrived) if arrived else ((), ())
    return [add_low(own, other, tokens) for own, other in zip(row_halves(ranges), arrived)]


def own_columns(attended):
    blocks = jnp.split(attended, lax.axis_size("tensor"))
    size = len(blocks)
    return [blocks[0]] + [
        lax.ppermute(blocks[size - step], "tensor", [(i, (i + step) % size) for i in range(size)])
        for step in range(1, size)
    ]


def swap(values, axis, bit):
    return lax.ppermute(values, axis, [(i, i ^ (1 << bit)) for i in range(lax.axis_size(axis))])


def bit_of(axis, bit):
    return (lax.axis_index(axis) >> bit) & 1


def axis_orders():
    bits = (lax.axis_size("dp") - 1).bit_length()
    return list(range(1, bits)), list(range(bits - 1, 0, -1))


class Butterfly:
    def __init__(self, halved, orders):
        self.orders, self.level, self.levels = orders, 0, len(orders[0])
        self.ready, self.kept = [away for away, _ in halved], [kept for _, kept in halved]

    def step(self, *after):
        level, levels = self.level, self.levels
        if level == 2 * levels:
            return self
        bits = [order[level] if level < levels else order[2 * levels - 1 - level] for order in self.orders]
        arrived = [swap(away, "dp", bit) for away, bit in zip(self.ready, bits)]
        self.level += 1
        if self.level < levels:
            halved = [
                halve(
                    (kept, 0, kept.shape[0]),
                    (other, 0, kept.shape[0]),
                    jnp.full((1,), bit_of("dp", order[self.level]), jnp.int32),
                    after,
                )
                for kept, other, order in zip(self.kept, arrived, self.orders)
            ]
            self.ready, self.kept = [away for away, _ in halved], [kept for _, kept in halved]
        elif self.level == levels:
            self.ready = [
                add_low([whole_range(kept)], [whole_range(other)], after) for kept, other in zip(self.kept, arrived)
            ]
        elif self.level < 2 * levels:
            self.ready = [join(both, after) for both in zip(self.ready, arrived)]
        else:
            self.ready = [join([array for both in zip(self.ready, arrived) for array in both], after)]
        return self

    def gathered(self, *after):
        while self.level < 2 * self.levels:
            self.step(*after)
        return self.ready[0]


def own_scalars(order):
    return jnp.stack([bit_of("dp", 0), bit_of("dp", order[0])]).astype(jnp.int32)


def pieces_of(joined, parts, part=None):
    count = parts << ((lax.axis_size("dp") - 1).bit_length() - 1)
    rows = joined.shape[0] // count
    each = count // parts
    return [
        (half, 0, count, rows) if part is None else (half, part * each, each, rows)
        for half in (joined, swap(joined, "dp", 0))
    ]


class SumEverywhere:
    def __init__(self, values):
        self.values = values
        self.left = [
            (axis, bit) for axis in ("tensor", "dp") for bit in range((lax.axis_size(axis) - 1).bit_length())
        ]

    def step(self, *after):
        axis, bit = self.left.pop(0)
        arrived = swap(self.values, axis, bit)
        self.values = add_low([whole_range(self.values)], [whole_range(arrived)], after, jnp.float32)
        return self.values

    def finished(self, last):
        while len(self.left) > last:
            self.step()
        return self.values


def piece_rows(orders):
    levels = len(orders[0])
    entries = []
    for flip in (0, 1):
        core = bit_of("dp", 0) ^ flip
        for k, order in enumerate(orders):
            for position in range(1 << levels):
                row = jnp.int32(0)
                for level, bit in enumerate(order):
                    digit = (position >> (levels - 1 - level)) & 1
                    row = row * 2 + (bit_of("dp", bit) ^ digit)
                entries.append((core * len(orders) + k) * (1 << levels) + row)
    return jnp.stack(entries).astype(jnp.int32)


def segments_from(slot_lengths, group_rows):
    bounds = jnp.cumsum(slot_lengths)
    row_ids = jnp.arange(group_rows, dtype=jnp.int32)
    segment = jnp.sum((row_ids[:, None] >= bounds[None, :]).astype(jnp.int32), axis=1)
    starting = jnp.concatenate([jnp.zeros((1,), jnp.int32), bounds])
    labels = jnp.arange(starting.shape[0], dtype=jnp.int32)
    begins = jnp.sum(jnp.where(segment[:, None] == labels[None, :], starting[None, :], 0), axis=1)
    return (segment, begins)


def group_layout(lengths, permutation, group_rows, seq_count):
    group_index = lax.axis_index("dp")
    chosen = lax.dynamic_slice_in_dim(permutation, group_index * seq_count, seq_count)
    matches = chosen[:, None] == jnp.arange(permutation.shape[0], dtype=jnp.int32)[None, :]
    slot_lengths = jnp.sum(jnp.where(matches, lengths[None, :], 0), axis=1)
    return segments_from(slot_lengths, group_rows)


def rope_tables(position):
    halfway = HEAD_DIM // 2
    frequency = THETA ** (-(2.0 * jnp.arange(halfway, dtype=jnp.float32)) / HEAD_DIM)
    angles = position.astype(jnp.float32)[:, None] * frequency[None, :]
    cosine, sine = jnp.cos(angles), jnp.sin(angles)
    return jnp.concatenate([cosine, cosine], axis=1), jnp.concatenate([-sine, sine], axis=1)


def gather_rows(*weights):
    return lax.all_gather(jnp.concatenate(weights, axis=1), "dp", axis=0, tiled=True)


def per_device(
    streams,
    cotangent,
    lengths,
    permutation,
    query_weight,
    key_weight,
    value_weight,
    out_weight,
    gate_weight,
    up_weight,
    down_weight,
    mix_static,
    mix_weight,
    mix_scale,
):
    MARKS.clear()
    qkv_full = gather_rows(query_weight, key_weight, value_weight)
    gate_up_full = gather_rows(gate_weight, up_weight)
    down_full = gather_rows(down_weight)
    local_rows, count, width = streams.shape
    uses = mix_static.shape[2]
    sizes = (count, uses)
    size = lax.axis_size("tensor")
    group_rows = local_rows * size
    mine = lax.axis_index("tensor")
    place_index = jnp.full((1,), mine, jnp.int32)
    core = jnp.full((1,), bit_of("dp", 0), jnp.int32)
    units = gate_weight.shape[1]
    seq_count = permutation.shape[0] // lax.axis_size("dp")

    inputs = streams.reshape(local_rows, count * width)
    cotangents = cotangent.reshape(local_rows, count * width)
    tables_a = mix_tables(mix_static[0], mix_weight[0], mix_scale[0])
    tables_f = mix_tables(mix_static[1], mix_weight[1], mix_scale[1])
    segment, begins = group_layout(lengths, permutation, group_rows, seq_count)
    cosine, sine = rope_tables(jnp.arange(group_rows, dtype=jnp.int32) - begins)
    starts = jnp.broadcast_to(begins[:, None], (group_rows, LANES))
    local_segment = lax.dynamic_slice_in_dim(segment, mine * local_rows, local_rows)
    valid = jnp.broadcast_to((local_segment < seq_count).astype(jnp.float32)[:, None], (local_rows, LANES))

    others = [
        lax.ppermute(out_weight, "tensor", [(i, (i + step) % size) for i in range(size)]) for step in range(1, size)
    ]
    normed_a, saved_a = open_attention(inputs, tables_a, *sizes)
    out_full = gather_rows(out_weight, *hold(others, normed_a))
    input_blocks = ring_gather(normed_a)
    query, key, value, attended, log_totals = attend(
        [matmul(block, qkv_full) for block in input_blocks], place_index, starts, cosine, sine
    )
    out_a = out_project(own_columns(attended), out_full)
    half_rows = local_rows // 2
    normed_f, d_out_f, saved_f, middle = open_feedforward(
        inputs, saved_a, out_a, cotangents, valid, tables_f, *sizes
    )
    orders = axis_orders()
    steps = 2 * len(orders[0])
    whole_table, half_tables = piece_rows(orders), [piece_rows([order]) for order in orders]

    def pair_of(arrays, pair):
        return arrays[2 * pair : 2 * pair + 2]

    blocks, gates, ups, partials_f, filled = [normed_f], [], [], [], []

    def forward(pair, filled):
        gate, up, partial, filled = forward_units(pair, size, pair_of(blocks, pair), gate_up_full, down_full, filled)
        gates.append(gate)
        ups.append(up)
        partials_f.append(partial)
        return filled

    for step in range(1, size):
        blocks.append(ring_shift(blocks[-1]))
        if step % 2 == 0:
            filled = forward(step // 2 - 1, filled)
    last_pair = size // 2 - 1
    grads, partials_n, filled_back = list(hold([d_out_f], blocks[-1], *partials_f)), [], []
    for step in range(1, size):
        arrived = ring_shift(grads[-1])
        if step == 1:
            filled = forward(last_pair, filled)
            (arrived,) = hold([arrived], partials_f[-1])
        elif step % 2 == 0:
            pair = step // 2 - 1
            partial, filled_back = backward_units(
                pair, size, pair_of(grads, pair), gates[pair], ups[pair], gate_up_full, down_full, filled_back
            )
            partials_n.append(partial)
            (arrived,) = hold([arrived], partial)
        grads.append(arrived)
    feedforward_rows, hidden_rows = filled

    def both_parts(index):
        first = (index % 2) * local_rows
        return [(partials_f[index // 2], first, local_rows), (partials_n[index // 2], first, local_rows)]

    half = width // 2
    totals = ring_sums(1, size, both_parts(1), (), [grads[-1]])
    for step in range(2, size + 1):
        arrived, total = [ring_shift(one) for one in totals], totals[0]
        tokens = []
        if step == 2:
            partial, filled_back = backward_units(
                last_pair,
                size,
                pair_of(grads, last_pair),
                gates[last_pair],
                ups[last_pair],
                gate_up_full,
                down_full,
                filled_back,
                [total],
            )
            partials_n.append(partial)
            grad_rows, *unit_rows = filled_back
            aways = [away_product(core, [feedforward_rows], rows, units, 0, []) for rows in unit_rows]
            tokens = aways
        elif step == 3:
            others = [swap(away, "dp", 0) for away in hold(aways, total)]
            down_away = away_product(core, [grad_rows], hidden_rows, units, 0, [], [total])
            gate_up_sum = Butterfly(
                [
                    own_product(own_scalars(order), [feedforward_rows], rows, other, units, 0, 0, half, [], [down_away])
                    for order, rows, other in zip(orders, unit_rows, others)
                ],
                orders,
            )
            tokens = [*gate_up_sum.ready, down_away]
        elif step == 4:
            down_other = swap(*hold([down_away], total), "dp", 0)
            down_sum = Butterfly(
                [
                    own_product(
                        own_scalars(order), [grad_rows], hidden_rows, down_other, units, 0, k * half // 2, half // 2, [], [total]
                    )
                    for k, order in enumerate(orders)
                ],
                orders,
            )
            tokens = down_sum.ready
        if step < size:
            here = [(arrived[0], 0, local_rows), (arrived[0], local_rows, local_rows)]
            totals = ring_sums(step, size, both_parts(step), here, tokens)
    filled, sums_f = [], []
    for k, both in enumerate(arrived):
        first = k * half_rows
        own_f, own_n = (partials_f[0], first), (partials_n[0], first)
        rest = [(a, first) for a in (valid, saved_a, out_a)]
        arrays = [(a, first) for a in (middle, saved_f, cotangents)]
        *filled, weight_sum, small = close_mix(
            True,
            first,
            half_rows,
            [*arrays, (both, half_rows), own_n, (both, 0), own_f, *rest],
            tables_f,
            *sizes,
            filled,
            tokens,
        )
        sums_f.append((weight_sum, small))
        tokens = []
    middle_grad, d_branch_a, d_out_a = filled

    def finished(tokens):
        filled = []
        for k, both in enumerate(arrived_last):
            filled = [finish(k * half_rows, middle, saved_f, (both, 0, half_rows), partials_f[0], *sizes, filled, tokens)]
        return filled[0]

    arrived_last = arrived

    output_grads = [d_out_a]
    for step in range(1, size):
        arrived = ring_shift(output_grads[-1])
        after = output_grads[-1]
        tokens = []
        if step == 1:
            out_streams = finished([after])
            tokens = [*gate_up_sum.step(after).ready, *down_sum.step(after).ready, out_streams]
        elif step == 2:
            tokens = gate_up_sum.step(after).ready
        if tokens:
            (arrived,) = hold([arrived], *tokens)
        output_grads.append(arrived)
        if step == 3:
            tokens = gate_up_sum.step(after).ready
    attended_grads = [project([block], out_full, attended.shape[1]) for block in output_grads]
    output_rows = output_grads
    d_qkv = attend_back(
        [query, key, value, log_totals], attended_grads, place_index, starts, cosine, sine, tokens
    )
    total = backproject((d_qkv, local_rows), 1, 1, qkv_full, jnp.bfloat16)
    columns = attended.shape[1]
    for step in range(2, size + 1):
        arrived = ring_shift(total)
        tokens = []
        if step == 2:
            away = away_product(core, input_blocks, d_qkv, 4 * columns, 0, [], [total])
            away = away_product(core, output_rows, attended, 4 * columns, 3 * columns, [away])
            own_partials = [backproject((d_qkv, local_rows), 2, 1, qkv_full, jnp.float32, [away])]
            gate_up_joined = gate_up_sum.gathered(*own_partials)
            tokens = [away, gate_up_joined, *down_sum.step(*own_partials).ready]
        elif step == 3:
            (away,) = hold([away], total)
            other = swap(away, "dp", 0)
            own_partials.append(backproject((d_qkv, local_rows), 3 % size, size - 3, qkv_full, jnp.float32, [total]))
            halved = []
            for k, order in enumerate(orders):
                place = (4 * columns, 0, k * half // 2, half // 2)
                scalars = own_scalars(order)
                both = own_product(scalars, input_blocks, d_qkv, other, *place, [], [own_partials[-1]])
                place = (4 * columns, 3 * columns, k * half // 2, half // 2)
                halved.append(own_product(scalars, output_rows, attended, other, *place, both))
            attention_sum = Butterfly(halved, orders)
            tokens = [*attention_sum.ready, *down_sum.step(*attention_sum.ready).ready]
        elif step == 4:
            (gate_up_joined,) = hold([gate_up_joined], total)
            gate_pieces, up_pieces = (pieces_of(gate_up_joined, 2, k) for k in range(2))
            own_partial = backproject((d_qkv, local_rows), 0, 1, qkv_full, jnp.float32, [total])
            (gate_grad,) = assemble(gate_pieces, [units], half_tables[0], [own_partial])
            tokens = attention_sum.step(gate_grad).ready
        if step < size:
            place = (own_partials[0], 0) if step == 2 else (own_partials[1], (step - 3) * local_rows)
            total = add_low([(*place, local_rows)], [whole_range(arrived)], tokens)
    arrays = [(a, 0) for a in (inputs, saved_a, middle_grad, arrived, own_partial, d_branch_a)]
    input_grad, weight_sum_a, small_a = close_mix(
        False,
        0,
        local_rows,
        arrays,
        tables_a,
        *sizes,
        tokens=tokens,
    )
    height = width // LANES

    def flat(weight_sum, small):
        summed = weight_sum[:uses] + weight_sum[8 : 8 + uses]
        return jnp.concatenate([summed.reshape(uses * height, LANES), small])

    def unpacked(sums):
        constants = sums[uses * height : uses * height + 2, : count * uses].reshape(2, count, uses)
        return constants[0], sums[: uses * height].reshape(uses, width).T, jnp.sum(constants[1], axis=0)

    weight_sum_f, small_f = (one + other for one, other in zip(*sums_f))
    sums = SumEverywhere(jnp.concatenate([flat(weight_sum_f, small_f), flat(weight_sum_a, small_a)]))
    attention_sum.step(small_a)
    (up_grad,) = assemble(up_pieces, [units], half_tables[1], [sums.values, *attention_sum.ready])
    attention_sum.step(sums.step(up_grad))
    down_joined = down_sum.gathered(*attention_sum.ready)
    after = sums.step(down_joined)
    (down_grad,) = assemble(pieces_of(down_joined, 2), [units], whole_table, [after])
    attention_joined = attention_sum.gathered(sums.step(down_grad))
    after = sums.step(attention_joined)
    query_grad, key_grad, value_grad, out_grad = assemble(
        pieces_of(attention_joined, 2), [columns] * 4, whole_table, [sums.finished(0)]
    )
    (static_f, weight_f, scale_f), (static_a, weight_a, scale_a) = (
        unpacked(part) for part in jnp.split(sums.finished(0), 2)
    )
    return (
        out_streams,
        input_grad,
        query_grad,
        key_grad,
        value_grad,
        out_grad,
        gate_grad,
        up_grad,
        down_grad,
        jnp.stack([static_a, static_f]),
        jnp.stack([weight_a, weight_f]),
        jnp.stack([scale_a, scale_f]),
    )


def solution(mesh):
    placed = (
        P(("dp", "tensor"), None, None),
        P(("dp", "tensor"), None, None),
        P(),
        P(),
        P("dp", "tensor"),
        P("dp", "tensor"),
        P("dp", "tensor"),
        P("dp", "tensor"),
        P("dp", "tensor"),
        P("dp", "tensor"),
        P("dp", "tensor"),
        P(),
        P(),
        P(),
    )
    return jax.shard_map(
        per_device,
        mesh=mesh,
        in_specs=placed,
        out_specs=(
            P(("dp", "tensor"), None, None),
            P(("dp", "tensor"), None, None),
            P(None, "tensor"),
            P(None, "tensor"),
            P(None, "tensor"),
            P(None, "tensor"),
            P(None, "tensor"),
            P(None, "tensor"),
            P(None, "tensor"),
            P(),
            P(),
            P(),
        ),
        check_vma=False,
    )
```

```python
import functools
import math
import jax
import jax.numpy as jnp
from jax import lax
from jax.experimental import pallas as pl
from jax.experimental.pallas import tpu as pltpu
from jax.sharding import PartitionSpec as P

HEAD_DIM = 128
EPSILON = 1e-05
THETA = 10000.0
MASKED = -1e30
LANES = 128
GROUP = 16
CHUNK = 512
PARAMS = pltpu.CompilerParams(vmem_limit_bytes=50 * 1024 * 1024)


def matmul(left, right):
    return jnp.dot(left, right, preferred_element_type=jnp.float32)


def times_transposed(left, right):
    return lax.dot_general(
        left, right, (((1,), (1,)), ((), ())), preferred_element_type=jnp.float32
    )


def transposed_times(left, right):
    return lax.dot_general(
        left, right, (((0,), (0,)), ((), ())), preferred_element_type=jnp.float32
    )


MARKS = {}


def marked(results, mark):
    for one in results:
        MARKS[id(one)] = (one, mark)
    return results


def waits(tokens):
    each = {id(t): t for t in (MARKS[id(one)][1] if id(one) in MARKS else one for one in tokens)}
    return list(each.values())


MARK_SPEC = pl.BlockSpec((8, LANES), lambda *index: (0, 0))
MARK_SHAPE = jax.ShapeDtypeStruct((8, LANES), jnp.float32)


def anywhere(count):
    return [pl.BlockSpec(memory_space=pl.ANY)] * count


def cost(microseconds=0):
    return pl.CostEstimate(flops=int(microseconds * 1e9), bytes_accessed=0, transcendentals=0)


def hold(values, *tokens):
    tokens = waits(tokens)

    def nothing(*refs):
        pass

    return pl.pallas_call(
        nothing,
        in_specs=anywhere(len(values) + len(tokens)),
        out_specs=anywhere(len(values)),
        out_shape=[jax.ShapeDtypeStruct(a.shape, a.dtype) for a in values],
        input_output_aliases={k: k for k in range(len(values))},
        name="hold",
    )(*values, *tokens)


def lanes_of(rows):
    return lax.broadcasted_iota(jnp.int32, (rows, LANES), 1)


def column(values, lane):
    return values[:, lane : lane + 1]


def place(values, columns, first):
    lane = lanes_of(values.shape[0])
    for offset, one in enumerate(columns):
        values = jnp.where(lane == first + offset, one, values)
    return values


def fold(values):
    total = values[:, :LANES]
    for start in range(LANES, values.shape[1], LANES):
        total = total + values[:, start : start + LANES]
    return total


def row_sum(values):
    return jnp.sum(values, axis=1, keepdims=True)


def rolled(values, shift):
    shift = shift % LANES
    return values if shift == 0 else pltpu.roll(values, shift, 1)


def coefficients(projected, means, rsqrts, param_ref, sums_ref, streams, uses, parts, centred):
    rows = projected[0].shape[0]
    lane = lanes_of(rows)
    gathered = jnp.zeros((rows, LANES), jnp.float32)
    sums = jnp.zeros((rows, LANES), jnp.float32)
    for j in range(streams):
        total = joined(projected[j], parts)
        if not centred:
            total = total - means[j] * sums_ref[0:1, :]
        total = total * rsqrts[j]
        inside = (lane >= j * uses) & (lane < (j + 1) * uses)
        gathered = jnp.where(inside, rolled(total, j * uses), gathered)
        sums = jnp.where(inside, rolled(jnp.broadcast_to(sums_ref[0:1, :], (rows, LANES)), j * uses), sums)
    bent = jnp.tanh(gathered)
    return gathered, bent, param_ref[0:1, :] + param_ref[1:2, :] * bent, sums


def pack_saved(coeffs, bent, gathered, sums, means, rsqrts, mean_e, rsqrt_e, streams, uses):
    lane = lanes_of(coeffs.shape[0])
    count = streams * uses
    saved = jnp.where(lane < count, coeffs, 0.0)
    saved = jnp.where((lane >= count) & (lane < 2 * count), rolled(bent, count), saved)
    saved = jnp.where((lane >= 2 * count) & (lane < 3 * count), rolled(gathered, 2 * count), saved)
    first = 3 * count + 2 * streams + 2
    saved = jnp.where((lane >= first) & (lane < first + count), rolled(sums, first), saved)
    return place(saved, [*means, *rsqrts, mean_e, rsqrt_e], 3 * count)


def centre_stats(total, values_of, width):
    mean = row_sum(total) * (1.0 / width)
    spread = None
    for start in range(0, width, CHUNK):
        centred = values_of(start) - mean
        square = fold(centred * centred)
        spread = square if spread is None else spread + square
    return mean, lax.rsqrt(row_sum(spread) * (1.0 / width) + EPSILON)


def entering_norm(read, coeffs, streams, uses, width, entering_ref, rows):
    total = None
    for start in range(0, width, CHUNK):
        entering = column(coeffs, 0) * read(0, start)
        for j in range(1, streams):
            entering = entering + column(coeffs, j * uses) * read(j, start)
        entering_ref[rows, start : start + CHUNK] = entering
        part = fold(entering)
        total = part if total is None else total + part
    return centre_stats(total, lambda start: entering_ref[rows, start : start + CHUNK], width)


def weight_parts(w_ref, parts_ref, sums_ref, parts):
    @pl.when(pl.program_id(0) == 0)
    def _():
        rest = w_ref[...]
        rows, width = rest.shape
        each = []
        for _ in range(parts):
            each.append(rest.astype(jnp.bfloat16).astype(jnp.float32))
            rest = rest - each[-1]
        each.append(jnp.zeros((LANES - parts * rows, width), jnp.float32))
        parts_ref[...] = jnp.concatenate(each, axis=0).astype(jnp.bfloat16)
        sums = times_transposed(jnp.ones((8, width), jnp.bfloat16), parts_ref[...])
        sums_ref[...] = joined(sums, parts)


def joined(values, parts):
    total = values
    for part in range(1, parts):
        total = total + rolled(values, -8 * part)
    return total


def open_attention_kernel(
    streams, uses, width, x_ref, w_ref, param_ref, normed_ref, saved_ref, raw_ref, entering_ref, parts_ref, sums_ref
):
    block = x_ref.shape[0]
    weight_parts(w_ref, parts_ref, sums_ref, 3)
    stacked = jnp.concatenate([x_ref[:, j * width : (j + 1) * width] for j in range(streams)], axis=0)
    raw_ref[...] = times_transposed(stacked, parts_ref[...])

    def body(index, carry):
        first = pl.multiple_of(index * GROUP, GROUP)
        rows = pl.ds(first, GROUP)

        def read(j, start):
            return x_ref[rows, j * width + start : j * width + start + CHUNK].astype(jnp.float32)

        means, rsqrts, projected = [], [], []
        for j in range(streams):
            total = None
            for start in range(0, width, CHUNK):
                part = fold(read(j, start))
                total = part if total is None else total + part
            mean, rsqrt = centre_stats(total, functools.partial(read, j), width)
            means.append(mean)
            rsqrts.append(rsqrt)
            projected.append(raw_ref[pl.ds(pl.multiple_of(j * block + first, GROUP), GROUP), :])
        gathered, bent, coeffs, sums = coefficients(
            projected, means, rsqrts, param_ref, sums_ref, streams, uses, 3, False
        )
        mean_e, rsqrt_e = entering_norm(read, coeffs, streams, uses, width, entering_ref, rows)
        for start in range(0, width, CHUNK):
            normed_ref[rows, start : start + CHUNK] = (
                (entering_ref[rows, start : start + CHUNK] - mean_e) * rsqrt_e
            ).astype(jnp.bfloat16)
        saved_ref[rows, :] = pack_saved(
            coeffs, bent, gathered, sums, means, rsqrts, mean_e, rsqrt_e, streams, uses
        )
        return carry

    lax.fori_loop(0, block // GROUP, body, 0)


def open_feedforward_kernel(streams, uses, width, *refs):
    x_ref, saved_a_ref, out_ref, g_ref, valid_ref, w_ref, param_ref = refs[:7]
    normed_ref, grad_ref, saved_ref, h_ref = refs[7:11]
    high_ref, low_ref, raw_ref, entering_ref, stats_ref, parts_ref, sums_ref = refs[11:]
    block = x_ref.shape[0]
    weight_parts(w_ref, parts_ref, sums_ref, 2)
    count = streams * uses

    def first_pass(index, carry):
        first = pl.multiple_of(index * GROUP, GROUP)
        rows = pl.ds(first, GROUP)
        coeffs = saved_a_ref[rows, :]
        totals = [None] * streams
        for start in range(0, width, CHUNK):
            out = out_ref[rows, start : start + CHUNK]
            values = [
                x_ref[rows, j * width + start : j * width + start + CHUNK].astype(jnp.float32)
                for j in range(streams)
            ]
            for i in range(streams):
                mixed = column(coeffs, i * uses + streams + 1) * out
                for j in range(streams):
                    mixed = mixed + column(coeffs, j * uses + 1 + i) * values[j]
                h_ref[rows, i * width + start : i * width + start + CHUNK] = mixed
                part = fold(mixed)
                totals[i] = part if totals[i] is None else totals[i] + part
        stats = jnp.zeros((GROUP, LANES), jnp.float32)
        means, rsqrts = [], []
        for i in range(streams):
            mean = row_sum(totals[i]) * (1.0 / width)
            spread = None
            for start in range(0, width, CHUNK):
                centred = h_ref[rows, i * width + start : i * width + start + CHUNK] - mean
                high = centred.astype(jnp.bfloat16)
                target = pl.ds(pl.multiple_of(i * block + first, GROUP), GROUP)
                high_ref[target, start : start + CHUNK] = high
                low_ref[target, start : start + CHUNK] = (centred - high.astype(jnp.float32)).astype(jnp.bfloat16)
                square = fold(centred * centred)
                spread = square if spread is None else spread + square
            means.append(mean)
            rsqrts.append(lax.rsqrt(row_sum(spread) * (1.0 / width) + EPSILON))
        stats_ref[rows, :] = place(stats, [*means, *rsqrts], 0)
        return carry

    lax.fori_loop(0, block // GROUP, first_pass, 0)
    raw_ref[...] = times_transposed(high_ref[...], parts_ref[...]) + times_transposed(
        low_ref[...], parts_ref[...]
    )

    def second_pass(index, carry):
        first = pl.multiple_of(index * GROUP, GROUP)
        rows = pl.ds(first, GROUP)
        stats = stats_ref[rows, :]
        means = [column(stats, j) for j in range(streams)]
        rsqrts = [column(stats, streams + j) for j in range(streams)]
        projected = [raw_ref[pl.ds(pl.multiple_of(j * block + first, GROUP), GROUP), :] for j in range(streams)]
        gathered, bent, coeffs, sums = coefficients(
            projected, means, rsqrts, param_ref, sums_ref, streams, uses, 2, True
        )

        def read(j, start):
            return h_ref[rows, j * width + start : j * width + start + CHUNK]

        mean_e, rsqrt_e = entering_norm(read, coeffs, streams, uses, width, entering_ref, rows)
        branch = [column(coeffs, i * uses + streams + 1) * valid_ref[rows, 0:1] for i in range(streams)]
        for start in range(0, width, CHUNK):
            normed_ref[rows, start : start + CHUNK] = (
                (entering_ref[rows, start : start + CHUNK] - mean_e) * rsqrt_e
            ).astype(jnp.bfloat16)
            grad = None
            for i in range(streams):
                term = branch[i] * g_ref[rows, i * width + start : i * width + start + CHUNK].astype(jnp.float32)
                grad = term if grad is None else grad + term
            grad_ref[rows, start : start + CHUNK] = grad.astype(jnp.bfloat16)
        saved_ref[rows, :] = pack_saved(
            coeffs, bent, gathered, sums, means, rsqrts, mean_e, rsqrt_e, streams, uses
        )
        return carry

    lax.fori_loop(0, block // GROUP, second_pass, 0)


def finish_kernel(streams, uses, width, h_ref, saved_ref, arrived_ref, partial_ref, *refs):
    y_ref, mark_ref = refs[-2:]
    mark_ref[...] = jnp.zeros_like(mark_ref)

    def body(index, carry):
        rows = pl.ds(pl.multiple_of(index * GROUP, GROUP), GROUP)
        coeffs = saved_ref[rows, :]
        for start in range(0, width, CHUNK):
            out = arrived_ref[rows, start : start + CHUNK].astype(jnp.float32) + partial_ref[rows, start : start + CHUNK]
            values = [h_ref[rows, j * width + start : j * width + start + CHUNK] for j in range(streams)]
            for i in range(streams):
                mixed = column(coeffs, i * uses + streams + 1) * out
                for j in range(streams):
                    mixed = mixed + column(coeffs, j * uses + 1 + i) * values[j]
                y_ref[rows, i, start : start + CHUNK] = mixed.astype(jnp.bfloat16)
        return carry

    lax.fori_loop(0, h_ref.shape[0] // GROUP, body, 0)


def close_kernel(streams, uses, width, inner, kept, *refs):
    inputs = 12 if inner else 8
    refs = refs[:inputs] + refs[inputs + kept :]
    if inner:
        (h_ref, saved_ref, g_ref, arrived_ref, partial_ref, arrived_f_ref, partial_f_ref, valid_ref, saved_a_ref,
         out_a_ref, wt_ref, param_ref, grad_ref, branch_ref, below_ref, weight_ref, small_ref,
         centre_ref, du_ref, left_ref, dl_ref, cols_ref, sums_ref, parts_ref) = refs
    else:
        (h_ref, saved_ref, g_ref, arrived_ref, partial_ref, branch_in_ref, wt_ref, param_ref,
         grad_ref, weight_ref, small_ref, centre_ref, du_ref, left_ref, dl_ref, cols_ref, sums_ref, parts_ref) = refs
    block = h_ref.shape[0]
    count = streams * uses
    step = pl.program_id(0)
    base = pl.multiple_of(step * block, GROUP)
    all_rows = centre_ref.shape[0] // streams

    @pl.when(step == 0)
    def _():
        sums_ref[...] = jnp.zeros_like(sums_ref)
        weights = wt_ref[...]
        high = weights.astype(jnp.bfloat16).astype(jnp.float32)
        rest = jnp.zeros((LANES - 3 * weights.shape[0], width), jnp.float32)
        parts_ref[...] = jnp.concatenate([high, high, weights - high, rest], axis=0).astype(jnp.bfloat16)

    def read_h(rows, j, start):
        return h_ref[rows, j * width + start : j * width + start + CHUNK].astype(jnp.float32)

    def read_g(rows, i, start):
        values = g_ref[rows, i * width + start : i * width + start + CHUNK].astype(jnp.float32)
        return values * valid_ref[rows, 0:1] if inner else values

    def read_dn(rows, start):
        return arrived_ref[rows, start : start + CHUNK].astype(jnp.float32) + partial_ref[rows, start : start + CHUNK]

    def first_pass(index, carry):
        first = pl.multiple_of(index * GROUP, GROUP)
        rows = pl.ds(first, GROUP)
        saved = saved_ref[rows, :]
        means = [column(saved, 3 * count + j) for j in range(streams)]
        rsqrts = [column(saved, 3 * count + streams + j) for j in range(streams)]
        mean_e = column(saved, 3 * count + 2 * streams)
        rsqrt_e = column(saved, 3 * count + 2 * streams + 1)
        sums = {}

        def add(key, values):
            part = fold(values)
            sums[key] = part if key not in sums else sums[key] + part

        for start in range(0, width, CHUNK):
            dn = read_dn(rows, start)
            values = [read_h(rows, j, start) for j in range(streams)]
            for j in range(streams):
                target = pl.ds(pl.multiple_of(j * all_rows + base + first, GROUP), GROUP)
                centre_ref[target, start : start + CHUNK] = (values[j] - means[j]).astype(jnp.bfloat16)
            entering = column(saved, 0) * values[0]
            for j in range(1, streams):
                entering = entering + column(saved, j * uses) * values[j]
            normed = (entering - mean_e) * rsqrt_e
            add("dn", dn)
            add("dnn", dn * normed)
            for j in range(streams):
                add(("dnh", j), dn * values[j])
                add(("nh", j), normed * values[j])
            if inner:
                out = (
                    arrived_f_ref[rows, start : start + CHUNK].astype(jnp.float32)
                    + partial_f_ref[rows, start : start + CHUNK]
                )
            for i in range(streams):
                g = read_g(rows, i, start)
                for j in range(streams):
                    add(("gh", j, i), g * values[j])
                if inner:
                    add(("go", i), g * out)
        total = {key: row_sum(value) for key, value in sums.items()}
        mean_dn = total["dn"] * (1.0 / width)
        mean_dnn = total["dnn"] * (1.0 / width)
        columns = []
        for j in range(streams):
            columns.append(
                rsqrt_e * (total["dnh", j] - total["dn"] * means[j] - mean_dnn * total["nh", j])
            )
            columns.extend(total["gh", j, i] for i in range(streams))
            columns.append(total["go", j] if inner else branch_in_ref[rows, j : j + 1])
        d_coeffs = place(jnp.zeros((GROUP, LANES), jnp.float32), columns, 0)
        lane = lanes_of(GROUP)
        bent = jnp.where(lane < count, rolled(saved, -count), 0.0)
        projected = jnp.where(lane < count, rolled(saved, -2 * count), 0.0)
        sums_ref[0] += d_coeffs
        sums_ref[1] += d_coeffs * bent
        du = d_coeffs * param_ref[1:2, :] * (1.0 - bent * bent)
        with_mean = du * jnp.where(lane < count, rolled(saved, -(3 * count + 2 * streams + 2)), 0.0) * (1.0 / width)
        with_value = du * projected * (1.0 / width)
        shifts, slopes = [], []
        scaled = jnp.zeros((GROUP, LANES), jnp.float32)
        for j in range(streams):
            inside = (lane >= j * uses) & (lane < (j + 1) * uses)
            slope = rsqrts[j] * rsqrts[j] * row_sum(jnp.where(inside, with_value, 0.0))
            shifts.append(means[j] * slope - rsqrts[j] * row_sum(jnp.where(inside, with_mean, 0.0)))
            slopes.append(slope)
            scaled = jnp.where(inside, du * rsqrts[j], scaled)
        high = scaled.astype(jnp.bfloat16).astype(jnp.float32)
        low = (scaled - high).astype(jnp.bfloat16).astype(jnp.float32)
        for j in range(streams):
            own_high, own_low = rolled(high, -j * uses), rolled(low, -j * uses)
            left = jnp.where(lane < uses, own_high, 0.0)
            left = jnp.where((lane >= 8) & (lane < 8 + uses), rolled(own_low, 8), left)
            left = jnp.where((lane >= 16) & (lane < 16 + uses), rolled(own_high, 16), left)
            left_ref[pl.ds(pl.multiple_of(j * block + first, GROUP), GROUP), :] = left.astype(jnp.bfloat16)
            pair = jnp.where(lane < 8 + uses, left, 0.0)
            du_ref[pl.ds(pl.multiple_of(j * all_rows + base + first, GROUP), GROUP), :] = pair.astype(jnp.bfloat16)
        cols_ref[rows, :] = place(
            jnp.zeros((GROUP, LANES), jnp.float32), [mean_dn, mean_dnn, *shifts, *slopes], 0
        )
        return carry

    lax.fori_loop(0, block // GROUP, first_pass, 0)
    dl_ref[...] = jnp.dot(left_ref[...], parts_ref[...], preferred_element_type=jnp.float32)

    def second_pass(index, carry):
        first = pl.multiple_of(index * GROUP, GROUP)
        rows = pl.ds(first, GROUP)
        saved = saved_ref[rows, :]
        cols = cols_ref[rows, :]
        mean_e = column(saved, 3 * count + 2 * streams)
        rsqrt_e = column(saved, 3 * count + 2 * streams + 1)
        scaled_mean = column(cols, 0) * rsqrt_e
        scaled_slope = column(cols, 1) * rsqrt_e
        branch_sums = [None] * streams
        for start in range(0, width, CHUNK):
            values = [read_h(rows, j, start) for j in range(streams)]
            entering = column(saved, 0) * values[0]
            for j in range(1, streams):
                entering = entering + column(saved, j * uses) * values[j]
            normed = (entering - mean_e) * rsqrt_e
            de = rsqrt_e * read_dn(rows, start) - scaled_mean - normed * scaled_slope
            gs = [read_g(rows, i, start) for i in range(streams)]
            below = None
            for j in range(streams):
                grad = column(saved, j * uses) * de + column(cols, 2 + j)
                grad = grad - values[j] * column(cols, 2 + streams + j)
                grad = grad + dl_ref[pl.ds(pl.multiple_of(j * block + first, GROUP), GROUP), start : start + CHUNK]
                for i in range(streams):
                    grad = grad + column(saved, j * uses + 1 + i) * gs[i]
                if inner:
                    grad_ref[rows, j * width + start : j * width + start + CHUNK] = grad
                else:
                    grad_ref[rows, j, start : start + CHUNK] = grad.astype(jnp.bfloat16)
                if inner:
                    part = fold(grad * out_a_ref[rows, start : start + CHUNK])
                    branch_sums[j] = part if branch_sums[j] is None else branch_sums[j] + part
                    term = saved_a_ref[rows, j * uses + streams + 1 : j * uses + streams + 2] * grad
                    below = term if below is None else below + term
            if inner:
                below_ref[rows, start : start + CHUNK] = below.astype(jnp.bfloat16)
        if inner:
            branch_ref[rows, :] = place(
                jnp.zeros((GROUP, LANES), jnp.float32), [row_sum(one) for one in branch_sums], 0
            )
        return carry

    lax.fori_loop(0, block // GROUP, second_pass, 0)

    @pl.when(step == pl.num_programs(0) - 1)
    def _():
        product = lax.dot_general(
            du_ref[...], centre_ref[...], (((0,), (0,)), ((), ())), preferred_element_type=jnp.float32
        )
        weight_ref[...] = product[: weight_ref.shape[0]]
        small_ref[0:1, :] = jnp.sum(sums_ref[0], axis=0, keepdims=True)
        small_ref[1:2, :] = jnp.sum(sums_ref[1], axis=0, keepdims=True)


def rows_block(rows):
    return min(64, rows)


def specs_for(arrays, block, whole):
    specs = []
    for k, entry in enumerate(arrays):
        array, first = entry if isinstance(entry, tuple) else (entry, 0)
        if k in whole:
            specs.append(pl.BlockSpec(array.shape, lambda i: (0, 0)))
        else:
            specs.append(pl.BlockSpec((block, array.shape[1]), lambda i, first=first // block: (first + i, 0)))
    return specs


def plain(arrays):
    return [entry[0] if isinstance(entry, tuple) else entry for entry in arrays]


def mix_tables(static, weight, scale):
    streams, uses = static.shape
    count = streams * uses
    constants = jnp.stack([static.reshape(count), jnp.tile(scale, streams)])
    return jnp.pad(weight.T, ((0, 8 - uses), (0, 0))), jnp.pad(constants, ((0, 6), (0, LANES - count)))


def open_attention(x, tables, streams, uses):
    rows, width = x.shape[0], x.shape[1] // streams
    block = rows_block(rows)
    arrays = [x, *tables]
    return pl.pallas_call(
        functools.partial(open_attention_kernel, streams, uses, width),
        grid=(rows // block,),
        in_specs=specs_for(arrays, block, {1, 2}),
        out_specs=[pl.BlockSpec((block, width), lambda i: (i, 0)), pl.BlockSpec((block, LANES), lambda i: (i, 0))],
        out_shape=[jax.ShapeDtypeStruct((rows, width), jnp.bfloat16), jax.ShapeDtypeStruct((rows, LANES), jnp.float32)],
        scratch_shapes=[
            pltpu.VMEM((streams * block, LANES), jnp.float32),
            pltpu.VMEM((block, width), jnp.float32),
            pltpu.VMEM((LANES, width), jnp.bfloat16),
            pltpu.VMEM((8, LANES), jnp.float32),
        ],
        compiler_params=PARAMS,
        cost_estimate=cost(),
        name="open_attention",
    )(*plain(arrays))


def open_feedforward(x, saved_a, out_a, g, valid, tables, streams, uses):
    rows, width = x.shape[0], x.shape[1] // streams
    block = rows_block(rows)
    arrays = [x, saved_a, out_a, g, valid, *tables]

    def by_rows(columns):
        return pl.BlockSpec((block, columns), lambda i: (i, 0))

    return pl.pallas_call(
        functools.partial(open_feedforward_kernel, streams, uses, width),
        grid=(rows // block,),
        in_specs=specs_for(arrays, block, {5, 6}),
        out_specs=[by_rows(width), by_rows(width), by_rows(LANES), by_rows(streams * width)],
        out_shape=[
            jax.ShapeDtypeStruct((rows, width), jnp.bfloat16),
            jax.ShapeDtypeStruct((rows, width), jnp.bfloat16),
            jax.ShapeDtypeStruct((rows, LANES), jnp.float32),
            jax.ShapeDtypeStruct((rows, streams * width), jnp.float32),
        ],
        scratch_shapes=[
            pltpu.VMEM((streams * block, width), jnp.bfloat16),
            pltpu.VMEM((streams * block, width), jnp.bfloat16),
            pltpu.VMEM((streams * block, LANES), jnp.float32),
            pltpu.VMEM((block, width), jnp.float32),
            pltpu.VMEM((block, LANES), jnp.float32),
            pltpu.VMEM((LANES, width), jnp.bfloat16),
            pltpu.VMEM((8, LANES), jnp.float32),
        ],
        compiler_params=PARAMS,
        cost_estimate=cost(),
        name="open_feedforward",
    )(*plain(arrays))


def finish(first, h, saved, arrived, partial, streams, uses, filled, tokens=()):
    tokens = waits(tokens)
    rows, width = h.shape[0], h.shape[1] // streams
    block = rows_block(arrived[2])
    arrays = [(h, first), (saved, first), arrived[:2], (partial, first)]
    result, mark = pl.pallas_call(
        functools.partial(finish_kernel, streams, uses, width),
        grid=(arrived[2] // block,),
        in_specs=specs_for(arrays, block, set()) + anywhere(len(filled) + len(tokens)),
        out_specs=[pl.BlockSpec((block, streams, width), lambda i: (first // block + i, 0, 0)), MARK_SPEC],
        out_shape=[jax.ShapeDtypeStruct((rows, streams, width), jnp.bfloat16), MARK_SHAPE],
        input_output_aliases={4 + k: k for k in range(len(filled))},
        compiler_params=PARAMS,
        cost_estimate=cost(),
        name="finish",
    )(*plain(arrays), *filled, *tokens)
    return marked([result], mark)[0]


def close_mix(inner, first, rows, arrays, tables, streams, uses, filled=(), tokens=()):
    tokens = [*filled, *waits(tokens)]
    h = arrays[0][0]
    whole, width = h.shape[0], h.shape[1] // streams
    block = rows_block(rows)
    arrays = [*arrays, *tables]
    last = len(arrays)

    def by_rows(columns):
        return pl.BlockSpec((block, columns), lambda i: (first // block + i, 0))

    def fixed(height, columns):
        return pl.BlockSpec((height, columns), lambda i: (0, 0))

    if inner:
        out_specs = [by_rows(streams * width)]
        out_shape = [jax.ShapeDtypeStruct((whole, streams * width), jnp.float32)]
    else:
        out_specs = [pl.BlockSpec((block, streams, width), lambda i: (i, 0, 0))]
        out_shape = [jax.ShapeDtypeStruct((rows, streams, width), jnp.bfloat16)]
    if inner:
        out_specs += [by_rows(LANES), by_rows(width)]
        out_shape += [
            jax.ShapeDtypeStruct((whole, LANES), jnp.float32),
            jax.ShapeDtypeStruct((whole, width), jnp.bfloat16),
        ]
    out_specs += [fixed(16, width), fixed(8, LANES)]
    out_shape += [jax.ShapeDtypeStruct((16, width), jnp.float32), jax.ShapeDtypeStruct((8, LANES), jnp.float32)]
    return pl.pallas_call(
        functools.partial(close_kernel, streams, uses, width, inner, len(tokens)),
        grid=(rows // block,),
        in_specs=specs_for(arrays, block, {last - 2, last - 1}) + anywhere(len(tokens)),
        out_specs=out_specs,
        out_shape=out_shape,
        scratch_shapes=[
            pltpu.VMEM((streams * rows, width), jnp.bfloat16),
            pltpu.VMEM((streams * rows, LANES), jnp.bfloat16),
            pltpu.VMEM((streams * block, LANES), jnp.bfloat16),
            pltpu.VMEM((streams * block, width), jnp.float32),
            pltpu.VMEM((block, LANES), jnp.float32),
            pltpu.VMEM((2, GROUP, LANES), jnp.float32),
            pltpu.VMEM((LANES, width), jnp.bfloat16),
        ],
        input_output_aliases={len(arrays) + k: k for k in range(len(filled))},
        compiler_params=PARAMS,
        cost_estimate=cost(30 if inner else 0),
        name="close_feedforward" if inner else "close_attention",
    )(*plain(arrays), *tokens)


QUERY_ROWS = 256


def turn(values, cosine, sine):
    return values * cosine + pltpu.roll(values, HEAD_DIM // 2, 1) * sine


def turn_back(values, cosine, sine):
    return values * cosine - pltpu.roll(values, HEAD_DIM // 2, 1) * sine


def block_offset(mine, step, size, rows):
    return pl.multiple_of(lax.rem(mine + size - step, size) * rows, rows)


def allowed_keys(start_ref, first, rows, keys):
    row = first + lax.broadcasted_iota(jnp.int32, (rows, keys), 0)
    key = lax.broadcasted_iota(jnp.int32, (rows, keys), 1)
    return (key <= row) & (key >= start_ref[first : first + rows, 0:1])


def attend_kernel(size, *refs):
    mine_ref, start_ref, cosine_ref, sine_ref = refs[:4]
    raw = [refs[4 + 3 * s : 7 + 3 * s] for s in range(size)]
    q_ref, k_ref, v_ref, out_ref, log_ref, attended_ref = refs[4 + 3 * size :]
    mine = mine_ref[0]
    block = raw[0][0].shape[0]
    total = size * block
    for step in range(size):
        rows = pl.ds(block_offset(mine, step, size, block), block)
        cosine, sine = cosine_ref[rows, :], sine_ref[rows, :]
        q_ref[rows, :] = turn(raw[step][0][...], cosine, sine).astype(jnp.bfloat16)
        k_ref[rows, :] = turn(raw[step][1][...], cosine, sine).astype(jnp.bfloat16)
        v_ref[rows, :] = raw[step][2][...].astype(jnp.bfloat16)
    height = min(QUERY_ROWS, total)
    for first in range(0, total, height):
        keys = first + height
        scores = times_transposed(q_ref[first:keys, :], k_ref[:keys, :]) * HEAD_DIM**-0.5
        scores = jnp.where(allowed_keys(start_ref, first, height, keys), scores, MASKED)
        highest = jnp.max(scores, axis=1, keepdims=True)
        exponent = jnp.exp(scores - highest)
        row_total = jnp.sum(exponent, axis=1, keepdims=True)
        probs = (exponent * (1.0 / row_total)).astype(jnp.bfloat16)
        attended_ref[first:keys, :] = jnp.dot(
            probs, v_ref[:keys, :], preferred_element_type=jnp.float32
        ).astype(jnp.bfloat16)
        log_ref[first:keys, :] = jnp.broadcast_to(highest + jnp.log(row_total), (height, LANES))
    for step in range(size):
        rows = pl.ds(block_offset(mine, step, size, block), block)
        out_ref[step * block : (step + 1) * block, :] = attended_ref[rows, :]


def attend_back_kernel(size, kept, *refs):
    mine_ref, start_ref, cosine_ref, sine_ref, q_ref, k_ref, v_ref, log_ref = refs[:8]
    grads = refs[8 : 8 + size]
    dqkv_ref, d_out_ref, dq_ref, dk_ref, dv_ref = refs[8 + size + kept :]
    mine = mine_ref[0]
    head, heads = pl.program_id(0), pl.num_programs(0)
    block = grads[0].shape[0]
    total = size * block
    for step in range(size):
        d_out_ref[pl.ds(block_offset(mine, step, size, block), block), :] = grads[step][...]
    height = min(QUERY_ROWS, total)
    dk_ref[...] = jnp.zeros_like(dk_ref)
    dv_ref[...] = jnp.zeros_like(dv_ref)
    for first in range(0, total, height):
        keys = first + height
        q, d_out = q_ref[first:keys, :], d_out_ref[first:keys, :]
        k, v = k_ref[:keys, :], v_ref[:keys, :]
        scores = times_transposed(q, k) * HEAD_DIM**-0.5
        probs = jnp.where(
            allowed_keys(start_ref, first, height, keys), jnp.exp(scores - log_ref[first:keys, 0:1]), 0.0
        )
        d_probs = times_transposed(d_out, v)
        centre = jnp.sum(probs * d_probs, axis=1, keepdims=True)
        d_scores = (probs * (d_probs - centre)).astype(jnp.bfloat16)
        dv_ref[:keys, :] += transposed_times(probs.astype(jnp.bfloat16), d_out)
        dk_ref[:keys, :] += transposed_times(d_scores, q)
        dq_ref[first:keys, :] = jnp.dot(d_scores, k, preferred_element_type=jnp.float32)
    for step in range(size):
        rows = pl.ds(block_offset(mine, step, size, block), block)
        cosine, sine = cosine_ref[rows, :], sine_ref[rows, :]
        target = slice(step * block, (step + 1) * block)
        for part, values in enumerate(
            (
                turn_back(dq_ref[rows, :] * HEAD_DIM**-0.5, cosine, sine),
                turn_back(dk_ref[rows, :] * HEAD_DIM**-0.5, cosine, sine),
                dv_ref[rows, :],
            )
        ):
            columns = pl.ds(pl.multiple_of((part * heads + head) * HEAD_DIM, HEAD_DIM), HEAD_DIM)
            dqkv_ref[target, columns] = values.astype(jnp.bfloat16)


def whole_spec(shape):
    return pl.BlockSpec(shape, lambda h: (0,) * len(shape))


def head_spec(rows, first=0):
    return pl.BlockSpec((rows, HEAD_DIM), lambda h: (0, first + h))


def attend(raw_blocks, mine, starts, cosine, sine):
    size, block = len(raw_blocks), raw_blocks[0].shape[0]
    heads = raw_blocks[0].shape[1] // (3 * HEAD_DIM)
    total = size * block
    flat = jax.ShapeDtypeStruct((total, heads * HEAD_DIM), jnp.bfloat16)
    return pl.pallas_call(
        functools.partial(attend_kernel, size),
        grid=(heads,),
        in_specs=[pl.BlockSpec(memory_space=pltpu.SMEM)]
        + [whole_spec(a.shape) for a in (starts, cosine, sine)]
        + [head_spec(block, part * heads) for _ in range(size) for part in range(3)],
        out_specs=[head_spec(total)] * 5,
        out_shape=[flat] * 4 + [jax.ShapeDtypeStruct(flat.shape, jnp.float32)],
        scratch_shapes=[pltpu.VMEM((total, HEAD_DIM), jnp.bfloat16)],
        compiler_params=PARAMS,
        cost_estimate=cost(),
        name="attend",
    )(mine, starts, cosine, sine, *[raw for raw in raw_blocks for _ in range(3)])


def attend_back(heads_kept, grad_blocks, mine, starts, cosine, sine, tokens):
    tokens = waits(tokens)
    size, block = len(grad_blocks), grad_blocks[0].shape[0]
    total, columns = heads_kept[0].shape
    heads = columns // HEAD_DIM
    return pl.pallas_call(
        functools.partial(attend_back_kernel, size, len(tokens)),
        grid=(heads,),
        in_specs=[pl.BlockSpec(memory_space=pltpu.SMEM)]
        + [whole_spec(a.shape) for a in (starts, cosine, sine)]
        + [head_spec(total)] * 4
        + [head_spec(block)] * size
        + anywhere(len(tokens)),
        out_specs=whole_spec((total, 3 * columns)),
        out_shape=jax.ShapeDtypeStruct((total, 3 * columns), jnp.bfloat16),
        scratch_shapes=[pltpu.VMEM((total, HEAD_DIM), jnp.bfloat16)] + [pltpu.VMEM((total, HEAD_DIM), jnp.float32)] * 3,
        compiler_params=PARAMS,
        cost_estimate=cost(),
        name="attend_back",
    )(mine, starts, cosine, sine, *heads_kept, *grad_blocks, *tokens)


UNIT_TILE = 512


def forward_units_kernel(blocks, kept, *refs):
    gate_w_ref, up_w_ref = refs[blocks : blocks + 2]
    gate_ref, up_ref, rows_ref, hidden_ref, mark_ref = refs[blocks + 2 + kept :]
    mark_ref[...] = jnp.zeros_like(mark_ref)
    x = jnp.concatenate([ref[...] for ref in refs[:blocks]], axis=0)
    gate, up = matmul(x, gate_w_ref[...]), matmul(x, up_w_ref[...])
    gate_ref[...] = gate
    up_ref[...] = up
    hidden_ref[...] = (gate / (1.0 + jnp.exp(-gate)) * up).astype(jnp.bfloat16)

    @pl.when(pl.program_id(0) == 0)
    def _():
        rows_ref[...] = x


def backward_units_kernel(kept, *refs):
    first_ref, second_ref, gate_ref, up_ref, down_w_ref, gate_w_ref, up_w_ref = refs[:7]
    partial_ref, rows_ref, d_gate_ref, d_up_ref, mark_ref = refs[7 + kept :]
    mark_ref[...] = jnp.zeros_like(mark_ref)
    d_out = jnp.concatenate([first_ref[...], second_ref[...]], axis=0)
    d_hidden = matmul(d_out, down_w_ref[...])
    gate = gate_ref[...]
    sigmoid = 1.0 / (1.0 + jnp.exp(-gate))
    d_gate = (d_hidden * up_ref[...] * (sigmoid + gate * sigmoid * (1.0 - sigmoid))).astype(jnp.bfloat16)
    d_up = (d_hidden * gate * sigmoid).astype(jnp.bfloat16)
    d_gate_ref[...] = d_gate
    d_up_ref[...] = d_up
    part = times_transposed(d_gate, gate_w_ref[...]) + times_transposed(d_up, up_w_ref[...])

    @pl.when(pl.program_id(0) == 0)
    def _():
        partial_ref[...] = part
        rows_ref[...] = d_out

    @pl.when(pl.program_id(0) > 0)
    def _():
        partial_ref[...] += part


def forward_units(pair, size, blocks, gate_up, filled, tokens=()):
    tokens = waits(tokens)
    each, width = blocks[0].shape
    count = len(blocks)
    rows = each * count // 2
    units = gate_up.shape[1] // 2
    tile = min(UNIT_TILE, units)
    tiles = units // tile
    weight = functools.partial(pl.BlockSpec, (width, tile))
    outs = pl.pallas_call(
        functools.partial(forward_units_kernel, count, len(filled) + len(tokens)),
        grid=(tiles,),
        in_specs=[pl.BlockSpec((each, width), lambda i: (0, 0))] * count
        + [weight(lambda i: (0, i)), weight(lambda i: (0, tiles + i))]
        + anywhere(len(filled) + len(tokens)),
        out_specs=[
            pl.BlockSpec((2 * rows, tile), lambda i: (0, i)),
            pl.BlockSpec((2 * rows, tile), lambda i: (0, i)),
            pl.BlockSpec((2 * rows, width), lambda i: (pair, 0)),
            pl.BlockSpec((2 * rows, tile), lambda i: (pair, i)),
            MARK_SPEC,
        ],
        out_shape=[
            jax.ShapeDtypeStruct((2 * rows, units), jnp.float32),
            jax.ShapeDtypeStruct((2 * rows, units), jnp.float32),
            jax.ShapeDtypeStruct((size * rows, width), jnp.bfloat16),
            jax.ShapeDtypeStruct((size * rows, units), jnp.bfloat16),
            MARK_SHAPE,
        ],
        input_output_aliases={count + 2 + k: 2 + k for k in range(len(filled))},
        compiler_params=PARAMS,
        cost_estimate=cost(),
        name="forward_units",
    )(*blocks, gate_up, gate_up, *filled, *tokens)
    outs = marked(outs[:-1], outs[-1])
    return outs[0], outs[1], outs[2:]


def backward_units(pair, size, blocks, gate, up, gate_up, down, filled, tokens=()):
    tokens = waits(tokens)
    rows, width = blocks[0].shape
    units = down.shape[1]
    tile = min(UNIT_TILE, units)
    tiles = units // tile
    weight = functools.partial(pl.BlockSpec, (width, tile))
    by_tile = pl.BlockSpec((2 * rows, tile), lambda i: (0, i))
    outs = pl.pallas_call(
        functools.partial(backward_units_kernel, len(filled) + len(tokens)),
        grid=(tiles,),
        in_specs=[pl.BlockSpec((rows, width), lambda i: (0, 0))] * 2
        + [by_tile, by_tile]
        + [weight(lambda i: (0, i)), weight(lambda i: (0, i)), weight(lambda i: (0, tiles + i))]
        + anywhere(len(filled) + len(tokens)),
        out_specs=[
            pl.BlockSpec((2 * rows, width), lambda i: (0, 0)),
            pl.BlockSpec((2 * rows, width), lambda i: (pair, 0)),
            pl.BlockSpec((2 * rows, tile), lambda i: (pair, i)),
            pl.BlockSpec((2 * rows, tile), lambda i: (pair, i)),
            MARK_SPEC,
        ],
        out_shape=[
            jax.ShapeDtypeStruct((2 * rows, width), jnp.float32),
            jax.ShapeDtypeStruct((size * rows, width), jnp.bfloat16),
            jax.ShapeDtypeStruct((size * rows, units), jnp.bfloat16),
            jax.ShapeDtypeStruct((size * rows, units), jnp.bfloat16),
            MARK_SHAPE,
        ],
        input_output_aliases={7 + k: 1 + k for k in range(len(filled))},
        compiler_params=PARAMS,
        cost_estimate=cost(),
        name="backward_units",
    )(*blocks, gate, up, down, gate_up, gate_up, *filled, *tokens)
    outs = marked(outs[:-1], outs[-1])
    return outs[0], outs[1:]


def assemble_kernel(count, pieces, kept, table_ref, *refs):
    sources, outs, mark_ref = refs[:count], refs[count + kept : -1], refs[-1]
    mark_ref[...] = jnp.zeros_like(mark_ref)
    for k in range(count):

        @pl.when(pl.program_id(0) // pieces == k)
        def _(k=k):
            first = 0
            for out_ref in outs:
                columns = out_ref.shape[1]
                out_ref[...] = sources[k][:, first : first + columns].astype(jnp.float32)
                first += columns


def assemble(arrays, widths, table, tokens=()):
    tokens = waits(tokens)
    count = len(arrays)
    pieces = arrays[0][2]
    rows, columns = arrays[0][3], arrays[0][0].shape[1]
    *results, mark = pl.pallas_call(
        functools.partial(assemble_kernel, count, pieces, len(tokens)),
        grid_spec=pltpu.PrefetchScalarGridSpec(
            num_scalar_prefetch=1,
            grid=(count * pieces,),
            in_specs=[
                pl.BlockSpec(
                    (rows, columns),
                    lambda i, t, k=k, first=first: (first + jnp.clip(i - k * pieces, 0, pieces - 1), 0),
                )
                for k, (_, first, _, _) in enumerate(arrays)
            ]
            + anywhere(len(tokens)),
            out_specs=[pl.BlockSpec((rows, width), lambda i, t: (t[i], 0)) for width in widths] + [MARK_SPEC],
        ),
        out_shape=[jax.ShapeDtypeStruct((count * pieces * rows, width), jnp.float32) for width in widths] + [MARK_SHAPE],
        compiler_params=PARAMS,
        cost_estimate=cost(),
        name="assemble",
    )(table, *(array for array, *_ in arrays), *tokens)
    return marked(results, mark)


PRODUCT_TILE = 1024


def across_of(width, first):
    if width <= 2 * PRODUCT_TILE and first % width == 0:
        return width if width * 3 <= 5 * PRODUCT_TILE else width // 2
    return math.gcd(PRODUCT_TILE, width, first or width)


def joined_left(refs):
    left = [ref[...] for ref in refs]
    return left[0] if len(left) == 1 else jnp.concatenate(left, axis=0)


def away_kernel(blocks, core_ref, *refs):
    refs[-1][...] = jnp.zeros_like(refs[-1])
    refs[-2][...] = transposed_times(joined_left(refs[:blocks]), refs[blocks][...]).astype(jnp.bfloat16)


def own_kernel(blocks, scalars_ref, *refs):
    away_ref, kept_ref, mark_ref = refs[-3:]
    mark_ref[...] = jnp.zeros_like(mark_ref)
    product = transposed_times(joined_left(refs[:blocks]), refs[blocks][...])
    product = product + refs[blocks + 1][...].astype(jnp.float32)

    @pl.when(pl.program_id(0) == 0)
    def _():
        away_ref[...] = product.astype(jnp.bfloat16)

    @pl.when(pl.program_id(0) == 1)
    def _():
        kept_ref[...] = product


def away_product(core, left, right, columns, first, filled, tokens=()):
    tokens = waits(tokens)
    half = left[0].shape[1] // 2
    rows, width = right.shape
    down, across = min(PRODUCT_TILE, half), across_of(width, first)
    high, offset = half // down, first // across
    result, mark = pl.pallas_call(
        functools.partial(away_kernel, len(left)),
        grid_spec=pltpu.PrefetchScalarGridSpec(
            num_scalar_prefetch=1,
            grid=(high, width // across),
            in_specs=[
                pl.BlockSpec((block.shape[0], down), lambda i, j, c: (0, (1 - c[0]) * high + i)) for block in left
            ]
            + [pl.BlockSpec((rows, across), lambda i, j, c: (0, j))]
            + anywhere(len(filled) + len(tokens)),
            out_specs=[pl.BlockSpec((down, across), lambda i, j, c: (i, offset + j)), MARK_SPEC],
        ),
        out_shape=[jax.ShapeDtypeStruct((half, columns), jnp.bfloat16), MARK_SHAPE],
        input_output_aliases={2 + len(left): 0} if filled else {},
        compiler_params=PARAMS,
        cost_estimate=cost(),
        name="away_product",
    )(core, *left, right, *filled, *tokens)
    return marked([result], mark)[0]


def own_product(scalars, left, right, arrived, columns, first, rows_first, rows_here, filled, tokens=()):
    tokens = waits(tokens)
    half = left[0].shape[1] // 2
    rows, width = right.shape
    cut = rows_here // 2
    down, across = min(PRODUCT_TILE, cut), across_of(width, first)
    high, wide, offset = cut // down, width // across, first // across

    def row(g, i, c):
        return rows_first // down + jnp.where(g == 0, 1 - c[1], c[1]) * high + i

    *results, mark = pl.pallas_call(
        functools.partial(own_kernel, len(left)),
        grid_spec=pltpu.PrefetchScalarGridSpec(
            num_scalar_prefetch=1,
            grid=(2, high, wide),
            in_specs=[
                pl.BlockSpec((block.shape[0], down), lambda g, i, j, c: (0, c[0] * (half // down) + row(g, i, c)))
                for block in left
            ]
            + [
                pl.BlockSpec((rows, across), lambda g, i, j, c: (0, j)),
                pl.BlockSpec((down, across), lambda g, i, j, c: (row(g, i, c), offset + j)),
            ]
            + anywhere(len(filled) + len(tokens)),
            out_specs=[
                pl.BlockSpec(
                    (down, across),
                    lambda g, i, j, c: (jnp.where(g == 0, i, high - 1), offset + jnp.where(g == 0, j, wide - 1)),
                ),
                pl.BlockSpec(
                    (down, across),
                    lambda g, i, j, c: (jnp.where(g == 0, 0, i), offset + jnp.where(g == 0, 0, j)),
                ),
                MARK_SPEC,
            ],
        ),
        out_shape=[
            jax.ShapeDtypeStruct((cut, columns), jnp.bfloat16),
            jax.ShapeDtypeStruct((cut, columns), jnp.float32),
            MARK_SHAPE,
        ],
        input_output_aliases={3 + len(left) + k: k for k in range(len(filled))},
        compiler_params=PARAMS,
        cost_estimate=cost(),
        name="own_product",
    )(scalars, *left, right, arrived, *filled, *tokens)
    return marked(results, mark)


def backproject_kernel(d_ref, w_ref, *refs):
    refs[-1][...] = jnp.zeros_like(refs[-1])
    refs[-2][...] = times_transposed(d_ref[...], w_ref[...]).astype(refs[-2].dtype)


def backproject(rows_of, first, count, weight, kind, tokens=()):
    tokens = waits(tokens)
    array, rows = rows_of
    width, columns = weight.shape
    across = min(512, width)
    result, mark = pl.pallas_call(
        backproject_kernel,
        grid=(width // across, count),
        in_specs=[
            pl.BlockSpec((rows, columns), lambda j, i: (first + i, 0)),
            pl.BlockSpec((across, columns), lambda j, i: (j, 0)),
        ]
        + anywhere(len(tokens)),
        out_specs=[pl.BlockSpec((rows, across), lambda j, i: (i, j)), MARK_SPEC],
        out_shape=[jax.ShapeDtypeStruct((count * rows, width), kind), MARK_SHAPE],
        compiler_params=PARAMS,
        cost_estimate=cost(),
        name="backproject",
    )(array, weight, *tokens)
    return marked([result], mark)[0]


def project_kernel(count, *refs):
    refs[-1][...] = matmul(jnp.concatenate([ref[...] for ref in refs[:count]], axis=0), refs[count][...]).astype(jnp.bfloat16)


def project(blocks, weight, columns):
    rows, width = blocks[0].shape
    across = min(256, columns)
    return pl.pallas_call(
        functools.partial(project_kernel, len(blocks)),
        grid=(columns // across,),
        in_specs=[pl.BlockSpec((rows, width), lambda j: (0, 0))] * len(blocks)
        + [pl.BlockSpec((width, across), lambda j: (0, j))],
        out_specs=pl.BlockSpec((len(blocks) * rows, across), lambda j: (0, j)),
        out_shape=jax.ShapeDtypeStruct((len(blocks) * rows, columns), jnp.bfloat16),
        compiler_params=PARAMS,
        cost_estimate=cost(),
        name="project",
    )(*blocks, weight)


def out_project_kernel(count, *refs):
    refs[-1][...] = times_transposed(jnp.concatenate([ref[...] for ref in refs[:count]], axis=1), refs[count][...])


def out_project(blocks, weight):
    rows = blocks[0].shape[0]
    width, columns = weight.shape
    across = min(512, width)
    return pl.pallas_call(
        functools.partial(out_project_kernel, len(blocks)),
        grid=(width // across,),
        in_specs=[pl.BlockSpec(block.shape, lambda j: (0, 0)) for block in blocks]
        + [pl.BlockSpec((across, columns), lambda j: (j, 0))],
        out_specs=pl.BlockSpec((rows, across), lambda j: (0, j)),
        out_shape=jax.ShapeDtypeStruct((rows, width), jnp.float32),
        compiler_params=PARAMS,
        cost_estimate=cost(),
        name="out_project",
    )(*blocks, weight)


SUM_ROWS = 256


def halve_kernel(which_ref, own_ref, arrived_ref, *refs):
    away_ref, kept_ref, mark_ref = refs[-3:]
    mark_ref[...] = jnp.zeros_like(mark_ref)
    total = own_ref[...] + arrived_ref[...].astype(jnp.float32)

    @pl.when(pl.program_id(0) == 0)
    def _():
        away_ref[...] = total.astype(jnp.bfloat16)

    @pl.when(pl.program_id(0) == 1)
    def _():
        kept_ref[...] = total


def halve(own, arrived, which, tokens=()):
    tokens = waits(tokens)
    (own, own_first, rows), (arrived, arrived_first, _) = own, arrived
    half, columns = rows // 2, own.shape[1]
    tile = min(SUM_ROWS, half)
    tiles = half // tile

    def source(first):
        return pl.BlockSpec(
            (tile, columns), lambda g, t, w: (first // tile + jnp.where(g == 0, 1 - w[0], w[0]) * tiles + t, 0)
        )

    *results, mark = pl.pallas_call(
        halve_kernel,
        grid_spec=pltpu.PrefetchScalarGridSpec(
            num_scalar_prefetch=1,
            grid=(2, tiles),
            in_specs=[source(own_first), source(arrived_first)] + anywhere(len(tokens)),
            out_specs=[
                pl.BlockSpec((tile, columns), lambda g, t, w: (jnp.where(g == 0, t, tiles - 1), 0)),
                pl.BlockSpec((tile, columns), lambda g, t, w: (jnp.where(g == 0, 0, t), 0)),
                MARK_SPEC,
            ],
        ),
        out_shape=[
            jax.ShapeDtypeStruct((half, columns), jnp.bfloat16),
            jax.ShapeDtypeStruct((half, columns), jnp.float32),
            MARK_SHAPE,
        ],
        compiler_params=PARAMS,
        cost_estimate=cost(),
        name="halve",
    )(which, own, arrived, *tokens)
    return marked(results, mark)


def add_kernel(own, arrives, *refs):
    out_ref, mark_ref = refs[-2:]
    mark_ref[...] = jnp.zeros_like(mark_ref)
    rows = out_ref.shape[0] // own
    for k in range(own):
        values = refs[k][...].astype(jnp.float32)
        if arrives:
            values = values + refs[own + k][...].astype(jnp.float32)
        out_ref[k * rows : (k + 1) * rows, :] = values.astype(out_ref.dtype)


def add_low(own, arrived=(), tokens=(), kind=jnp.bfloat16):
    tokens = waits(tokens)
    rows, columns = own[0][2], own[0][0].shape[1]
    across = min(512, columns)
    total = rows * len(own)
    ranges = [*own, *arrived]
    result, mark = pl.pallas_call(
        functools.partial(add_kernel, len(own), bool(arrived)),
        grid=(columns // across,),
        in_specs=[
            pl.BlockSpec((rows, across), lambda j, first=first // rows: (first, j)) for _, first, rows in ranges
        ]
        + anywhere(len(tokens)),
        out_specs=[pl.BlockSpec((total, across), lambda j: (0, j)), MARK_SPEC],
        out_shape=[jax.ShapeDtypeStruct((total, columns), kind), MARK_SHAPE],
        compiler_params=PARAMS,
        cost_estimate=cost(),
        name="add_low",
    )(*(array for array, _, _ in ranges), *tokens)
    return marked([result], mark)[0]


def whole_range(array):
    return (array, 0, array.shape[0])


def join_kernel(count, tiles, *refs):
    out_ref, mark_ref = refs[-2:]
    mark_ref[...] = jnp.zeros_like(mark_ref)
    for k in range(count):

        @pl.when(pl.program_id(0) // tiles == k)
        def _(k=k):
            out_ref[...] = refs[k][...]


def join(arrays, tokens=()):
    tokens = waits(tokens)
    rows, columns = arrays[0].shape
    tile = min(2 * SUM_ROWS, rows)
    tiles = rows // tile
    result, mark = pl.pallas_call(
        functools.partial(join_kernel, len(arrays), tiles),
        grid=(len(arrays) * tiles,),
        in_specs=[
            pl.BlockSpec((tile, columns), lambda i, k=k: (jnp.clip(i - k * tiles, 0, tiles - 1), 0))
            for k in range(len(arrays))
        ]
        + anywhere(len(tokens)),
        out_specs=[pl.BlockSpec((tile, columns), lambda i: (i, 0)), MARK_SPEC],
        out_shape=[jax.ShapeDtypeStruct((len(arrays) * rows, columns), arrays[0].dtype), MARK_SHAPE],
        compiler_params=PARAMS,
        cost_estimate=cost(),
        name="join",
    )(*arrays, *tokens)
    return marked([result], mark)[0]


def ring_shift(block):
    size = lax.axis_size("tensor")
    return lax.ppermute(block, "tensor", [(i, (i + 1) % size) for i in range(size)])


def ring_gather(block):
    blocks = [block]
    for _ in range(lax.axis_size("tensor") - 1):
        blocks.append(ring_shift(blocks[-1]))
    return blocks


def row_halves(ranges):
    return [
        [(array, first + k * (rows // 2), rows // 2) for array, first, rows in ranges] for k in range(2)
    ]


def ring_sums(step, size, ranges, arrived, tokens):
    if step < size - 1:
        return [add_low(ranges, arrived, tokens)]
    arrived = row_halves(arrived) if arrived else ((), ())
    return [add_low(own, other, tokens) for own, other in zip(row_halves(ranges), arrived)]


def own_columns(attended):
    blocks = jnp.split(attended, lax.axis_size("tensor"))
    size = len(blocks)
    return [blocks[0]] + [
        lax.ppermute(blocks[size - step], "tensor", [(i, (i + step) % size) for i in range(size)])
        for step in range(1, size)
    ]


def swap(values, axis, bit):
    return lax.ppermute(values, axis, [(i, i ^ (1 << bit)) for i in range(lax.axis_size(axis))])


def bit_of(axis, bit):
    return (lax.axis_index(axis) >> bit) & 1


def axis_orders():
    bits = (lax.axis_size("dp") - 1).bit_length()
    return list(range(1, bits)), list(range(bits - 1, 0, -1))


class Butterfly:
    def __init__(self, halved, orders):
        self.orders, self.level, self.levels = orders, 0, len(orders[0])
        self.ready, self.kept = [away for away, _ in halved], [kept for _, kept in halved]

    def step(self, *after):
        level, levels = self.level, self.levels
        if level == 2 * levels:
            return self
        bits = [order[level] if level < levels else order[2 * levels - 1 - level] for order in self.orders]
        arrived = [swap(away, "dp", bit) for away, bit in zip(self.ready, bits)]
        self.level += 1
        if self.level < levels:
            halved = [
                halve(
                    (kept, 0, kept.shape[0]),
                    (other, 0, kept.shape[0]),
                    jnp.full((1,), bit_of("dp", order[self.level]), jnp.int32),
                    after,
                )
                for kept, other, order in zip(self.kept, arrived, self.orders)
            ]
            self.ready, self.kept = [away for away, _ in halved], [kept for _, kept in halved]
        elif self.level == levels:
            self.ready = [
                add_low([whole_range(kept)], [whole_range(other)], after) for kept, other in zip(self.kept, arrived)
            ]
        elif self.level < 2 * levels:
            self.ready = [join(both, after) for both in zip(self.ready, arrived)]
        else:
            self.ready = [join([array for both in zip(self.ready, arrived) for array in both], after)]
        return self

    def gathered(self, *after):
        while self.level < 2 * self.levels:
            self.step(*after)
        return self.ready[0]


def own_scalars(order):
    return jnp.stack([bit_of("dp", 0), bit_of("dp", order[0])]).astype(jnp.int32)


def pieces_of(joined, parts, part=None):
    count = parts << ((lax.axis_size("dp") - 1).bit_length() - 1)
    rows = joined.shape[0] // count
    each = count // parts
    return [
        (half, 0, count, rows) if part is None else (half, part * each, each, rows)
        for half in (joined, swap(joined, "dp", 0))
    ]


class SumEverywhere:
    def __init__(self, values):
        self.values = values
        self.left = [
            (axis, bit) for axis in ("tensor", "dp") for bit in range((lax.axis_size(axis) - 1).bit_length())
        ]

    def step(self, *after):
        axis, bit = self.left.pop(0)
        arrived = swap(self.values, axis, bit)
        self.values = add_low([whole_range(self.values)], [whole_range(arrived)], after, jnp.float32)
        return self.values

    def finished(self, last):
        while len(self.left) > last:
            self.step()
        return self.values


def piece_rows(orders):
    levels = len(orders[0])
    entries = []
    for flip in (0, 1):
        core = bit_of("dp", 0) ^ flip
        for k, order in enumerate(orders):
            for position in range(1 << levels):
                row = jnp.int32(0)
                for level, bit in enumerate(order):
                    digit = (position >> (levels - 1 - level)) & 1
                    row = row * 2 + (bit_of("dp", bit) ^ digit)
                entries.append((core * len(orders) + k) * (1 << levels) + row)
    return jnp.stack(entries).astype(jnp.int32)


def segments_from(slot_lengths, group_rows):
    bounds = jnp.cumsum(slot_lengths)
    row_ids = jnp.arange(group_rows, dtype=jnp.int32)
    segment = jnp.sum((row_ids[:, None] >= bounds[None, :]).astype(jnp.int32), axis=1)
    starting = jnp.concatenate([jnp.zeros((1,), jnp.int32), bounds])
    labels = jnp.arange(starting.shape[0], dtype=jnp.int32)
    begins = jnp.sum(jnp.where(segment[:, None] == labels[None, :], starting[None, :], 0), axis=1)
    return (segment, begins)


def group_layout(lengths, permutation, group_rows, seq_count):
    group_index = lax.axis_index("dp")
    chosen = lax.dynamic_slice_in_dim(permutation, group_index * seq_count, seq_count)
    matches = chosen[:, None] == jnp.arange(permutation.shape[0], dtype=jnp.int32)[None, :]
    slot_lengths = jnp.sum(jnp.where(matches, lengths[None, :], 0), axis=1)
    return segments_from(slot_lengths, group_rows)


def rope_tables(position):
    halfway = HEAD_DIM // 2
    frequency = THETA ** (-(2.0 * jnp.arange(halfway, dtype=jnp.float32)) / HEAD_DIM)
    angles = position.astype(jnp.float32)[:, None] * frequency[None, :]
    cosine, sine = jnp.cos(angles), jnp.sin(angles)
    return jnp.concatenate([cosine, cosine], axis=1), jnp.concatenate([-sine, sine], axis=1)


def gather_rows(*weights):
    return lax.all_gather(jnp.concatenate(weights, axis=1), "dp", axis=0, tiled=True)


def per_device(
    streams,
    cotangent,
    lengths,
    permutation,
    query_weight,
    key_weight,
    value_weight,
    out_weight,
    gate_weight,
    up_weight,
    down_weight,
    mix_static,
    mix_weight,
    mix_scale,
):
    MARKS.clear()
    qkv_full = gather_rows(query_weight, key_weight, value_weight)
    gate_up_full = gather_rows(gate_weight, up_weight)
    down_full = gather_rows(down_weight)
    local_rows, count, width = streams.shape
    uses = mix_static.shape[2]
    sizes = (count, uses)
    size = lax.axis_size("tensor")
    group_rows = local_rows * size
    mine = lax.axis_index("tensor")
    place_index = jnp.full((1,), mine, jnp.int32)
    core = jnp.full((1,), bit_of("dp", 0), jnp.int32)
    units = gate_weight.shape[1]
    seq_count = permutation.shape[0] // lax.axis_size("dp")

    inputs = streams.reshape(local_rows, count * width)
    cotangents = cotangent.reshape(local_rows, count * width)
    tables_a = mix_tables(mix_static[0], mix_weight[0], mix_scale[0])
    tables_f = mix_tables(mix_static[1], mix_weight[1], mix_scale[1])
    segment, begins = group_layout(lengths, permutation, group_rows, seq_count)
    cosine, sine = rope_tables(jnp.arange(group_rows, dtype=jnp.int32) - begins)
    starts = jnp.broadcast_to(begins[:, None], (group_rows, LANES))
    local_segment = lax.dynamic_slice_in_dim(segment, mine * local_rows, local_rows)
    valid = jnp.broadcast_to((local_segment < seq_count).astype(jnp.float32)[:, None], (local_rows, LANES))

    others = [
        lax.ppermute(out_weight, "tensor", [(i, (i + step) % size) for i in range(size)]) for step in range(1, size)
    ]
    normed_a, saved_a = open_attention(inputs, tables_a, *sizes)
    out_full = gather_rows(out_weight, *hold(others, normed_a))
    input_blocks = ring_gather(normed_a)
    query, key, value, attended, log_totals = attend(
        [matmul(block, qkv_full) for block in input_blocks], place_index, starts, cosine, sine
    )
    out_a = out_project(own_columns(attended), out_full)
    half_rows = local_rows // 2
    normed_f, d_out_f, saved_f, middle = open_feedforward(
        inputs, saved_a, out_a, cotangents, valid, tables_f, *sizes
    )
    orders = axis_orders()
    steps = 2 * len(orders[0])
    whole_table, half_tables = piece_rows(orders), [piece_rows([order]) for order in orders]

    def pair_of(arrays, pair):
        return arrays[2 * pair : 2 * pair + 2]

    blocks, gates, ups, filled = [normed_f], [], [], []

    def forward(pair, filled):
        gate, up, filled = forward_units(pair, size, pair_of(blocks, pair), gate_up_full, filled)
        gates.append(gate)
        ups.append(up)
        return filled

    for step in range(1, size):
        blocks.append(ring_shift(blocks[-1]))
        if step % 2 == 0:
            filled = forward(step // 2 - 1, filled)
    last_pair = size // 2 - 1
    grads, partials_n, filled_back = list(hold([d_out_f], blocks[-1], *gates)), [], []
    for step in range(1, size):
        arrived = ring_shift(grads[-1])
        if step == 1:
            filled = forward(last_pair, filled)
            (arrived,) = hold([arrived], gates[-1])
        elif step % 2 == 0:
            pair = step // 2 - 1
            partial, filled_back = backward_units(
                pair, size, pair_of(grads, pair), gates[pair], ups[pair], gate_up_full, down_full, filled_back
            )
            partials_n.append(partial)
            (arrived,) = hold([arrived], partial)
        grads.append(arrived)
    feedforward_rows, hidden_rows = filled
    partials_f = backproject((hidden_rows, local_rows), 0, size, down_full, jnp.float32, partials_n)

    def both_parts(index):
        first = (index % 2) * local_rows
        return [(partials_f, index * local_rows, local_rows), (partials_n[index // 2], first, local_rows)]

    half = width // 2
    totals = ring_sums(1, size, both_parts(1), (), [grads[-1]])
    for step in range(2, size + 1):
        arrived, total = [ring_shift(one) for one in totals], totals[0]
        tokens = []
        if step == 2:
            partial, filled_back = backward_units(
                last_pair,
                size,
                pair_of(grads, last_pair),
                gates[last_pair],
                ups[last_pair],
                gate_up_full,
                down_full,
                filled_back,
                [total],
            )
            partials_n.append(partial)
            grad_rows, *unit_rows = filled_back
            aways = [away_product(core, [feedforward_rows], rows, units, 0, []) for rows in unit_rows]
            tokens = aways
        elif step == 3:
            others = [swap(away, "dp", 0) for away in hold(aways, total)]
            down_away = away_product(core, [grad_rows], hidden_rows, units, 0, [], [total])
            gate_up_sum = Butterfly(
                [
                    own_product(own_scalars(order), [feedforward_rows], rows, other, units, 0, 0, half, [], [down_away])
                    for order, rows, other in zip(orders, unit_rows, others)
                ],
                orders,
            )
            tokens = [*gate_up_sum.ready, down_away]
        elif step == 4:
            down_other = swap(*hold([down_away], total), "dp", 0)
            down_sum = Butterfly(
                [
                    own_product(
                        own_scalars(order), [grad_rows], hidden_rows, down_other, units, 0, k * half // 2, half // 2, [], [total]
                    )
                    for k, order in enumerate(orders)
                ],
                orders,
            )
            tokens = down_sum.ready
        if step < size:
            here = [(arrived[0], 0, local_rows), (arrived[0], local_rows, local_rows)]
            totals = ring_sums(step, size, both_parts(step), here, tokens)
    filled, sums_f = [], []
    for k, both in enumerate(arrived):
        first = k * half_rows
        own_f, own_n = (partials_f, first), (partials_n[0], first)
        rest = [(a, first) for a in (valid, saved_a, out_a)]
        arrays = [(a, first) for a in (middle, saved_f, cotangents)]
        *filled, weight_sum, small = close_mix(
            True,
            first,
            half_rows,
            [*arrays, (both, half_rows), own_n, (both, 0), own_f, *rest],
            tables_f,
            *sizes,
            filled,
            tokens,
        )
        sums_f.append((weight_sum, small))
        tokens = []
    middle_grad, d_branch_a, d_out_a = filled

    def finished(tokens):
        filled = []
        for k, both in enumerate(arrived_last):
            filled = [finish(k * half_rows, middle, saved_f, (both, 0, half_rows), partials_f, *sizes, filled, tokens)]
        return filled[0]

    arrived_last = arrived

    output_grads = [d_out_a]
    for step in range(1, size):
        arrived = ring_shift(output_grads[-1])
        after = output_grads[-1]
        tokens = []
        if step == 1:
            tokens = [*gate_up_sum.step(after).ready, *down_sum.step(after).ready]
        elif step == 2:
            out_streams = finished(gate_up_sum.step(after).ready)
            tokens = [*gate_up_sum.ready, out_streams]
        if tokens:
            (arrived,) = hold([arrived], *tokens)
        output_grads.append(arrived)
        if step == 3:
            tokens = gate_up_sum.step(after).ready
    attended_grads = [project([block], out_full, attended.shape[1]) for block in output_grads]
    output_rows = output_grads
    d_qkv = attend_back(
        [query, key, value, log_totals], attended_grads, place_index, starts, cosine, sine, tokens
    )
    total = backproject((d_qkv, local_rows), 1, 1, qkv_full, jnp.bfloat16)
    columns = attended.shape[1]
    for step in range(2, size + 1):
        arrived = ring_shift(total)
        tokens = []
        if step == 2:
            away = away_product(core, input_blocks, d_qkv, 4 * columns, 0, [], [total])
            away = away_product(core, output_rows, attended, 4 * columns, 3 * columns, [away])
            own_partials = [backproject((d_qkv, local_rows), 2, 1, qkv_full, jnp.float32, [away])]
            gate_up_joined = gate_up_sum.gathered(*own_partials)
            tokens = [away, gate_up_joined, *down_sum.step(*own_partials).ready]
        elif step == 3:
            (away,) = hold([away], total)
            other = swap(away, "dp", 0)
            own_partials.append(backproject((d_qkv, local_rows), 3 % size, size - 3, qkv_full, jnp.float32, [total]))
            halved = []
            for k, order in enumerate(orders):
                place = (4 * columns, 0, k * half // 2, half // 2)
                scalars = own_scalars(order)
                both = own_product(scalars, input_blocks, d_qkv, other, *place, [], [own_partials[-1]])
                place = (4 * columns, 3 * columns, k * half // 2, half // 2)
                halved.append(own_product(scalars, output_rows, attended, other, *place, both))
            attention_sum = Butterfly(halved, orders)
            tokens = [*attention_sum.ready, *down_sum.step(*attention_sum.ready).ready]
        elif step == 4:
            (gate_up_joined,) = hold([gate_up_joined], total)
            gate_pieces, up_pieces = (pieces_of(gate_up_joined, 2, k) for k in range(2))
            own_partial = backproject((d_qkv, local_rows), 0, 1, qkv_full, jnp.float32, [total])
            (gate_grad,) = assemble(gate_pieces, [units], half_tables[0], [own_partial])
            tokens = attention_sum.step(gate_grad).ready
        if step < size:
            place = (own_partials[0], 0) if step == 2 else (own_partials[1], (step - 3) * local_rows)
            total = add_low([(*place, local_rows)], [whole_range(arrived)], tokens)
    arrays = [(a, 0) for a in (inputs, saved_a, middle_grad, arrived, own_partial, d_branch_a)]
    input_grad, weight_sum_a, small_a = close_mix(
        False,
        0,
        local_rows,
        arrays,
        tables_a,
        *sizes,
        tokens=tokens,
    )
    height = width // LANES

    def flat(weight_sum, small):
        summed = weight_sum[:uses] + weight_sum[8 : 8 + uses]
        return jnp.concatenate([summed.reshape(uses * height, LANES), small])

    def unpacked(sums):
        constants = sums[uses * height : uses * height + 2, : count * uses].reshape(2, count, uses)
        return constants[0], sums[: uses * height].reshape(uses, width).T, jnp.sum(constants[1], axis=0)

    weight_sum_f, small_f = (one + other for one, other in zip(*sums_f))
    sums = SumEverywhere(jnp.concatenate([flat(weight_sum_f, small_f), flat(weight_sum_a, small_a)]))
    attention_sum.step(small_a)
    (up_grad,) = assemble(up_pieces, [units], half_tables[1], [sums.values, *attention_sum.ready])
    attention_sum.step(sums.step(up_grad))
    down_joined = down_sum.gathered(*attention_sum.ready)
    after = sums.step(down_joined)
    (down_grad,) = assemble(pieces_of(down_joined, 2), [units], whole_table, [after])
    attention_joined = attention_sum.gathered(sums.step(down_grad))
    after = sums.step(attention_joined)
    query_grad, key_grad, value_grad, out_grad = assemble(
        pieces_of(attention_joined, 2), [columns] * 4, whole_table, [sums.finished(0)]
    )
    (static_f, weight_f, scale_f), (static_a, weight_a, scale_a) = (
        unpacked(part) for part in jnp.split(sums.finished(0), 2)
    )
    return (
        out_streams,
        input_grad,
        query_grad,
        key_grad,
        value_grad,
        out_grad,
        gate_grad,
        up_grad,
        down_grad,
        jnp.stack([static_a, static_f]),
        jnp.stack([weight_a, weight_f]),
        jnp.stack([scale_a, scale_f]),
    )


def solution(mesh):
    placed = (
        P(("dp", "tensor"), None, None),
        P(("dp", "tensor"), None, None),
        P(),
        P(),
        P("dp", "tensor"),
        P("dp", "tensor"),
        P("dp", "tensor"),
        P("dp", "tensor"),
        P("dp", "tensor"),
        P("dp", "tensor"),
        P("dp", "tensor"),
        P(),
        P(),
        P(),
    )
    return jax.shard_map(
        per_device,
        mesh=mesh,
        in_specs=placed,
        out_specs=(
            P(("dp", "tensor"), None, None),
            P(("dp", "tensor"), None, None),
            P(None, "tensor"),
            P(None, "tensor"),
            P(None, "tensor"),
            P(None, "tensor"),
            P(None, "tensor"),
            P(None, "tensor"),
            P(None, "tensor"),
            P(),
            P(),
            P(),
        ),
        check_vma=False,
    )
```

```python
import functools
import math
import jax
import jax.numpy as jnp
from jax import lax
from jax.experimental import pallas as pl
from jax.experimental.pallas import tpu as pltpu
from jax.sharding import PartitionSpec as P

HEAD_DIM = 128
EPSILON = 1e-05
THETA = 10000.0
MASKED = -1e30
LANES = 128
GROUP = 16
CHUNK = 512
PARAMS = pltpu.CompilerParams(vmem_limit_bytes=58 * 1024 * 1024)


def matmul(left, right):
    return jnp.dot(left, right, preferred_element_type=jnp.float32)


def times_transposed(left, right):
    return lax.dot_general(
        left, right, (((1,), (1,)), ((), ())), preferred_element_type=jnp.float32
    )


def transposed_times(left, right):
    return lax.dot_general(
        left, right, (((0,), (0,)), ((), ())), preferred_element_type=jnp.float32
    )


MARKS = {}


def marked(results, mark):
    for one in results:
        MARKS[id(one)] = (one, mark)
    return results


def waits(tokens):
    each = {id(t): t for t in (MARKS[id(one)][1] if id(one) in MARKS else one for one in tokens)}
    return list(each.values())


MARK_SPEC = pl.BlockSpec((8, LANES), lambda *index: (0, 0))
MARK_SHAPE = jax.ShapeDtypeStruct((8, LANES), jnp.float32)


def anywhere(count):
    return [pl.BlockSpec(memory_space=pl.ANY)] * count


def cost(microseconds=0):
    return pl.CostEstimate(flops=int(microseconds * 1e9), bytes_accessed=0, transcendentals=0)


def hold(values, *tokens):
    tokens = waits(tokens)

    def nothing(*refs):
        pass

    return pl.pallas_call(
        nothing,
        in_specs=anywhere(len(values) + len(tokens)),
        out_specs=anywhere(len(values)),
        out_shape=[jax.ShapeDtypeStruct(a.shape, a.dtype) for a in values],
        input_output_aliases={k: k for k in range(len(values))},
        name="hold",
    )(*values, *tokens)


def lanes_of(rows):
    return lax.broadcasted_iota(jnp.int32, (rows, LANES), 1)


def column(values, lane):
    return values[:, lane : lane + 1]


def place(values, columns, first):
    lane = lanes_of(values.shape[0])
    for offset, one in enumerate(columns):
        values = jnp.where(lane == first + offset, one, values)
    return values


def fold(values):
    total = values[:, :LANES]
    for start in range(LANES, values.shape[1], LANES):
        total = total + values[:, start : start + LANES]
    return total


def row_sum(values):
    return jnp.sum(values, axis=1, keepdims=True)


def rolled(values, shift):
    shift = shift % LANES
    return values if shift == 0 else pltpu.roll(values, shift, 1)


def coefficients(projected, means, rsqrts, param_ref, sums_ref, streams, uses, parts, centred):
    rows = projected[0].shape[0]
    lane = lanes_of(rows)
    gathered = jnp.zeros((rows, LANES), jnp.float32)
    sums = jnp.zeros((rows, LANES), jnp.float32)
    for j in range(streams):
        total = joined(projected[j], parts)
        if not centred:
            total = total - means[j] * sums_ref[0:1, :]
        total = total * rsqrts[j]
        inside = (lane >= j * uses) & (lane < (j + 1) * uses)
        gathered = jnp.where(inside, rolled(total, j * uses), gathered)
        sums = jnp.where(inside, rolled(jnp.broadcast_to(sums_ref[0:1, :], (rows, LANES)), j * uses), sums)
    bent = jnp.tanh(gathered)
    return gathered, bent, param_ref[0:1, :] + param_ref[1:2, :] * bent, sums


def pack_saved(coeffs, bent, gathered, sums, means, rsqrts, mean_e, rsqrt_e, streams, uses):
    lane = lanes_of(coeffs.shape[0])
    count = streams * uses
    saved = jnp.where(lane < count, coeffs, 0.0)
    saved = jnp.where((lane >= count) & (lane < 2 * count), rolled(bent, count), saved)
    saved = jnp.where((lane >= 2 * count) & (lane < 3 * count), rolled(gathered, 2 * count), saved)
    first = 3 * count + 2 * streams + 2
    saved = jnp.where((lane >= first) & (lane < first + count), rolled(sums, first), saved)
    return place(saved, [*means, *rsqrts, mean_e, rsqrt_e], 3 * count)


def centre_stats(total, values_of, width):
    mean = row_sum(total) * (1.0 / width)
    spread = None
    for start in range(0, width, CHUNK):
        centred = values_of(start) - mean
        square = fold(centred * centred)
        spread = square if spread is None else spread + square
    return mean, lax.rsqrt(row_sum(spread) * (1.0 / width) + EPSILON)


def entering_norm(read, coeffs, streams, uses, width, entering_ref, rows):
    total = None
    for start in range(0, width, CHUNK):
        entering = column(coeffs, 0) * read(0, start)
        for j in range(1, streams):
            entering = entering + column(coeffs, j * uses) * read(j, start)
        entering_ref[rows, start : start + CHUNK] = entering
        part = fold(entering)
        total = part if total is None else total + part
    return centre_stats(total, lambda start: entering_ref[rows, start : start + CHUNK], width)


def weight_parts(w_ref, parts_ref, sums_ref, parts):
    @pl.when(pl.program_id(0) == 0)
    def _():
        rest = w_ref[...]
        rows, width = rest.shape
        each = []
        for _ in range(parts):
            each.append(rest.astype(jnp.bfloat16).astype(jnp.float32))
            rest = rest - each[-1]
        each.append(jnp.zeros((LANES - parts * rows, width), jnp.float32))
        parts_ref[...] = jnp.concatenate(each, axis=0).astype(jnp.bfloat16)
        sums = times_transposed(jnp.ones((8, width), jnp.bfloat16), parts_ref[...])
        sums_ref[...] = joined(sums, parts)


def joined(values, parts):
    total = values
    for part in range(1, parts):
        total = total + rolled(values, -8 * part)
    return total


def open_attention_kernel(
    streams, uses, width, x_ref, w_ref, param_ref, normed_ref, saved_ref, raw_ref, entering_ref, parts_ref, sums_ref
):
    block = x_ref.shape[0]
    weight_parts(w_ref, parts_ref, sums_ref, 3)
    stacked = jnp.concatenate([x_ref[:, j * width : (j + 1) * width] for j in range(streams)], axis=0)
    raw_ref[...] = times_transposed(stacked, parts_ref[...])

    def body(index, carry):
        first = pl.multiple_of(index * GROUP, GROUP)
        rows = pl.ds(first, GROUP)

        def read(j, start):
            return x_ref[rows, j * width + start : j * width + start + CHUNK].astype(jnp.float32)

        means, rsqrts, projected = [], [], []
        for j in range(streams):
            total = None
            for start in range(0, width, CHUNK):
                part = fold(read(j, start))
                total = part if total is None else total + part
            mean, rsqrt = centre_stats(total, functools.partial(read, j), width)
            means.append(mean)
            rsqrts.append(rsqrt)
            projected.append(raw_ref[pl.ds(pl.multiple_of(j * block + first, GROUP), GROUP), :])
        gathered, bent, coeffs, sums = coefficients(
            projected, means, rsqrts, param_ref, sums_ref, streams, uses, 3, False
        )
        mean_e, rsqrt_e = entering_norm(read, coeffs, streams, uses, width, entering_ref, rows)
        for start in range(0, width, CHUNK):
            normed_ref[rows, start : start + CHUNK] = (
                (entering_ref[rows, start : start + CHUNK] - mean_e) * rsqrt_e
            ).astype(jnp.bfloat16)
        saved_ref[rows, :] = pack_saved(
            coeffs, bent, gathered, sums, means, rsqrts, mean_e, rsqrt_e, streams, uses
        )
        return carry

    lax.fori_loop(0, block // GROUP, body, 0)


def open_feedforward_kernel(streams, uses, width, *refs):
    x_ref, saved_a_ref, out_ref, g_ref, valid_ref, w_ref, param_ref = refs[:7]
    normed_ref, grad_ref, saved_ref, h_ref = refs[7:11]
    high_ref, low_ref, raw_ref, entering_ref, stats_ref, parts_ref, sums_ref = refs[11:]
    block = x_ref.shape[0]
    weight_parts(w_ref, parts_ref, sums_ref, 2)
    count = streams * uses

    def first_pass(index, carry):
        first = pl.multiple_of(index * GROUP, GROUP)
        rows = pl.ds(first, GROUP)
        coeffs = saved_a_ref[rows, :]
        totals = [None] * streams
        for start in range(0, width, CHUNK):
            out = out_ref[rows, start : start + CHUNK]
            values = [
                x_ref[rows, j * width + start : j * width + start + CHUNK].astype(jnp.float32)
                for j in range(streams)
            ]
            for i in range(streams):
                mixed = column(coeffs, i * uses + streams + 1) * out
                for j in range(streams):
                    mixed = mixed + column(coeffs, j * uses + 1 + i) * values[j]
                h_ref[rows, i * width + start : i * width + start + CHUNK] = mixed
                part = fold(mixed)
                totals[i] = part if totals[i] is None else totals[i] + part
        stats = jnp.zeros((GROUP, LANES), jnp.float32)
        means, rsqrts = [], []
        for i in range(streams):
            mean = row_sum(totals[i]) * (1.0 / width)
            spread = None
            for start in range(0, width, CHUNK):
                centred = h_ref[rows, i * width + start : i * width + start + CHUNK] - mean
                high = centred.astype(jnp.bfloat16)
                target = pl.ds(pl.multiple_of(i * block + first, GROUP), GROUP)
                high_ref[target, start : start + CHUNK] = high
                low_ref[target, start : start + CHUNK] = (centred - high.astype(jnp.float32)).astype(jnp.bfloat16)
                square = fold(centred * centred)
                spread = square if spread is None else spread + square
            means.append(mean)
            rsqrts.append(lax.rsqrt(row_sum(spread) * (1.0 / width) + EPSILON))
        stats_ref[rows, :] = place(stats, [*means, *rsqrts], 0)
        return carry

    lax.fori_loop(0, block // GROUP, first_pass, 0)
    raw_ref[...] = times_transposed(high_ref[...], parts_ref[...]) + times_transposed(
        low_ref[...], parts_ref[...]
    )

    def second_pass(index, carry):
        first = pl.multiple_of(index * GROUP, GROUP)
        rows = pl.ds(first, GROUP)
        stats = stats_ref[rows, :]
        means = [column(stats, j) for j in range(streams)]
        rsqrts = [column(stats, streams + j) for j in range(streams)]
        projected = [raw_ref[pl.ds(pl.multiple_of(j * block + first, GROUP), GROUP), :] for j in range(streams)]
        gathered, bent, coeffs, sums = coefficients(
            projected, means, rsqrts, param_ref, sums_ref, streams, uses, 2, True
        )

        def read(j, start):
            return h_ref[rows, j * width + start : j * width + start + CHUNK]

        mean_e, rsqrt_e = entering_norm(read, coeffs, streams, uses, width, entering_ref, rows)
        branch = [column(coeffs, i * uses + streams + 1) * valid_ref[rows, 0:1] for i in range(streams)]
        for start in range(0, width, CHUNK):
            normed_ref[rows, start : start + CHUNK] = (
                (entering_ref[rows, start : start + CHUNK] - mean_e) * rsqrt_e
            ).astype(jnp.bfloat16)
            grad = None
            for i in range(streams):
                term = branch[i] * g_ref[rows, i * width + start : i * width + start + CHUNK].astype(jnp.float32)
                grad = term if grad is None else grad + term
            grad_ref[rows, start : start + CHUNK] = grad.astype(jnp.bfloat16)
        saved_ref[rows, :] = pack_saved(
            coeffs, bent, gathered, sums, means, rsqrts, mean_e, rsqrt_e, streams, uses
        )
        return carry

    lax.fori_loop(0, block // GROUP, second_pass, 0)


def finish_kernel(streams, uses, width, h_ref, saved_ref, arrived_ref, partial_ref, *refs):
    y_ref, mark_ref = refs[-2:]
    mark_ref[...] = jnp.zeros_like(mark_ref)

    def body(index, carry):
        rows = pl.ds(pl.multiple_of(index * GROUP, GROUP), GROUP)
        coeffs = saved_ref[rows, :]
        for start in range(0, width, CHUNK):
            out = arrived_ref[rows, start : start + CHUNK].astype(jnp.float32) + partial_ref[rows, start : start + CHUNK]
            values = [h_ref[rows, j * width + start : j * width + start + CHUNK] for j in range(streams)]
            for i in range(streams):
                mixed = column(coeffs, i * uses + streams + 1) * out
                for j in range(streams):
                    mixed = mixed + column(coeffs, j * uses + 1 + i) * values[j]
                y_ref[rows, i, start : start + CHUNK] = mixed.astype(jnp.bfloat16)
        return carry

    lax.fori_loop(0, h_ref.shape[0] // GROUP, body, 0)


def close_kernel(streams, uses, width, inner, kept, *refs):
    inputs = 12 if inner else 8
    refs = refs[:inputs] + refs[inputs + kept :]
    if inner:
        (h_ref, saved_ref, g_ref, arrived_ref, partial_ref, arrived_f_ref, partial_f_ref, valid_ref, saved_a_ref,
         out_a_ref, wt_ref, param_ref, grad_ref, branch_ref, below_ref, weight_ref, small_ref,
         centre_ref, du_ref, left_ref, dl_ref, cols_ref, sums_ref, parts_ref) = refs
    else:
        (h_ref, saved_ref, g_ref, arrived_ref, partial_ref, branch_in_ref, wt_ref, param_ref,
         grad_ref, weight_ref, small_ref, centre_ref, du_ref, left_ref, dl_ref, cols_ref, sums_ref, parts_ref) = refs
    block = h_ref.shape[0]
    count = streams * uses
    step = pl.program_id(0)
    base = pl.multiple_of(step * block, GROUP)
    all_rows = centre_ref.shape[0] // streams

    @pl.when(step == 0)
    def _():
        sums_ref[...] = jnp.zeros_like(sums_ref)
        weights = wt_ref[...]
        high = weights.astype(jnp.bfloat16).astype(jnp.float32)
        rest = jnp.zeros((LANES - 3 * weights.shape[0], width), jnp.float32)
        parts_ref[...] = jnp.concatenate([high, high, weights - high, rest], axis=0).astype(jnp.bfloat16)

    def read_h(rows, j, start):
        return h_ref[rows, j * width + start : j * width + start + CHUNK].astype(jnp.float32)

    def read_g(rows, i, start):
        values = g_ref[rows, i * width + start : i * width + start + CHUNK].astype(jnp.float32)
        return values * valid_ref[rows, 0:1] if inner else values

    def read_dn(rows, start):
        return arrived_ref[rows, start : start + CHUNK].astype(jnp.float32) + partial_ref[rows, start : start + CHUNK]

    def first_pass(index, carry):
        first = pl.multiple_of(index * GROUP, GROUP)
        rows = pl.ds(first, GROUP)
        saved = saved_ref[rows, :]
        means = [column(saved, 3 * count + j) for j in range(streams)]
        rsqrts = [column(saved, 3 * count + streams + j) for j in range(streams)]
        mean_e = column(saved, 3 * count + 2 * streams)
        rsqrt_e = column(saved, 3 * count + 2 * streams + 1)
        sums = {}

        def add(key, values):
            part = fold(values)
            sums[key] = part if key not in sums else sums[key] + part

        for start in range(0, width, CHUNK):
            dn = read_dn(rows, start)
            values = [read_h(rows, j, start) for j in range(streams)]
            for j in range(streams):
                target = pl.ds(pl.multiple_of(j * all_rows + base + first, GROUP), GROUP)
                centre_ref[target, start : start + CHUNK] = (values[j] - means[j]).astype(jnp.bfloat16)
            entering = column(saved, 0) * values[0]
            for j in range(1, streams):
                entering = entering + column(saved, j * uses) * values[j]
            normed = (entering - mean_e) * rsqrt_e
            add("dn", dn)
            add("dnn", dn * normed)
            for j in range(streams):
                add(("dnh", j), dn * values[j])
                add(("nh", j), normed * values[j])
            if inner:
                out = (
                    arrived_f_ref[rows, start : start + CHUNK].astype(jnp.float32)
                    + partial_f_ref[rows, start : start + CHUNK]
                )
            for i in range(streams):
                g = read_g(rows, i, start)
                for j in range(streams):
                    add(("gh", j, i), g * values[j])
                if inner:
                    add(("go", i), g * out)
        total = {key: row_sum(value) for key, value in sums.items()}
        mean_dn = total["dn"] * (1.0 / width)
        mean_dnn = total["dnn"] * (1.0 / width)
        columns = []
        for j in range(streams):
            columns.append(
                rsqrt_e * (total["dnh", j] - total["dn"] * means[j] - mean_dnn * total["nh", j])
            )
            columns.extend(total["gh", j, i] for i in range(streams))
            columns.append(total["go", j] if inner else branch_in_ref[rows, j : j + 1])
        d_coeffs = place(jnp.zeros((GROUP, LANES), jnp.float32), columns, 0)
        lane = lanes_of(GROUP)
        bent = jnp.where(lane < count, rolled(saved, -count), 0.0)
        projected = jnp.where(lane < count, rolled(saved, -2 * count), 0.0)
        sums_ref[0] += d_coeffs
        sums_ref[1] += d_coeffs * bent
        du = d_coeffs * param_ref[1:2, :] * (1.0 - bent * bent)
        with_mean = du * jnp.where(lane < count, rolled(saved, -(3 * count + 2 * streams + 2)), 0.0) * (1.0 / width)
        with_value = du * projected * (1.0 / width)
        shifts, slopes = [], []
        scaled = jnp.zeros((GROUP, LANES), jnp.float32)
        for j in range(streams):
            inside = (lane >= j * uses) & (lane < (j + 1) * uses)
            slope = rsqrts[j] * rsqrts[j] * row_sum(jnp.where(inside, with_value, 0.0))
            shifts.append(means[j] * slope - rsqrts[j] * row_sum(jnp.where(inside, with_mean, 0.0)))
            slopes.append(slope)
            scaled = jnp.where(inside, du * rsqrts[j], scaled)
        high = scaled.astype(jnp.bfloat16).astype(jnp.float32)
        low = (scaled - high).astype(jnp.bfloat16).astype(jnp.float32)
        for j in range(streams):
            own_high, own_low = rolled(high, -j * uses), rolled(low, -j * uses)
            left = jnp.where(lane < uses, own_high, 0.0)
            left = jnp.where((lane >= 8) & (lane < 8 + uses), rolled(own_low, 8), left)
            left = jnp.where((lane >= 16) & (lane < 16 + uses), rolled(own_high, 16), left)
            left_ref[pl.ds(pl.multiple_of(j * block + first, GROUP), GROUP), :] = left.astype(jnp.bfloat16)
            pair = jnp.where(lane < 8 + uses, left, 0.0)
            du_ref[pl.ds(pl.multiple_of(j * all_rows + base + first, GROUP), GROUP), :] = pair.astype(jnp.bfloat16)
        cols_ref[rows, :] = place(
            jnp.zeros((GROUP, LANES), jnp.float32), [mean_dn, mean_dnn, *shifts, *slopes], 0
        )
        return carry

    lax.fori_loop(0, block // GROUP, first_pass, 0)
    dl_ref[...] = jnp.dot(left_ref[...], parts_ref[...], preferred_element_type=jnp.float32)

    def second_pass(index, carry):
        first = pl.multiple_of(index * GROUP, GROUP)
        rows = pl.ds(first, GROUP)
        saved = saved_ref[rows, :]
        cols = cols_ref[rows, :]
        mean_e = column(saved, 3 * count + 2 * streams)
        rsqrt_e = column(saved, 3 * count + 2 * streams + 1)
        scaled_mean = column(cols, 0) * rsqrt_e
        scaled_slope = column(cols, 1) * rsqrt_e
        branch_sums = [None] * streams
        for start in range(0, width, CHUNK):
            values = [read_h(rows, j, start) for j in range(streams)]
            entering = column(saved, 0) * values[0]
            for j in range(1, streams):
                entering = entering + column(saved, j * uses) * values[j]
            normed = (entering - mean_e) * rsqrt_e
            de = rsqrt_e * read_dn(rows, start) - scaled_mean - normed * scaled_slope
            gs = [read_g(rows, i, start) for i in range(streams)]
            below = None
            for j in range(streams):
                grad = column(saved, j * uses) * de + column(cols, 2 + j)
                grad = grad - values[j] * column(cols, 2 + streams + j)
                grad = grad + dl_ref[pl.ds(pl.multiple_of(j * block + first, GROUP), GROUP), start : start + CHUNK]
                for i in range(streams):
                    grad = grad + column(saved, j * uses + 1 + i) * gs[i]
                if inner:
                    grad_ref[rows, j * width + start : j * width + start + CHUNK] = grad
                else:
                    grad_ref[rows, j, start : start + CHUNK] = grad.astype(jnp.bfloat16)
                if inner:
                    part = fold(grad * out_a_ref[rows, start : start + CHUNK])
                    branch_sums[j] = part if branch_sums[j] is None else branch_sums[j] + part
                    term = saved_a_ref[rows, j * uses + streams + 1 : j * uses + streams + 2] * grad
                    below = term if below is None else below + term
            if inner:
                below_ref[rows, start : start + CHUNK] = below.astype(jnp.bfloat16)
        if inner:
            branch_ref[rows, :] = place(
                jnp.zeros((GROUP, LANES), jnp.float32), [row_sum(one) for one in branch_sums], 0
            )
        return carry

    lax.fori_loop(0, block // GROUP, second_pass, 0)

    @pl.when(step == pl.num_programs(0) - 1)
    def _():
        product = lax.dot_general(
            du_ref[...], centre_ref[...], (((0,), (0,)), ((), ())), preferred_element_type=jnp.float32
        )
        weight_ref[...] = product[: weight_ref.shape[0]]
        small_ref[0:1, :] = jnp.sum(sums_ref[0], axis=0, keepdims=True)
        small_ref[1:2, :] = jnp.sum(sums_ref[1], axis=0, keepdims=True)


def rows_block(rows):
    return min(64, rows)


def specs_for(arrays, block, whole):
    specs = []
    for k, entry in enumerate(arrays):
        array, first = entry if isinstance(entry, tuple) else (entry, 0)
        if k in whole:
            specs.append(pl.BlockSpec(array.shape, lambda i: (0, 0)))
        else:
            specs.append(pl.BlockSpec((block, array.shape[1]), lambda i, first=first // block: (first + i, 0)))
    return specs


def plain(arrays):
    return [entry[0] if isinstance(entry, tuple) else entry for entry in arrays]


def mix_tables(static, weight, scale):
    streams, uses = static.shape
    count = streams * uses
    constants = jnp.stack([static.reshape(count), jnp.tile(scale, streams)])
    return jnp.pad(weight.T, ((0, 8 - uses), (0, 0))), jnp.pad(constants, ((0, 6), (0, LANES - count)))


def open_attention(x, tables, streams, uses):
    rows, width = x.shape[0], x.shape[1] // streams
    block = rows_block(rows)
    arrays = [x, *tables]
    return pl.pallas_call(
        functools.partial(open_attention_kernel, streams, uses, width),
        grid=(rows // block,),
        in_specs=specs_for(arrays, block, {1, 2}),
        out_specs=[pl.BlockSpec((block, width), lambda i: (i, 0)), pl.BlockSpec((block, LANES), lambda i: (i, 0))],
        out_shape=[jax.ShapeDtypeStruct((rows, width), jnp.bfloat16), jax.ShapeDtypeStruct((rows, LANES), jnp.float32)],
        scratch_shapes=[
            pltpu.VMEM((streams * block, LANES), jnp.float32),
            pltpu.VMEM((block, width), jnp.float32),
            pltpu.VMEM((LANES, width), jnp.bfloat16),
            pltpu.VMEM((8, LANES), jnp.float32),
        ],
        compiler_params=PARAMS,
        cost_estimate=cost(),
        name="open_attention",
    )(*plain(arrays))


def open_feedforward(x, saved_a, out_a, g, valid, tables, streams, uses):
    rows, width = x.shape[0], x.shape[1] // streams
    block = rows_block(rows)
    arrays = [x, saved_a, out_a, g, valid, *tables]

    def by_rows(columns):
        return pl.BlockSpec((block, columns), lambda i: (i, 0))

    return pl.pallas_call(
        functools.partial(open_feedforward_kernel, streams, uses, width),
        grid=(rows // block,),
        in_specs=specs_for(arrays, block, {5, 6}),
        out_specs=[by_rows(width), by_rows(width), by_rows(LANES), by_rows(streams * width)],
        out_shape=[
            jax.ShapeDtypeStruct((rows, width), jnp.bfloat16),
            jax.ShapeDtypeStruct((rows, width), jnp.bfloat16),
            jax.ShapeDtypeStruct((rows, LANES), jnp.float32),
            jax.ShapeDtypeStruct((rows, streams * width), jnp.float32),
        ],
        scratch_shapes=[
            pltpu.VMEM((streams * block, width), jnp.bfloat16),
            pltpu.VMEM((streams * block, width), jnp.bfloat16),
            pltpu.VMEM((streams * block, LANES), jnp.float32),
            pltpu.VMEM((block, width), jnp.float32),
            pltpu.VMEM((block, LANES), jnp.float32),
            pltpu.VMEM((LANES, width), jnp.bfloat16),
            pltpu.VMEM((8, LANES), jnp.float32),
        ],
        compiler_params=PARAMS,
        cost_estimate=cost(),
        name="open_feedforward",
    )(*plain(arrays))


def finish(first, h, saved, arrived, partial, streams, uses, filled, tokens=()):
    tokens = waits(tokens)
    rows, width = h.shape[0], h.shape[1] // streams
    block = rows_block(arrived[2])
    arrays = [(h, first), (saved, first), arrived[:2], (partial, first)]
    result, mark = pl.pallas_call(
        functools.partial(finish_kernel, streams, uses, width),
        grid=(arrived[2] // block,),
        in_specs=specs_for(arrays, block, set()) + anywhere(len(filled) + len(tokens)),
        out_specs=[pl.BlockSpec((block, streams, width), lambda i: (first // block + i, 0, 0)), MARK_SPEC],
        out_shape=[jax.ShapeDtypeStruct((rows, streams, width), jnp.bfloat16), MARK_SHAPE],
        input_output_aliases={4 + k: k for k in range(len(filled))},
        compiler_params=PARAMS,
        cost_estimate=cost(),
        name="finish",
    )(*plain(arrays), *filled, *tokens)
    return marked([result], mark)[0]


def close_mix(inner, first, rows, arrays, tables, streams, uses, filled=(), tokens=()):
    tokens = [*filled, *waits(tokens)]
    h = arrays[0][0]
    whole, width = h.shape[0], h.shape[1] // streams
    block = rows_block(rows)
    arrays = [*arrays, *tables]
    last = len(arrays)

    def by_rows(columns):
        return pl.BlockSpec((block, columns), lambda i: (first // block + i, 0))

    def fixed(height, columns):
        return pl.BlockSpec((height, columns), lambda i: (0, 0))

    if inner:
        out_specs = [by_rows(streams * width)]
        out_shape = [jax.ShapeDtypeStruct((whole, streams * width), jnp.float32)]
    else:
        out_specs = [pl.BlockSpec((block, streams, width), lambda i: (i, 0, 0))]
        out_shape = [jax.ShapeDtypeStruct((rows, streams, width), jnp.bfloat16)]
    if inner:
        out_specs += [by_rows(LANES), by_rows(width)]
        out_shape += [
            jax.ShapeDtypeStruct((whole, LANES), jnp.float32),
            jax.ShapeDtypeStruct((whole, width), jnp.bfloat16),
        ]
    out_specs += [fixed(16, width), fixed(8, LANES)]
    out_shape += [jax.ShapeDtypeStruct((16, width), jnp.float32), jax.ShapeDtypeStruct((8, LANES), jnp.float32)]
    return pl.pallas_call(
        functools.partial(close_kernel, streams, uses, width, inner, len(tokens)),
        grid=(rows // block,),
        in_specs=specs_for(arrays, block, {last - 2, last - 1}) + anywhere(len(tokens)),
        out_specs=out_specs,
        out_shape=out_shape,
        scratch_shapes=[
            pltpu.VMEM((streams * rows, width), jnp.bfloat16),
            pltpu.VMEM((streams * rows, LANES), jnp.bfloat16),
            pltpu.VMEM((streams * block, LANES), jnp.bfloat16),
            pltpu.VMEM((streams * block, width), jnp.float32),
            pltpu.VMEM((block, LANES), jnp.float32),
            pltpu.VMEM((2, GROUP, LANES), jnp.float32),
            pltpu.VMEM((LANES, width), jnp.bfloat16),
        ],
        input_output_aliases={len(arrays) + k: k for k in range(len(filled))},
        compiler_params=PARAMS,
        cost_estimate=cost(30 if inner else 0),
        name="close_feedforward" if inner else "close_attention",
    )(*plain(arrays), *tokens)


QUERY_ROWS = 256


def turn(values, cosine, sine):
    return values * cosine + pltpu.roll(values, HEAD_DIM // 2, 1) * sine


def turn_back(values, cosine, sine):
    return values * cosine - pltpu.roll(values, HEAD_DIM // 2, 1) * sine


def block_offset(mine, step, size, rows):
    return pl.multiple_of(lax.rem(mine + size - step, size) * rows, rows)


def allowed_keys(start_ref, first, rows, keys):
    row = first + lax.broadcasted_iota(jnp.int32, (rows, keys), 0)
    key = lax.broadcasted_iota(jnp.int32, (rows, keys), 1)
    return (key <= row) & (key >= start_ref[first : first + rows, 0:1])


def attend_kernel(size, *refs):
    mine_ref, start_ref, cosine_ref, sine_ref = refs[:4]
    raw = [refs[4 + 3 * s : 7 + 3 * s] for s in range(size)]
    q_ref, k_ref, v_ref, out_ref, log_ref, attended_ref = refs[4 + 3 * size :]
    mine = mine_ref[0]
    block = raw[0][0].shape[0]
    total = size * block
    for step in range(size):
        rows = pl.ds(block_offset(mine, step, size, block), block)
        cosine, sine = cosine_ref[rows, :], sine_ref[rows, :]
        q_ref[rows, :] = turn(raw[step][0][...], cosine, sine).astype(jnp.bfloat16)
        k_ref[rows, :] = turn(raw[step][1][...], cosine, sine).astype(jnp.bfloat16)
        v_ref[rows, :] = raw[step][2][...].astype(jnp.bfloat16)
    height = min(QUERY_ROWS, total)
    for first in range(0, total, height):
        keys = first + height
        scores = times_transposed(q_ref[first:keys, :], k_ref[:keys, :]) * HEAD_DIM**-0.5
        scores = jnp.where(allowed_keys(start_ref, first, height, keys), scores, MASKED)
        highest = jnp.max(scores, axis=1, keepdims=True)
        exponent = jnp.exp(scores - highest)
        row_total = jnp.sum(exponent, axis=1, keepdims=True)
        probs = (exponent * (1.0 / row_total)).astype(jnp.bfloat16)
        attended_ref[first:keys, :] = jnp.dot(
            probs, v_ref[:keys, :], preferred_element_type=jnp.float32
        ).astype(jnp.bfloat16)
        log_ref[first:keys, :] = jnp.broadcast_to(highest + jnp.log(row_total), (height, LANES))
    for step in range(size):
        rows = pl.ds(block_offset(mine, step, size, block), block)
        out_ref[step * block : (step + 1) * block, :] = attended_ref[rows, :]


def attend_back_kernel(size, kept, *refs):
    mine_ref, start_ref, cosine_ref, sine_ref, q_ref, k_ref, v_ref, log_ref = refs[:8]
    grads = refs[8 : 8 + size]
    dqkv_ref, d_out_ref, dq_ref, dk_ref, dv_ref = refs[8 + size + kept :]
    mine = mine_ref[0]
    head, heads = pl.program_id(0), pl.num_programs(0)
    block = grads[0].shape[0]
    total = size * block
    for step in range(size):
        d_out_ref[pl.ds(block_offset(mine, step, size, block), block), :] = grads[step][...]
    height = min(QUERY_ROWS, total)
    dk_ref[...] = jnp.zeros_like(dk_ref)
    dv_ref[...] = jnp.zeros_like(dv_ref)
    for first in range(0, total, height):
        keys = first + height
        q, d_out = q_ref[first:keys, :], d_out_ref[first:keys, :]
        k, v = k_ref[:keys, :], v_ref[:keys, :]
        scores = times_transposed(q, k) * HEAD_DIM**-0.5
        probs = jnp.where(
            allowed_keys(start_ref, first, height, keys), jnp.exp(scores - log_ref[first:keys, 0:1]), 0.0
        )
        d_probs = times_transposed(d_out, v)
        centre = jnp.sum(probs * d_probs, axis=1, keepdims=True)
        d_scores = (probs * (d_probs - centre)).astype(jnp.bfloat16)
        dv_ref[:keys, :] += transposed_times(probs.astype(jnp.bfloat16), d_out)
        dk_ref[:keys, :] += transposed_times(d_scores, q)
        dq_ref[first:keys, :] = jnp.dot(d_scores, k, preferred_element_type=jnp.float32)
    for step in range(size):
        rows = pl.ds(block_offset(mine, step, size, block), block)
        cosine, sine = cosine_ref[rows, :], sine_ref[rows, :]
        target = slice(step * block, (step + 1) * block)
        for part, values in enumerate(
            (
                turn_back(dq_ref[rows, :] * HEAD_DIM**-0.5, cosine, sine),
                turn_back(dk_ref[rows, :] * HEAD_DIM**-0.5, cosine, sine),
                dv_ref[rows, :],
            )
        ):
            columns = pl.ds(pl.multiple_of((part * heads + head) * HEAD_DIM, HEAD_DIM), HEAD_DIM)
            dqkv_ref[target, columns] = values.astype(jnp.bfloat16)


def whole_spec(shape):
    return pl.BlockSpec(shape, lambda h: (0,) * len(shape))


def head_spec(rows, first=0):
    return pl.BlockSpec((rows, HEAD_DIM), lambda h: (0, first + h))


def attend(raw_blocks, mine, starts, cosine, sine):
    size, block = len(raw_blocks), raw_blocks[0].shape[0]
    heads = raw_blocks[0].shape[1] // (3 * HEAD_DIM)
    total = size * block
    flat = jax.ShapeDtypeStruct((total, heads * HEAD_DIM), jnp.bfloat16)
    return pl.pallas_call(
        functools.partial(attend_kernel, size),
        grid=(heads,),
        in_specs=[pl.BlockSpec(memory_space=pltpu.SMEM)]
        + [whole_spec(a.shape) for a in (starts, cosine, sine)]
        + [head_spec(block, part * heads) for _ in range(size) for part in range(3)],
        out_specs=[head_spec(total)] * 5,
        out_shape=[flat] * 4 + [jax.ShapeDtypeStruct(flat.shape, jnp.float32)],
        scratch_shapes=[pltpu.VMEM((total, HEAD_DIM), jnp.bfloat16)],
        compiler_params=PARAMS,
        cost_estimate=cost(),
        name="attend",
    )(mine, starts, cosine, sine, *[raw for raw in raw_blocks for _ in range(3)])


def attend_back(heads_kept, grad_blocks, mine, starts, cosine, sine, tokens):
    tokens = waits(tokens)
    size, block = len(grad_blocks), grad_blocks[0].shape[0]
    total, columns = heads_kept[0].shape
    heads = columns // HEAD_DIM
    return pl.pallas_call(
        functools.partial(attend_back_kernel, size, len(tokens)),
        grid=(heads,),
        in_specs=[pl.BlockSpec(memory_space=pltpu.SMEM)]
        + [whole_spec(a.shape) for a in (starts, cosine, sine)]
        + [head_spec(total)] * 4
        + [head_spec(block)] * size
        + anywhere(len(tokens)),
        out_specs=whole_spec((total, 3 * columns)),
        out_shape=jax.ShapeDtypeStruct((total, 3 * columns), jnp.bfloat16),
        scratch_shapes=[pltpu.VMEM((total, HEAD_DIM), jnp.bfloat16)] + [pltpu.VMEM((total, HEAD_DIM), jnp.float32)] * 3,
        compiler_params=PARAMS,
        cost_estimate=cost(),
        name="attend_back",
    )(mine, starts, cosine, sine, *heads_kept, *grad_blocks, *tokens)


UNIT_TILE = 512


def forward_units_kernel(blocks, kept, *refs):
    gate_w_ref, up_w_ref = refs[blocks : blocks + 2]
    gate_ref, up_ref, rows_ref, hidden_ref, mark_ref = refs[blocks + 2 + kept :]
    mark_ref[...] = jnp.zeros_like(mark_ref)
    x = jnp.concatenate([ref[...] for ref in refs[:blocks]], axis=0)
    gate, up = matmul(x, gate_w_ref[...]), matmul(x, up_w_ref[...])
    gate_ref[...] = gate
    up_ref[...] = up
    hidden_ref[...] = (gate / (1.0 + jnp.exp(-gate)) * up).astype(jnp.bfloat16)

    @pl.when(pl.program_id(0) == 0)
    def _():
        rows_ref[...] = x


def backward_units_kernel(kept, *refs):
    first_ref, second_ref, gate_ref, up_ref, down_w_ref, gate_w_ref, up_w_ref = refs[:7]
    partial_ref, rows_ref, d_gate_ref, d_up_ref, mark_ref = refs[7 + kept :]
    mark_ref[...] = jnp.zeros_like(mark_ref)
    d_out = jnp.concatenate([first_ref[...], second_ref[...]], axis=0)
    d_hidden = matmul(d_out, down_w_ref[...])
    gate = gate_ref[...]
    sigmoid = 1.0 / (1.0 + jnp.exp(-gate))
    d_gate = (d_hidden * up_ref[...] * (sigmoid + gate * sigmoid * (1.0 - sigmoid))).astype(jnp.bfloat16)
    d_up = (d_hidden * gate * sigmoid).astype(jnp.bfloat16)
    d_gate_ref[...] = d_gate
    d_up_ref[...] = d_up
    part = times_transposed(d_gate, gate_w_ref[...]) + times_transposed(d_up, up_w_ref[...])

    @pl.when(pl.program_id(0) == 0)
    def _():
        partial_ref[...] = part
        rows_ref[...] = d_out

    @pl.when(pl.program_id(0) > 0)
    def _():
        partial_ref[...] += part


def forward_units(pair, size, blocks, gate_up, filled, tokens=()):
    tokens = waits(tokens)
    each, width = blocks[0].shape
    count = len(blocks)
    rows = each * count // 2
    units = gate_up.shape[1] // 2
    tile = min(UNIT_TILE, units)
    tiles = units // tile
    weight = functools.partial(pl.BlockSpec, (width, tile))
    outs = pl.pallas_call(
        functools.partial(forward_units_kernel, count, len(filled) + len(tokens)),
        grid=(tiles,),
        in_specs=[pl.BlockSpec((each, width), lambda i: (0, 0))] * count
        + [weight(lambda i: (0, i)), weight(lambda i: (0, tiles + i))]
        + anywhere(len(filled) + len(tokens)),
        out_specs=[
            pl.BlockSpec((2 * rows, tile), lambda i: (0, i)),
            pl.BlockSpec((2 * rows, tile), lambda i: (0, i)),
            pl.BlockSpec((2 * rows, width), lambda i: (pair, 0)),
            pl.BlockSpec((2 * rows, tile), lambda i: (pair, i)),
            MARK_SPEC,
        ],
        out_shape=[
            jax.ShapeDtypeStruct((2 * rows, units), jnp.float32),
            jax.ShapeDtypeStruct((2 * rows, units), jnp.float32),
            jax.ShapeDtypeStruct((size * rows, width), jnp.bfloat16),
            jax.ShapeDtypeStruct((size * rows, units), jnp.bfloat16),
            MARK_SHAPE,
        ],
        input_output_aliases={count + 2 + k: 2 + k for k in range(len(filled))},
        compiler_params=PARAMS,
        cost_estimate=cost(),
        name="forward_units",
    )(*blocks, gate_up, gate_up, *filled, *tokens)
    outs = marked(outs[:-1], outs[-1])
    return outs[0], outs[1], outs[2:]


def backward_units(pair, size, blocks, gate, up, gate_up, down, filled, tokens=()):
    tokens = waits(tokens)
    rows, width = blocks[0].shape
    units = down.shape[1]
    tile = min(UNIT_TILE, units)
    tiles = units // tile
    weight = functools.partial(pl.BlockSpec, (width, tile))
    by_tile = pl.BlockSpec((2 * rows, tile), lambda i: (0, i))
    outs = pl.pallas_call(
        functools.partial(backward_units_kernel, len(filled) + len(tokens)),
        grid=(tiles,),
        in_specs=[pl.BlockSpec((rows, width), lambda i: (0, 0))] * 2
        + [by_tile, by_tile]
        + [weight(lambda i: (0, i)), weight(lambda i: (0, i)), weight(lambda i: (0, tiles + i))]
        + anywhere(len(filled) + len(tokens)),
        out_specs=[
            pl.BlockSpec((2 * rows, width), lambda i: (0, 0)),
            pl.BlockSpec((2 * rows, width), lambda i: (pair, 0)),
            pl.BlockSpec((2 * rows, tile), lambda i: (pair, i)),
            pl.BlockSpec((2 * rows, tile), lambda i: (pair, i)),
            MARK_SPEC,
        ],
        out_shape=[
            jax.ShapeDtypeStruct((2 * rows, width), jnp.float32),
            jax.ShapeDtypeStruct((size * rows, width), jnp.bfloat16),
            jax.ShapeDtypeStruct((size * rows, units), jnp.bfloat16),
            jax.ShapeDtypeStruct((size * rows, units), jnp.bfloat16),
            MARK_SHAPE,
        ],
        input_output_aliases={7 + k: 1 + k for k in range(len(filled))},
        compiler_params=PARAMS,
        cost_estimate=cost(),
        name="backward_units",
    )(*blocks, gate, up, down, gate_up, gate_up, *filled, *tokens)
    outs = marked(outs[:-1], outs[-1])
    return outs[0], outs[1:]


def assemble_kernel(count, pieces, kept, table_ref, *refs):
    sources, outs, mark_ref = refs[:count], refs[count + kept : -1], refs[-1]
    mark_ref[...] = jnp.zeros_like(mark_ref)
    for k in range(count):

        @pl.when(pl.program_id(0) // pieces == k)
        def _(k=k):
            first = 0
            for out_ref in outs:
                columns = out_ref.shape[1]
                out_ref[...] = sources[k][:, first : first + columns].astype(jnp.float32)
                first += columns


def assemble(arrays, widths, table, tokens=()):
    tokens = waits(tokens)
    count = len(arrays)
    pieces = arrays[0][2]
    rows, columns = arrays[0][3], arrays[0][0].shape[1]
    *results, mark = pl.pallas_call(
        functools.partial(assemble_kernel, count, pieces, len(tokens)),
        grid_spec=pltpu.PrefetchScalarGridSpec(
            num_scalar_prefetch=1,
            grid=(count * pieces,),
            in_specs=[
                pl.BlockSpec(
                    (rows, columns),
                    lambda i, t, k=k, first=first: (first + jnp.clip(i - k * pieces, 0, pieces - 1), 0),
                )
                for k, (_, first, _, _) in enumerate(arrays)
            ]
            + anywhere(len(tokens)),
            out_specs=[pl.BlockSpec((rows, width), lambda i, t: (t[i], 0)) for width in widths] + [MARK_SPEC],
        ),
        out_shape=[jax.ShapeDtypeStruct((count * pieces * rows, width), jnp.float32) for width in widths] + [MARK_SHAPE],
        compiler_params=PARAMS,
        cost_estimate=cost(),
        name="assemble",
    )(table, *(array for array, *_ in arrays), *tokens)
    return marked(results, mark)


PRODUCT_TILE = 1024


def across_of(width, first):
    if width <= 2 * PRODUCT_TILE and first % width == 0:
        return width if width * 3 <= 5 * PRODUCT_TILE else width // 2
    return math.gcd(PRODUCT_TILE, width, first or width)


def joined_left(refs):
    left = [ref[...] for ref in refs]
    return left[0] if len(left) == 1 else jnp.concatenate(left, axis=0)


def away_kernel(blocks, core_ref, *refs):
    refs[-1][...] = jnp.zeros_like(refs[-1])
    refs[-2][...] = transposed_times(joined_left(refs[:blocks]), refs[blocks][...]).astype(jnp.bfloat16)


def own_kernel(blocks, scalars_ref, *refs):
    away_ref, kept_ref, mark_ref = refs[-3:]
    mark_ref[...] = jnp.zeros_like(mark_ref)
    product = transposed_times(joined_left(refs[:blocks]), refs[blocks][...])
    product = product + refs[blocks + 1][...].astype(jnp.float32)

    @pl.when(pl.program_id(0) == 0)
    def _():
        away_ref[...] = product.astype(jnp.bfloat16)

    @pl.when(pl.program_id(0) == 1)
    def _():
        kept_ref[...] = product


def away_product(core, left, right, columns, first, filled, tokens=()):
    tokens = waits(tokens)
    half = left[0].shape[1] // 2
    rows, width = right.shape
    down, across = min(PRODUCT_TILE, half), across_of(width, first)
    high, offset = half // down, first // across
    result, mark = pl.pallas_call(
        functools.partial(away_kernel, len(left)),
        grid_spec=pltpu.PrefetchScalarGridSpec(
            num_scalar_prefetch=1,
            grid=(high, width // across),
            in_specs=[
                pl.BlockSpec((block.shape[0], down), lambda i, j, c: (0, (1 - c[0]) * high + i)) for block in left
            ]
            + [pl.BlockSpec((rows, across), lambda i, j, c: (0, j))]
            + anywhere(len(filled) + len(tokens)),
            out_specs=[pl.BlockSpec((down, across), lambda i, j, c: (i, offset + j)), MARK_SPEC],
        ),
        out_shape=[jax.ShapeDtypeStruct((half, columns), jnp.bfloat16), MARK_SHAPE],
        input_output_aliases={2 + len(left): 0} if filled else {},
        compiler_params=PARAMS,
        cost_estimate=cost(),
        name="away_product",
    )(core, *left, right, *filled, *tokens)
    return marked([result], mark)[0]


def own_product(scalars, left, right, arrived, columns, first, rows_first, rows_here, filled, tokens=()):
    tokens = waits(tokens)
    half = left[0].shape[1] // 2
    rows, width = right.shape
    cut = rows_here // 2
    down, across = min(PRODUCT_TILE, cut), across_of(width, first)
    high, wide, offset = cut // down, width // across, first // across

    def row(g, i, c):
        return rows_first // down + jnp.where(g == 0, 1 - c[1], c[1]) * high + i

    *results, mark = pl.pallas_call(
        functools.partial(own_kernel, len(left)),
        grid_spec=pltpu.PrefetchScalarGridSpec(
            num_scalar_prefetch=1,
            grid=(2, high, wide),
            in_specs=[
                pl.BlockSpec((block.shape[0], down), lambda g, i, j, c: (0, c[0] * (half // down) + row(g, i, c)))
                for block in left
            ]
            + [
                pl.BlockSpec((rows, across), lambda g, i, j, c: (0, j)),
                pl.BlockSpec((down, across), lambda g, i, j, c: (row(g, i, c), offset + j)),
            ]
            + anywhere(len(filled) + len(tokens)),
            out_specs=[
                pl.BlockSpec(
                    (down, across),
                    lambda g, i, j, c: (jnp.where(g == 0, i, high - 1), offset + jnp.where(g == 0, j, wide - 1)),
                ),
                pl.BlockSpec(
                    (down, across),
                    lambda g, i, j, c: (jnp.where(g == 0, 0, i), offset + jnp.where(g == 0, 0, j)),
                ),
                MARK_SPEC,
            ],
        ),
        out_shape=[
            jax.ShapeDtypeStruct((cut, columns), jnp.bfloat16),
            jax.ShapeDtypeStruct((cut, columns), jnp.float32),
            MARK_SHAPE,
        ],
        input_output_aliases={3 + len(left) + k: k for k in range(len(filled))},
        compiler_params=PARAMS,
        cost_estimate=cost(),
        name="own_product",
    )(scalars, *left, right, arrived, *filled, *tokens)
    return marked(results, mark)


def backproject_kernel(d_ref, w_ref, *refs):
    refs[-1][...] = jnp.zeros_like(refs[-1])
    refs[-2][...] = times_transposed(d_ref[...], w_ref[...]).astype(refs[-2].dtype)


def backproject(rows_of, first, count, weight, kind, tokens=()):
    tokens = waits(tokens)
    array, rows = rows_of
    width, columns = weight.shape
    across = min(512, width)
    result, mark = pl.pallas_call(
        backproject_kernel,
        grid=(width // across, count),
        in_specs=[
            pl.BlockSpec((rows, columns), lambda j, i: (first + i, 0)),
            pl.BlockSpec((across, columns), lambda j, i: (j, 0)),
        ]
        + anywhere(len(tokens)),
        out_specs=[pl.BlockSpec((rows, across), lambda j, i: (i, j)), MARK_SPEC],
        out_shape=[jax.ShapeDtypeStruct((count * rows, width), kind), MARK_SHAPE],
        compiler_params=PARAMS,
        cost_estimate=cost(),
        name="backproject",
    )(array, weight, *tokens)
    return marked([result], mark)[0]


def project_kernel(count, *refs):
    refs[-1][...] = matmul(jnp.concatenate([ref[...] for ref in refs[:count]], axis=0), refs[count][...]).astype(jnp.bfloat16)


def project(blocks, weight, columns):
    rows, width = blocks[0].shape
    across = min(256, columns)
    return pl.pallas_call(
        functools.partial(project_kernel, len(blocks)),
        grid=(columns // across,),
        in_specs=[pl.BlockSpec((rows, width), lambda j: (0, 0))] * len(blocks)
        + [pl.BlockSpec((width, across), lambda j: (0, j))],
        out_specs=pl.BlockSpec((len(blocks) * rows, across), lambda j: (0, j)),
        out_shape=jax.ShapeDtypeStruct((len(blocks) * rows, columns), jnp.bfloat16),
        compiler_params=PARAMS,
        cost_estimate=cost(),
        name="project",
    )(*blocks, weight)


def out_project_kernel(count, *refs):
    refs[-1][...] = times_transposed(jnp.concatenate([ref[...] for ref in refs[:count]], axis=1), refs[count][...])


def out_project(blocks, weight):
    rows = blocks[0].shape[0]
    width, columns = weight.shape
    across = min(512, width)
    return pl.pallas_call(
        functools.partial(out_project_kernel, len(blocks)),
        grid=(width // across,),
        in_specs=[pl.BlockSpec(block.shape, lambda j: (0, 0)) for block in blocks]
        + [pl.BlockSpec((across, columns), lambda j: (j, 0))],
        out_specs=pl.BlockSpec((rows, across), lambda j: (0, j)),
        out_shape=jax.ShapeDtypeStruct((rows, width), jnp.float32),
        compiler_params=PARAMS,
        cost_estimate=cost(),
        name="out_project",
    )(*blocks, weight)


SUM_ROWS = 256


def halve_kernel(which_ref, own_ref, arrived_ref, *refs):
    away_ref, kept_ref, mark_ref = refs[-3:]
    mark_ref[...] = jnp.zeros_like(mark_ref)
    total = own_ref[...] + arrived_ref[...].astype(jnp.float32)

    @pl.when(pl.program_id(0) == 0)
    def _():
        away_ref[...] = total.astype(jnp.bfloat16)

    @pl.when(pl.program_id(0) == 1)
    def _():
        kept_ref[...] = total


def halve(own, arrived, which, tokens=()):
    tokens = waits(tokens)
    (own, own_first, rows), (arrived, arrived_first, _) = own, arrived
    half, columns = rows // 2, own.shape[1]
    tile = min(SUM_ROWS, half)
    tiles = half // tile

    def source(first):
        return pl.BlockSpec(
            (tile, columns), lambda g, t, w: (first // tile + jnp.where(g == 0, 1 - w[0], w[0]) * tiles + t, 0)
        )

    *results, mark = pl.pallas_call(
        halve_kernel,
        grid_spec=pltpu.PrefetchScalarGridSpec(
            num_scalar_prefetch=1,
            grid=(2, tiles),
            in_specs=[source(own_first), source(arrived_first)] + anywhere(len(tokens)),
            out_specs=[
                pl.BlockSpec((tile, columns), lambda g, t, w: (jnp.where(g == 0, t, tiles - 1), 0)),
                pl.BlockSpec((tile, columns), lambda g, t, w: (jnp.where(g == 0, 0, t), 0)),
                MARK_SPEC,
            ],
        ),
        out_shape=[
            jax.ShapeDtypeStruct((half, columns), jnp.bfloat16),
            jax.ShapeDtypeStruct((half, columns), jnp.float32),
            MARK_SHAPE,
        ],
        compiler_params=PARAMS,
        cost_estimate=cost(),
        name="halve",
    )(which, own, arrived, *tokens)
    return marked(results, mark)


def add_kernel(own, arrives, *refs):
    out_ref, mark_ref = refs[-2:]
    mark_ref[...] = jnp.zeros_like(mark_ref)
    rows = out_ref.shape[0] // own
    for k in range(own):
        values = refs[k][...].astype(jnp.float32)
        if arrives:
            values = values + refs[own + k][...].astype(jnp.float32)
        out_ref[k * rows : (k + 1) * rows, :] = values.astype(out_ref.dtype)


def add_low(own, arrived=(), tokens=(), kind=jnp.bfloat16):
    tokens = waits(tokens)
    rows, columns = own[0][2], own[0][0].shape[1]
    across = min(512, columns)
    total = rows * len(own)
    ranges = [*own, *arrived]
    result, mark = pl.pallas_call(
        functools.partial(add_kernel, len(own), bool(arrived)),
        grid=(columns // across,),
        in_specs=[
            pl.BlockSpec((rows, across), lambda j, first=first // rows: (first, j)) for _, first, rows in ranges
        ]
        + anywhere(len(tokens)),
        out_specs=[pl.BlockSpec((total, across), lambda j: (0, j)), MARK_SPEC],
        out_shape=[jax.ShapeDtypeStruct((total, columns), kind), MARK_SHAPE],
        compiler_params=PARAMS,
        cost_estimate=cost(),
        name="add_low",
    )(*(array for array, _, _ in ranges), *tokens)
    return marked([result], mark)[0]


def whole_range(array):
    return (array, 0, array.shape[0])


def join_kernel(count, tiles, *refs):
    out_ref, mark_ref = refs[-2:]
    mark_ref[...] = jnp.zeros_like(mark_ref)
    for k in range(count):

        @pl.when(pl.program_id(0) // tiles == k)
        def _(k=k):
            out_ref[...] = refs[k][...]


def join(arrays, tokens=()):
    tokens = waits(tokens)
    rows, columns = arrays[0].shape
    tile = min(2 * SUM_ROWS, rows)
    tiles = rows // tile
    result, mark = pl.pallas_call(
        functools.partial(join_kernel, len(arrays), tiles),
        grid=(len(arrays) * tiles,),
        in_specs=[
            pl.BlockSpec((tile, columns), lambda i, k=k: (jnp.clip(i - k * tiles, 0, tiles - 1), 0))
            for k in range(len(arrays))
        ]
        + anywhere(len(tokens)),
        out_specs=[pl.BlockSpec((tile, columns), lambda i: (i, 0)), MARK_SPEC],
        out_shape=[jax.ShapeDtypeStruct((len(arrays) * rows, columns), arrays[0].dtype), MARK_SHAPE],
        compiler_params=PARAMS,
        cost_estimate=cost(),
        name="join",
    )(*arrays, *tokens)
    return marked([result], mark)[0]


def ring_shift(block):
    size = lax.axis_size("tensor")
    return lax.ppermute(block, "tensor", [(i, (i + 1) % size) for i in range(size)])


def ring_gather(block):
    blocks = [block]
    for _ in range(lax.axis_size("tensor") - 1):
        blocks.append(ring_shift(blocks[-1]))
    return blocks


def row_halves(ranges):
    return [
        [(array, first + k * (rows // 2), rows // 2) for array, first, rows in ranges] for k in range(2)
    ]


def ring_sums(step, size, ranges, arrived, tokens):
    if step < size - 1:
        return [add_low(ranges, arrived, tokens)]
    arrived = row_halves(arrived) if arrived else ((), ())
    return [add_low(own, other, tokens) for own, other in zip(row_halves(ranges), arrived)]


def own_columns(attended):
    blocks = jnp.split(attended, lax.axis_size("tensor"))
    size = len(blocks)
    return [blocks[0]] + [
        lax.ppermute(blocks[size - step], "tensor", [(i, (i + step) % size) for i in range(size)])
        for step in range(1, size)
    ]


def swap(values, axis, bit):
    return lax.ppermute(values, axis, [(i, i ^ (1 << bit)) for i in range(lax.axis_size(axis))])


def bit_of(axis, bit):
    return (lax.axis_index(axis) >> bit) & 1


def axis_orders():
    bits = (lax.axis_size("dp") - 1).bit_length()
    return list(range(1, bits)), list(range(bits - 1, 0, -1))


class Butterfly:
    def __init__(self, halved, orders):
        self.orders, self.level, self.levels = orders, 0, len(orders[0])
        self.ready, self.kept = [away for away, _ in halved], [kept for _, kept in halved]

    def step(self, *after):
        level, levels = self.level, self.levels
        if level == 2 * levels:
            return self
        bits = [order[level] if level < levels else order[2 * levels - 1 - level] for order in self.orders]
        arrived = [swap(away, "dp", bit) for away, bit in zip(self.ready, bits)]
        self.level += 1
        if self.level < levels:
            halved = [
                halve(
                    (kept, 0, kept.shape[0]),
                    (other, 0, kept.shape[0]),
                    jnp.full((1,), bit_of("dp", order[self.level]), jnp.int32),
                    after,
                )
                for kept, other, order in zip(self.kept, arrived, self.orders)
            ]
            self.ready, self.kept = [away for away, _ in halved], [kept for _, kept in halved]
        elif self.level == levels:
            self.ready = [
                add_low([whole_range(kept)], [whole_range(other)], after) for kept, other in zip(self.kept, arrived)
            ]
        elif self.level < 2 * levels:
            self.ready = [join(both, after) for both in zip(self.ready, arrived)]
        else:
            self.ready = [join([array for both in zip(self.ready, arrived) for array in both], after)]
        return self

    def gathered(self, *after):
        while self.level < 2 * self.levels:
            self.step(*after)
        return self.ready[0]


def own_scalars(order):
    return jnp.stack([bit_of("dp", 0), bit_of("dp", order[0])]).astype(jnp.int32)


def pieces_of(joined, parts, part=None):
    count = parts << ((lax.axis_size("dp") - 1).bit_length() - 1)
    rows = joined.shape[0] // count
    each = count // parts
    return [
        (half, 0, count, rows) if part is None else (half, part * each, each, rows)
        for half in (joined, swap(joined, "dp", 0))
    ]


class SumEverywhere:
    def __init__(self, values):
        self.values = values
        self.left = [
            (axis, bit) for axis in ("tensor", "dp") for bit in range((lax.axis_size(axis) - 1).bit_length())
        ]

    def step(self, *after):
        axis, bit = self.left.pop(0)
        arrived = swap(self.values, axis, bit)
        self.values = add_low([whole_range(self.values)], [whole_range(arrived)], after, jnp.float32)
        return self.values

    def finished(self, last):
        while len(self.left) > last:
            self.step()
        return self.values


def piece_rows(orders):
    levels = len(orders[0])
    entries = []
    for flip in (0, 1):
        core = bit_of("dp", 0) ^ flip
        for k, order in enumerate(orders):
            for position in range(1 << levels):
                row = jnp.int32(0)
                for level, bit in enumerate(order):
                    digit = (position >> (levels - 1 - level)) & 1
                    row = row * 2 + (bit_of("dp", bit) ^ digit)
                entries.append((core * len(orders) + k) * (1 << levels) + row)
    return jnp.stack(entries).astype(jnp.int32)


def segments_from(slot_lengths, group_rows):
    bounds = jnp.cumsum(slot_lengths)
    row_ids = jnp.arange(group_rows, dtype=jnp.int32)
    segment = jnp.sum((row_ids[:, None] >= bounds[None, :]).astype(jnp.int32), axis=1)
    starting = jnp.concatenate([jnp.zeros((1,), jnp.int32), bounds])
    labels = jnp.arange(starting.shape[0], dtype=jnp.int32)
    begins = jnp.sum(jnp.where(segment[:, None] == labels[None, :], starting[None, :], 0), axis=1)
    return (segment, begins)


def group_layout(lengths, permutation, group_rows, seq_count):
    group_index = lax.axis_index("dp")
    chosen = lax.dynamic_slice_in_dim(permutation, group_index * seq_count, seq_count)
    matches = chosen[:, None] == jnp.arange(permutation.shape[0], dtype=jnp.int32)[None, :]
    slot_lengths = jnp.sum(jnp.where(matches, lengths[None, :], 0), axis=1)
    return segments_from(slot_lengths, group_rows)


def rope_tables(position):
    halfway = HEAD_DIM // 2
    frequency = THETA ** (-(2.0 * jnp.arange(halfway, dtype=jnp.float32)) / HEAD_DIM)
    angles = position.astype(jnp.float32)[:, None] * frequency[None, :]
    cosine, sine = jnp.cos(angles), jnp.sin(angles)
    return jnp.concatenate([cosine, cosine], axis=1), jnp.concatenate([-sine, sine], axis=1)


def gather_rows(*weights):
    return lax.all_gather(jnp.concatenate(weights, axis=1), "dp", axis=0, tiled=True)


def per_device(
    streams,
    cotangent,
    lengths,
    permutation,
    query_weight,
    key_weight,
    value_weight,
    out_weight,
    gate_weight,
    up_weight,
    down_weight,
    mix_static,
    mix_weight,
    mix_scale,
):
    MARKS.clear()
    qkv_full = gather_rows(query_weight, key_weight, value_weight)
    gate_up_full = gather_rows(gate_weight, up_weight)
    down_full = gather_rows(down_weight)
    local_rows, count, width = streams.shape
    uses = mix_static.shape[2]
    sizes = (count, uses)
    size = lax.axis_size("tensor")
    group_rows = local_rows * size
    mine = lax.axis_index("tensor")
    place_index = jnp.full((1,), mine, jnp.int32)
    core = jnp.full((1,), bit_of("dp", 0), jnp.int32)
    units = gate_weight.shape[1]
    seq_count = permutation.shape[0] // lax.axis_size("dp")

    inputs = streams.reshape(local_rows, count * width)
    cotangents = cotangent.reshape(local_rows, count * width)
    tables_a = mix_tables(mix_static[0], mix_weight[0], mix_scale[0])
    tables_f = mix_tables(mix_static[1], mix_weight[1], mix_scale[1])
    segment, begins = group_layout(lengths, permutation, group_rows, seq_count)
    cosine, sine = rope_tables(jnp.arange(group_rows, dtype=jnp.int32) - begins)
    starts = jnp.broadcast_to(begins[:, None], (group_rows, LANES))
    local_segment = lax.dynamic_slice_in_dim(segment, mine * local_rows, local_rows)
    valid = jnp.broadcast_to((local_segment < seq_count).astype(jnp.float32)[:, None], (local_rows, LANES))

    others = [
        lax.ppermute(out_weight, "tensor", [(i, (i + step) % size) for i in range(size)]) for step in range(1, size)
    ]
    normed_a, saved_a = open_attention(inputs, tables_a, *sizes)
    out_full = gather_rows(out_weight, *hold(others, normed_a))
    input_blocks = ring_gather(normed_a)
    query, key, value, attended, log_totals = attend(
        [matmul(block, qkv_full) for block in input_blocks], place_index, starts, cosine, sine
    )
    out_a = out_project(own_columns(attended), out_full)
    half_rows = local_rows // 2
    normed_f, d_out_f, saved_f, middle = open_feedforward(
        inputs, saved_a, out_a, cotangents, valid, tables_f, *sizes
    )
    orders = axis_orders()
    steps = 2 * len(orders[0])
    whole_table, half_tables = piece_rows(orders), [piece_rows([order]) for order in orders]

    def pair_of(arrays, pair):
        return arrays[2 * pair : 2 * pair + 2]

    blocks, gates, ups, filled = [normed_f], [], [], []

    def forward(pair, filled):
        gate, up, filled = forward_units(pair, size, pair_of(blocks, pair), gate_up_full, filled)
        gates.append(gate)
        ups.append(up)
        return filled

    for step in range(1, size):
        blocks.append(ring_shift(blocks[-1]))
        if step % 2 == 0:
            filled = forward(step // 2 - 1, filled)
    last_pair = size // 2 - 1
    grads, partials_n, filled_back = list(hold([d_out_f], blocks[-1], *gates)), [], []
    for step in range(1, size):
        arrived = ring_shift(grads[-1])
        if step == 1:
            filled = forward(last_pair, filled)
            (arrived,) = hold([arrived], gates[-1])
        elif step % 2 == 0:
            pair = step // 2 - 1
            partial, filled_back = backward_units(
                pair, size, pair_of(grads, pair), gates[pair], ups[pair], gate_up_full, down_full, filled_back
            )
            partials_n.append(partial)
            (arrived,) = hold([arrived], partial)
        grads.append(arrived)
    feedforward_rows, hidden_rows = filled
    partials_f = backproject((hidden_rows, local_rows), 0, size, down_full, jnp.float32, partials_n)

    def both_parts(index):
        first = (index % 2) * local_rows
        return [(partials_f, index * local_rows, local_rows), (partials_n[index // 2], first, local_rows)]

    half = width // 2
    totals = ring_sums(1, size, both_parts(1), (), [grads[-1]])
    for step in range(2, size + 1):
        arrived, total = [ring_shift(one) for one in totals], totals[0]
        tokens = []
        if step == 2:
            partial, filled_back = backward_units(
                last_pair,
                size,
                pair_of(grads, last_pair),
                gates[last_pair],
                ups[last_pair],
                gate_up_full,
                down_full,
                filled_back,
                [total],
            )
            partials_n.append(partial)
            grad_rows, *unit_rows = filled_back
            aways = [away_product(core, [feedforward_rows], rows, units, 0, []) for rows in unit_rows]
            tokens = aways
        elif step == 3:
            others = [swap(away, "dp", 0) for away in hold(aways, total)]
            down_away = away_product(core, [grad_rows], hidden_rows, units, 0, [], [total])
            gate_up_sum = Butterfly(
                [
                    own_product(own_scalars(order), [feedforward_rows], rows, other, units, 0, 0, half, [], [down_away])
                    for order, rows, other in zip(orders, unit_rows, others)
                ],
                orders,
            )
            tokens = [*gate_up_sum.ready, down_away]
        elif step == 4:
            down_other = swap(*hold([down_away], total), "dp", 0)
            down_sum = Butterfly(
                [
                    own_product(
                        own_scalars(order), [grad_rows], hidden_rows, down_other, units, 0, k * half // 2, half // 2, [], [total]
                    )
                    for k, order in enumerate(orders)
                ],
                orders,
            )
            tokens = down_sum.ready
        if step < size:
            here = [(arrived[0], 0, local_rows), (arrived[0], local_rows, local_rows)]
            totals = ring_sums(step, size, both_parts(step), here, tokens)
    filled, sums_f = [], []
    for k, both in enumerate(arrived):
        first = k * half_rows
        own_f, own_n = (partials_f, first), (partials_n[0], first)
        rest = [(a, first) for a in (valid, saved_a, out_a)]
        arrays = [(a, first) for a in (middle, saved_f, cotangents)]
        *filled, weight_sum, small = close_mix(
            True,
            first,
            half_rows,
            [*arrays, (both, half_rows), own_n, (both, 0), own_f, *rest],
            tables_f,
            *sizes,
            filled,
            tokens,
        )
        sums_f.append((weight_sum, small))
        tokens = []
    middle_grad, d_branch_a, d_out_a = filled

    def finished(tokens):
        filled = []
        for k, both in enumerate(arrived_last):
            filled = [finish(k * half_rows, middle, saved_f, (both, 0, half_rows), partials_f, *sizes, filled, tokens)]
        return filled[0]

    arrived_last = arrived

    output_grads = [d_out_a]
    for step in range(1, size):
        arrived = ring_shift(output_grads[-1])
        after = output_grads[-1]
        tokens = []
        if step == 1:
            tokens = [*gate_up_sum.step(after).ready, *down_sum.step(after).ready]
        elif step == 2:
            out_streams = finished(gate_up_sum.step(after).ready)
            tokens = [*gate_up_sum.ready, out_streams]
        if tokens:
            (arrived,) = hold([arrived], *tokens)
        output_grads.append(arrived)
        if step == 3:
            tokens = gate_up_sum.step(after).ready
    attended_grads = [project([block], out_full, attended.shape[1]) for block in output_grads]
    output_rows = output_grads
    d_qkv = attend_back(
        [query, key, value, log_totals], attended_grads, place_index, starts, cosine, sine, tokens
    )
    total = backproject((d_qkv, local_rows), 1, 1, qkv_full, jnp.bfloat16)
    columns = attended.shape[1]
    for step in range(2, size + 1):
        arrived = ring_shift(total)
        tokens = []
        if step == 2:
            away = away_product(core, input_blocks, d_qkv, 4 * columns, 0, [], [total])
            away = away_product(core, output_rows, attended, 4 * columns, 3 * columns, [away])
            own_partials = [backproject((d_qkv, local_rows), 2, 1, qkv_full, jnp.float32, [away])]
            gate_up_joined = gate_up_sum.gathered(*own_partials)
            tokens = [away, gate_up_joined, *down_sum.step(*own_partials).ready]
        elif step == 3:
            (away,) = hold([away], total)
            other = swap(away, "dp", 0)
            own_partials.append(backproject((d_qkv, local_rows), 3 % size, size - 3, qkv_full, jnp.float32, [total]))
            halved = []
            for k, order in enumerate(orders):
                place = (4 * columns, 0, k * half // 2, half // 2)
                scalars = own_scalars(order)
                both = own_product(scalars, input_blocks, d_qkv, other, *place, [], [own_partials[-1]])
                place = (4 * columns, 3 * columns, k * half // 2, half // 2)
                halved.append(own_product(scalars, output_rows, attended, other, *place, both))
            attention_sum = Butterfly(halved, orders)
            tokens = [*attention_sum.ready, *down_sum.step(*attention_sum.ready).ready]
        elif step == 4:
            (gate_up_joined,) = hold([gate_up_joined], total)
            gate_pieces, up_pieces = (pieces_of(gate_up_joined, 2, k) for k in range(2))
            own_partial = backproject((d_qkv, local_rows), 0, 1, qkv_full, jnp.float32, [total])
            (gate_grad,) = assemble(gate_pieces, [units], half_tables[0], [own_partial])
            tokens = attention_sum.step(gate_grad).ready
        if step < size:
            place = (own_partials[0], 0) if step == 2 else (own_partials[1], (step - 3) * local_rows)
            total = add_low([(*place, local_rows)], [whole_range(arrived)], tokens)
    arrays = [(a, 0) for a in (inputs, saved_a, middle_grad, arrived, own_partial, d_branch_a)]
    input_grad, weight_sum_a, small_a = close_mix(
        False,
        0,
        local_rows,
        arrays,
        tables_a,
        *sizes,
        tokens=tokens,
    )
    height = width // LANES

    def flat(weight_sum, small):
        summed = weight_sum[:uses] + weight_sum[8 : 8 + uses]
        return jnp.concatenate([summed.reshape(uses * height, LANES), small])

    def unpacked(sums):
        constants = sums[uses * height : uses * height + 2, : count * uses].reshape(2, count, uses)
        return constants[0], sums[: uses * height].reshape(uses, width).T, jnp.sum(constants[1], axis=0)

    weight_sum_f, small_f = (one + other for one, other in zip(*sums_f))
    sums = SumEverywhere(jnp.concatenate([flat(weight_sum_f, small_f), flat(weight_sum_a, small_a)]))
    attention_sum.step(small_a)
    (up_grad,) = assemble(up_pieces, [units], half_tables[1], [sums.values, *attention_sum.ready])
    attention_sum.step(sums.step(up_grad))
    down_joined = down_sum.gathered(*attention_sum.ready)
    after = sums.step(down_joined)
    (down_grad,) = assemble(pieces_of(down_joined, 2), [units], whole_table, [after])
    attention_joined = attention_sum.gathered(sums.step(down_grad))
    after = sums.step(attention_joined)
    query_grad, key_grad, value_grad, out_grad = assemble(
        pieces_of(attention_joined, 2), [columns] * 4, whole_table, [sums.finished(0)]
    )
    (static_f, weight_f, scale_f), (static_a, weight_a, scale_a) = (
        unpacked(part) for part in jnp.split(sums.finished(0), 2)
    )
    return (
        out_streams,
        input_grad,
        query_grad,
        key_grad,
        value_grad,
        out_grad,
        gate_grad,
        up_grad,
        down_grad,
        jnp.stack([static_a, static_f]),
        jnp.stack([weight_a, weight_f]),
        jnp.stack([scale_a, scale_f]),
    )


def solution(mesh):
    placed = (
        P(("dp", "tensor"), None, None),
        P(("dp", "tensor"), None, None),
        P(),
        P(),
        P("dp", "tensor"),
        P("dp", "tensor"),
        P("dp", "tensor"),
        P("dp", "tensor"),
        P("dp", "tensor"),
        P("dp", "tensor"),
        P("dp", "tensor"),
        P(),
        P(),
        P(),
    )
    return jax.shard_map(
        per_device,
        mesh=mesh,
        in_specs=placed,
        out_specs=(
            P(("dp", "tensor"), None, None),
            P(("dp", "tensor"), None, None),
            P(None, "tensor"),
            P(None, "tensor"),
            P(None, "tensor"),
            P(None, "tensor"),
            P(None, "tensor"),
            P(None, "tensor"),
            P(None, "tensor"),
            P(),
            P(),
            P(),
        ),
        check_vma=False,
    )
```
